256 devices in a mesh: role: 2 (over x_lo), shard: 128 (over z, y, x_hi, core).
Axes of the slice: x: 4 (x_hi: 2, x_lo: 2; x = x_hi * 2 + x_lo), y: 4, z: 8, core: 2. Of those that a mesh axis runs over, the one named last changes fastest.
Arguments:
- tables: float32 [2, 262144, 128], P('role', 'shard'), may hold values from -6 to 6
- row_squares: float32 [262144, 128], P('shard'), may hold values from 0.01 to 1
- update_slots: int32 [65536], P('shard'), may hold values from 0 to 2047, as said below
- update_counts: int32 [128], P('shard'), may hold values from 1 to 512, 32768 in all
- row_grads: float32 [65536, 128], P('shard'), may hold values from -6 to 6
- dense_state: float32 [2, 3, 512, 512], P('role'), may hold values from -0.6 to 0.6
- dense_squares: float32 [3, 512, 512], replicated, may hold values from 0.01 to 1
- dense_grads: float32 [128, 3, 512, 512], P('shard'), may hold values from -0.06 to 0.06
- cross_bias: float32 [3, 512], replicated, may hold values from -3 to 3
- out_weight: float32 [512], replicated, may hold values from -0.75 to 0.75
- cand_owner: int32 [2, 65536, 4], P('role', 'shard'), may hold values from 0 to 127, all different within a row; in each aligned block of 512 rows (0 to 511, 512 to 1023, ..., all dimensions but the last counted through in order) at most 32 rows name the same one
- cand_slot: int32 [2, 65536, 4], P('role', 'shard'), may hold values from 0 to 2047
Outputs:
- tables_out: float32 [2, 262144, 128], P('role', 'shard')
- scores: float32 [2, 65536], P('role', 'shard')
The draws below stay inside these ranges and needn't reach their ends.
Inputs may be any that keep to these rules, and one draw needn't show every extreme that they name: `update_slots`: the 512 slots of one shard name distinct rows. `update_counts`: the counts sum to 32768. `cand_owner`: the 4 owners of one example are distinct; among the 512 examples of one device no shard is named more than 32 times, a bound that some block reaches.
All inputs are finite; a program needn't handle non-finite values. No bound on the sum of `update_counts` on one device may be relied on, other than what follows from the above.
Results may differ from the reference program's by a relative error of at most 0.0084.
Values may be sent and summed in bfloat16 or wider, within the bound.
No kernel may reach another device: no remote copies, remote signals or barrier semaphores. Data moves between devices by JAX's collectives and lax.ppermute only.
A program may use at most 64 MiB of HBM per device.

```python
import math
import jax
import jax.numpy as jnp
import numpy as np
from jax import lax

EMB = 128
WIDTH = 512
FIELDS = 4
LAYERS = 3
ROWS_DEV = 2048
UPD_DEV = 512
CAND_DEV = 512
SHARDS = 128
TABLE_ROWS = 262144
UPDATES = 65536
CANDS = 65536
CAP = 32


def draw_update_slots(key, part):
    key = jax.random.fold_in(key, 7)
    shard_keys = jax.random.split(key, UPDATES // UPD_DEV)

    def one_shard(shard_key):
        return jax.random.permutation(shard_key, ROWS_DEV)[:UPD_DEV]
    return jax.vmap(one_shard)(shard_keys).reshape(-1).astype(jnp.int32)


def with_ends(array, own_key, smallest, largest):
    index_at = [jax.random.randint(jax.random.fold_in(own_key, axis), (), 0, length) for axis, length in enumerate(array.shape)]
    widest = array.shape.index(max(array.shape))
    neighbour = index_at[:widest] + [(index_at[widest] + 1) % array.shape[widest]] + index_at[widest + 1:]
    return array.at[tuple(index_at)].set(smallest).at[tuple(neighbour)].set(largest)


def level_of(rng, dims, cuts, least, high):
    def one(axis_at, parts):
        heights = jax.random.uniform(jax.random.fold_in(jax.random.fold_in(rng, 6), axis_at), (parts,), jnp.float32, least / len(cuts), high / len(cuts))
        return jnp.repeat(jnp.exp(heights), dims[axis_at] // parts).reshape((-1,) + (1,) * (len(dims) - axis_at - 1))

    gain = one(*cuts[0])
    for cut in cuts[1:]:
        gain = gain * one(*cut)
    return gain


def split_up(amount, total, reach, lean):
    portions = [(1 << 20) // math.isqrt(standing ** lean) + 1 for standing in range(2, amount + 1)]
    surplus, given = total - reach - (amount - 1), [1] * (amount - 1)
    while surplus > 0:
        movable = [i for i in range(amount - 1) if given[i] < reach]
        pool, remaining = sum([portions[i] for i in movable]), surplus
        for i in movable:
            addition = min(reach - given[i], max(1, remaining * portions[i] // pool), surplus)
            given[i] = given[i] + addition
            surplus = surplus - addition
    return np.array([reach] + given)


def ragged(own_key, count, total, limit, lean):
    if count == 2:
        one = jax.random.randint(own_key, (), max(1, total - limit), min(limit, total - 1) + 1)
        return jnp.stack([one, total - one])
    tallies = jnp.asarray(split_up(count, total, limit, lean), jnp.int32)
    twos = (count - 1) // 2
    source_of, sink = tallies[1:1 + 2 * twos:2], tallies[2:2 + 2 * twos:2]
    room = jnp.minimum(source_of - 1, limit - sink)
    moved = jax.random.randint(jax.random.fold_in(own_key, 1), (twos,), 0, 1 << 20) % (room + 1)
    tallies = tallies.at[1:1 + 2 * twos:2].set(source_of - moved).at[2:2 + 2 * twos:2].set(sink + moved)
    return tallies[jax.random.permutation(jax.random.fold_in(own_key, 2), count)]


def shared_out(rng, own, number, rows, count, top, reach, slope):
    ranking = jax.random.permutation(rng, count)
    heavy_load, usual = portions_of(count, rows * top, reach, slope, True), portions_of(count, rows * top, reach, slope, False)
    places = jnp.arange(count)

    def named(sizes, offset_by):
        used = int((sizes > 0).sum())
        fixed = max(1, used // 4)
        moved = fixed + (places - fixed + offset_by * (used - fixed)) % max(1, count - fixed)
        return jnp.zeros((count,), jnp.int32).at[ranking[jnp.where(places < fixed, places, moved)]].set(jnp.asarray(sizes, jnp.int32))

    sizes = jnp.where(number % 4 == 0, named(heavy_load, number // 4), named(usual, number - number // 4 - 1))
    mixed = jax.random.permutation(jax.random.fold_in(own, 3), count)
    source_of, sink = mixed[0:count // 2 * 2:2], mixed[1:count // 2 * 2:2]
    slack = jnp.minimum(sizes[source_of] - 1, reach - sizes[sink]) // 2
    slack = jnp.where((source_of == ranking[0]) | (sink == ranking[0]) | (sizes[sink] == 0), 0, jnp.maximum(slack, 0))
    moved = jax.random.randint(jax.random.fold_in(own, 4), (count // 2,), 0, 1 << 20) % (slack + 1)
    sizes = sizes.at[source_of].add(-moved).at[sink].add(moved)
    items = jnp.searchsorted(jnp.cumsum(sizes), jnp.arange(rows * top), side="right").astype(jnp.int32)
    table = items.reshape(top, rows).T
    table = table[jax.random.permutation(jax.random.fold_in(own, 1), rows)]
    offset_by = jax.random.randint(jax.random.fold_in(own, 2), (rows, 1), 0, top)
    return jnp.take_along_axis(table, (jnp.arange(top)[None, :] + offset_by) % top, axis=1)


def portions_of(count, total, bound, skew, full):
    weights = [(1 << 20) // math.isqrt(grade ** skew) + 1 for grade in range(1, count + 1)]
    largest = bound if full else min(bound, max(-(-total // count), total * weights[0] // sum(weights)))
    least = 1 if total - largest >= count - 1 else 0
    holding, surplus = [largest] + [least] * (count - 1), total - largest - least * (count - 1)
    while surplus > 0:
        free = [i for i in range(1, count) if holding[i] < largest] or [i for i in range(1, count) if holding[i] < bound]
        pool, left = sum([weights[i] for i in free]), surplus
        for i in free:
            more = min(bound - holding[i], max(1, left * weights[i] // pool), surplus)
            holding[i] = holding[i] + more
            surplus = surplus - more
    return np.array(holding)


def scatter_about(key, extent, scale, reach, cuts=(), held_as=jnp.bfloat16):
    drawn = scale * jax.random.normal(key, extent, jnp.float32)
    if cuts:
        drawn = drawn * level_of(key, extent, cuts, -0.22, 0.18)
    return jnp.clip(drawn, -reach, reach).astype(held_as)


def setup_inputs(seed: int = 0) -> dict:
    seeds = jax.random.split(jax.random.key(seed), 13)
    tables = scatter_about(seeds[0], (2, TABLE_ROWS, EMB), 1.0, 6.0, ((0, 2), (1, 128)), jnp.float32)
    row_squares = jnp.clip(jnp.exp(math.log(1.0) - 4.6051702 * jax.random.uniform(seeds[1], (TABLE_ROWS, EMB), jnp.float32) ** level_of(seeds[1], (TABLE_ROWS, EMB), ((0, 128),), -0.2, 0.2)), 0.01, 1.0)
    update_slots = draw_update_slots(jax.random.fold_in(seeds[12], 71), 0)
    update_counts = ragged(seeds[3], SHARDS, UPDATES // 2, UPD_DEV, 2).astype(jnp.int32)
    row_grads = scatter_about(seeds[4], (UPDATES, EMB), 1.0, 6.0, ((0, 128),), jnp.float32)
    dense_state = scatter_about(seeds[5], (2, LAYERS, WIDTH, WIDTH), 0.1, 0.6, ((0, 2),), jnp.float32)
    dense_squares = jnp.clip(jnp.exp(jax.random.uniform(seeds[6], (LAYERS, WIDTH, WIDTH), jnp.float32, math.log(0.01), math.log(1.0))), 0.01, 1.0)
    dense_grads = scatter_about(seeds[7], (SHARDS, LAYERS, WIDTH, WIDTH), 0.01, 0.06, ((0, 128),), jnp.float32)
    cross_bias = scatter_about(seeds[8], (LAYERS, WIDTH), 0.5, 3.0, (), jnp.float32)
    out_weight = scatter_about(seeds[9], (WIDTH,), (WIDTH // 8) ** -0.5, 0.75, (), jnp.float32)
    cand_owner_keys = jax.random.split(jax.random.fold_in(seeds[10], 1), 2 * CANDS // CAND_DEV)
    cand_owner_turns = jax.random.permutation(jax.random.fold_in(seeds[10], 3), 2 * CANDS // CAND_DEV)
    cand_owner = jax.vmap(lambda own, number: shared_out(jax.random.fold_in(seeds[10], 2), own, number, CAND_DEV, SHARDS, FIELDS, CAP, 2))(cand_owner_keys, cand_owner_turns).reshape((2, CANDS, FIELDS))
    cand_slot = with_ends(jax.random.randint(seeds[11], (2, CANDS, FIELDS), 0, ROWS_DEV), jax.random.fold_in(seeds[11], 1), 0, ROWS_DEV - 1).astype(jnp.int32)
    return dict(tables=tables, row_squares=row_squares, update_slots=update_slots, update_counts=update_counts, row_grads=row_grads, dense_state=dense_state, dense_squares=dense_squares, dense_grads=dense_grads, cross_bias=cross_bias, out_weight=out_weight, cand_owner=cand_owner, cand_slot=cand_slot)


ROW_SHRINK = 0.25
DENSE_SHRINK = 0.05

def ftrl_weight(linear, squares, shrink):
    return -(linear - jnp.clip(linear, -shrink, shrink)) / (1.0 + jnp.sqrt(squares))

def ftrl_step(linear, squares, gradient, shrink):
    prior = ftrl_weight(linear, squares, shrink)
    fresh_squares = squares + gradient * gradient
    sigma_step = jnp.sqrt(fresh_squares) - jnp.sqrt(squares)
    return (linear + gradient - sigma_step * prior, fresh_squares, prior)

def score_role(lookup_table, cross_weights, owners, slot_ids, cross_bias, out_weight):
    row_ids = owners * ROWS_DEV + slot_ids
    blocks = row_ids.reshape(-1, CAND_DEV, owners.shape[1])

    def score_block(block_rows):
        base_feats = lookup_table[block_rows].reshape(CAND_DEV, -1).astype(jnp.float32)
        crossed = base_feats
        for layer_idx in range(cross_weights.shape[0]):
            mixed_rows = jnp.dot(crossed.astype(jnp.bfloat16), cross_weights[layer_idx], preferred_element_type=jnp.float32)
            crossed = base_feats * (mixed_rows + cross_bias[layer_idx]) + crossed
        return lax.optimization_barrier(jnp.sum(crossed * out_weight, axis=1))
    return lax.map(score_block, blocks).reshape(-1)

def reference(tables, row_squares, update_slots, update_counts, row_grads, dense_state, dense_squares, dense_grads, cross_bias, out_weight, cand_owner, cand_slot):
    shards = update_counts.shape[0]
    table_rows = tables.shape[1]
    usable = jnp.arange(UPD_DEV, dtype=jnp.int32)[None, :] < update_counts[:, None]
    row_ids = (jnp.arange(shards, dtype=jnp.int32)[:, None] * ROWS_DEV + update_slots.reshape(shards, UPD_DEV)).reshape(-1)
    targets = jnp.where(usable.reshape(-1), row_ids, table_rows).astype(jnp.int32)
    fresh_linear, fresh_sumsq, unused = ftrl_step(tables[0][row_ids], row_squares[row_ids], row_grads, ROW_SHRINK)
    new_linear = tables[0].at[targets].set(fresh_linear, mode='drop')
    new_squares = row_squares.at[targets].set(fresh_sumsq, mode='drop')
    trainer_table = ftrl_weight(new_linear, new_squares, ROW_SHRINK)
    fresh_weights = ftrl_weight(fresh_linear, fresh_sumsq, ROW_SHRINK)
    serving_table = tables[1].at[targets].set(fresh_weights, mode='drop')
    summed = lax.optimization_barrier(jnp.sum(dense_grads, axis=0))
    dense_linear, dense_sumsq, prior_weights = ftrl_step(dense_state[0], dense_squares, summed, DENSE_SHRINK)
    fresh_dense = ftrl_weight(dense_linear, dense_sumsq, DENSE_SHRINK)
    served_dense = dense_state[1] + (fresh_dense - prior_weights)
    trainer_scores = score_role(trainer_table.astype(jnp.bfloat16), fresh_dense.astype(jnp.bfloat16), cand_owner[0], cand_slot[0], cross_bias, out_weight)
    serving_scores = score_role(serving_table.astype(jnp.bfloat16), served_dense.astype(jnp.bfloat16), cand_owner[1], cand_slot[1], cross_bias, out_weight)
    return (jnp.stack([new_linear, serving_table]), jnp.stack([trainer_scores, serving_scores]))
```

```python
import functools

import jax
import jax.numpy as jnp
from jax import lax
from jax.experimental import pallas as pl
from jax.experimental.pallas import tpu as pltpu
from jax.sharding import PartitionSpec as P

ROW_SHRINK = 0.25
DENSE_SHRINK = 0.05
CAP = 32
LANES = 128
SHARDS = 128
ROLES = 2
Z_SIZE, Y_SIZE, X_SIZE, CORES = 8, 4, 2, 2
VMEM_LIMIT = 40 * 1024 * 1024


def shard_at(z, y, x, core):
    return ((z * Y_SIZE + y) * X_SIZE + x) * CORES + core


def ftrl_weight(linear, squares, shrink):
    return -(linear - jnp.clip(linear, -shrink, shrink)) / (1.0 + jnp.sqrt(squares))


def ftrl_step(linear, squares, gradient, shrink):
    prior = ftrl_weight(linear, squares, shrink)
    fresh_squares = squares + gradient * gradient
    sigma_step = jnp.sqrt(fresh_squares) - jnp.sqrt(squares)
    return (linear + gradient - sigma_step * prior, fresh_squares, prior)


def iota(shape, dim):
    return lax.broadcasted_iota(jnp.int32, shape, dim)


def kernel_call(body, out_shape, flops=0, bytes_accessed=0, **options):
    return pl.pallas_call(
        body,
        out_shape=out_shape,
        compiler_params=pltpu.CompilerParams(vmem_limit_bytes=VMEM_LIMIT),
        cost_estimate=pl.CostEstimate(
            flops=flops, bytes_accessed=bytes_accessed, transcendentals=0
        ),
        **options,
    )


VMEM = pl.BlockSpec(memory_space=pltpu.VMEM)
SMEM = pl.BlockSpec(memory_space=pltpu.SMEM)


def routing_body(owner_ref, slot_ref, request_ref, place_ref):
    fields, examples = owner_ref.shape
    shape = (SHARDS, examples)
    shard_ids = iota(shape, 0)
    member = jnp.zeros(shape, jnp.float32)
    wanted = jnp.zeros(shape, jnp.float32)
    for field in range(fields):
        named = owner_ref[field : field + 1, :] == shard_ids
        member = jnp.where(named, 1.0, member)
        wanted = jnp.where(named, slot_ref[field : field + 1, :].astype(jnp.float32), wanted)
    earlier = jnp.where(iota((examples, examples), 0) < iota((examples, examples), 1), 1.0, 0.0)
    ranks = jnp.dot(
        member.astype(jnp.bfloat16),
        earlier.astype(jnp.bfloat16),
        preferred_element_type=jnp.float32,
    )
    places = []
    for field in range(fields):
        owners = owner_ref[field : field + 1, :]
        rank = jnp.sum(jnp.where(owners == shard_ids, ranks, 0.0), axis=0, keepdims=True)
        places.append(owners * CAP + rank.astype(jnp.int32))
    place_ref[...] = jnp.concatenate(
        places + [jnp.zeros((8 - fields, examples), jnp.int32)], axis=0
    )
    ranks = jnp.where(member > 0.5, ranks, -1.0)
    requests = jnp.zeros((SHARDS, LANES), jnp.float32)
    lanes = iota((SHARDS, LANES), 1)
    for rank in range(CAP):
        column = jnp.sum(
            jnp.where(ranks == float(rank), wanted, 0.0), axis=1, keepdims=True
        )
        requests = jnp.where(lanes == rank, column, requests)
    request_ref[...] = requests[:, :CAP].astype(jnp.int32)


def route(owners, slots):
    fields, examples = owners.shape
    return kernel_call(
        routing_body,
        (
            jax.ShapeDtypeStruct((SHARDS, CAP), jnp.int32),
            jax.ShapeDtypeStruct((8, examples), jnp.int32),
        ),
        flops=10_000_000,
        bytes_accessed=100_000,
        in_specs=[VMEM, VMEM],
        out_specs=(VMEM, VMEM),
    )(owners, slots)


def used_slots(slot_ref, count):
    slots = slot_ref[...]
    return jnp.where(iota(slots.shape, 1) < count, slots, -1)


def rows_of_block(slots, first, rows):
    hit = slots == iota((rows, slots.shape[1]), 0) + first
    return jnp.where(hit, 1.0, 0.0).astype(jnp.bfloat16)


def train_body(count_ref, slot_ref, held_ref, square_ref, grad_ref, new_ref, weight_ref, fresh_ref, parts, total):
    step = pl.program_id(0)
    rows = held_ref.shape[0]

    @pl.when(step == 0)
    def _():
        grads = grad_ref[...]
        high = grads.astype(jnp.bfloat16)
        rest = grads - high.astype(jnp.float32)
        middle = rest.astype(jnp.bfloat16)
        low = (rest - middle.astype(jnp.float32)).astype(jnp.bfloat16)
        parts[...] = jnp.concatenate([high, middle, low], axis=1)
        total[...] = jnp.zeros_like(total)

    spread = rows_of_block(used_slots(slot_ref, count_ref[0]), step * rows, rows)
    sums = jnp.dot(spread, parts[...], preferred_element_type=jnp.float32)
    gradient = (sums[:, :LANES] + sums[:, LANES : 2 * LANES]) + sums[:, 2 * LANES :]
    linear, squares, _ = ftrl_step(held_ref[...], square_ref[...], gradient, ROW_SHRINK)
    new_ref[...] = linear
    weights = ftrl_weight(linear, squares, ROW_SHRINK).astype(jnp.bfloat16)
    weight_ref[...] = weights
    total[...] += lax.dot_general(
        spread, weights, (((0,), (0,)), ((), ())), preferred_element_type=jnp.float32
    )

    @pl.when(step == pl.num_programs(0) - 1)
    def _():
        fresh_ref[...] = total[...].astype(jnp.bfloat16)


def train_rows(count, slots, held, squares, grads):
    rows, width = held.shape
    updates = grads.shape[0]
    block = 512
    by_rows = pl.BlockSpec((block, width), lambda i: (i, 0))
    return kernel_call(
        train_body,
        (
            jax.ShapeDtypeStruct((rows, width), jnp.float32),
            jax.ShapeDtypeStruct((rows, width), jnp.bfloat16),
            jax.ShapeDtypeStruct((updates, width), jnp.bfloat16),
        ),
        flops=2 * rows * updates * width * 4,
        bytes_accessed=8_000_000,
        grid=(rows // block,),
        in_specs=[
            SMEM,
            pl.BlockSpec((1, updates), lambda i: (0, 0)),
            by_rows,
            by_rows,
            pl.BlockSpec((updates, width), lambda i: (0, 0)),
        ],
        out_specs=(by_rows, by_rows, pl.BlockSpec((updates, width), lambda i: (0, 0))),
        scratch_shapes=[
            pltpu.VMEM((updates, 3 * width), jnp.bfloat16),
            pltpu.VMEM((updates, width), jnp.float32),
        ],
    )(count, slots, held, squares, grads)


def serve_body(role_ref, count_ref, slot_ref, arrived_ref, held_ref, new_ref, weight_ref, table_ref, lookup_ref):
    step = pl.program_id(0)
    rows = held_ref.shape[0]

    @pl.when(role_ref[0] == 0)
    def _():
        table_ref[...] = new_ref[...]
        lookup_ref[...] = weight_ref[...]

    @pl.when(role_ref[0] != 0)
    def _():
        spread = rows_of_block(used_slots(slot_ref, count_ref[0]), step * rows, rows)
        arrived = arrived_ref[...]
        sums = jnp.dot(
            spread,
            jnp.concatenate([arrived, jnp.ones_like(arrived)], axis=1),
            preferred_element_type=jnp.float32,
        )
        table = jnp.where(sums[:, LANES:] > 0.5, sums[:, :LANES], held_ref[...])
        table_ref[...] = table
        lookup_ref[...] = table.astype(jnp.bfloat16)


def serve_rows(role, count, slots, arrived, held, new_linear, weights):
    rows, width = held.shape
    updates = arrived.shape[0]
    block = 1024
    by_rows = pl.BlockSpec((block, width), lambda i: (i, 0))
    return kernel_call(
        serve_body,
        (
            jax.ShapeDtypeStruct((rows, width), jnp.float32),
            jax.ShapeDtypeStruct((rows, width), jnp.bfloat16),
        ),
        flops=2 * rows * updates * width * 2,
        bytes_accessed=5_000_000,
        grid=(rows // block,),
        in_specs=[
            SMEM,
            SMEM,
            pl.BlockSpec((1, updates), lambda i: (0, 0)),
            pl.BlockSpec((updates, width), lambda i: (0, 0)),
            by_rows,
            by_rows,
            by_rows,
        ],
        out_specs=(by_rows, by_rows),
    )(role, count, slots, arrived, held, new_linear, weights)


def one_hot_rows(column, width):
    rows = column.shape[0]
    spread = jnp.broadcast_to(column, (rows, LANES))
    within = jnp.where((spread & (LANES - 1)) == iota((rows, LANES), 1), 1.0, 0.0).astype(
        jnp.bfloat16
    )
    block = (spread >> 7).astype(jnp.float32).astype(jnp.bfloat16)
    none = jnp.zeros_like(within)
    return jnp.concatenate(
        [jnp.where(block == jnp.bfloat16(at), within, none) for at in range(width // LANES)],
        axis=1,
    )


def answer_body(request_ref, table_ref, answer_ref, columns):
    shards, capacity = request_ref.shape
    wide = jnp.concatenate(
        [request_ref[...], jnp.zeros((shards, LANES - capacity), jnp.int32)], axis=1
    )
    columns[...] = jnp.transpose(wide)[:capacity, :]
    group = 8
    for at in range(0, shards, group):
        asked = jnp.concatenate(
            [columns[:, shard : shard + 1] for shard in range(at, at + group)], axis=0
        )
        rows = jnp.dot(
            one_hot_rows(asked, table_ref.shape[0]),
            table_ref[...],
            preferred_element_type=jnp.float32,
        )
        answer_ref[at * capacity : (at + group) * capacity, :] = rows.astype(jnp.bfloat16)


def answer_rows(requests, table):
    shards, capacity = requests.shape
    rows, width = table.shape
    return kernel_call(
        answer_body,
        jax.ShapeDtypeStruct((shards * capacity, width), jnp.bfloat16),
        flops=2 * shards * capacity * rows * width,
        bytes_accessed=2_000_000,
        in_specs=[VMEM, VMEM],
        out_specs=VMEM,
        scratch_shapes=[pltpu.VMEM((capacity, shards), jnp.int32)],
    )(requests, table)


def arrange_body(place_ref, answer_ref, base_ref, columns):
    columns[...] = jnp.transpose(place_ref[...])
    examples = columns.shape[0]
    block = 256
    for field in range(base_ref.shape[1] // LANES):
        for at in range(0, examples, block):
            rows = jnp.dot(
                one_hot_rows(columns[at : at + block, field : field + 1], answer_ref.shape[0]),
                answer_ref[...],
                preferred_element_type=jnp.float32,
            )
            base_ref[at : at + block, field * LANES : (field + 1) * LANES] = rows.astype(
                jnp.bfloat16
            )


def arrange_rows(places, answers, fields):
    examples = places.shape[1]
    rows, width = answers.shape
    return kernel_call(
        arrange_body,
        jax.ShapeDtypeStruct((examples, fields * width), jnp.bfloat16),
        flops=2 * examples * fields * rows * width,
        bytes_accessed=2_000_000,
        in_specs=[VMEM, VMEM],
        out_specs=VMEM,
        scratch_shapes=[pltpu.VMEM((examples, 8), jnp.int32)],
    )(places, answers)


def cross_body(where_ref, base_ref, bias_ref, out_ref, *refs):
    block_refs, score_ref, weights = refs[: 2 * Y_SIZE], refs[2 * Y_SIZE], refs[2 * Y_SIZE + 1]
    y, core = where_ref[0], where_ref[1]
    rows, columns = block_refs[0].shape
    for ahead in range(Y_SIZE):
        first = pl.multiple_of(lax.rem(y + ahead, Y_SIZE) * rows, rows)
        for other in range(CORES):
            left = pl.multiple_of(lax.rem(core + other, CORES) * columns, columns)
            weights[pl.ds(first, rows), pl.ds(left, columns)] = block_refs[
                other * Y_SIZE + ahead
            ][...]
    width = base_ref.shape[1]
    base = base_ref[...].astype(jnp.float32)
    crossed = base
    for layer in range(bias_ref.shape[0]):
        mixed = jnp.dot(
            crossed.astype(jnp.bfloat16),
            weights[layer * width : (layer + 1) * width, :],
            preferred_element_type=jnp.float32,
        )
        crossed = base * (mixed + bias_ref[layer : layer + 1, :]) + crossed
    scores = jnp.sum(crossed * out_ref[...], axis=1, keepdims=True)
    score_ref[...] = jnp.transpose(jnp.broadcast_to(scores, (scores.shape[0], LANES)))[:8, :]


def cross_scores(where, base, bias, out_weight, blocks):
    examples, width = base.shape
    layers = bias.shape[0]
    return kernel_call(
        cross_body,
        jax.ShapeDtypeStruct((8, examples), jnp.float32),
        flops=2 * examples * width * width * layers,
        bytes_accessed=3_000_000,
        in_specs=[SMEM] + [VMEM] * (3 + len(blocks)),
        out_specs=VMEM,
        scratch_shapes=[pltpu.VMEM((layers * width, width), jnp.bfloat16)],
    )(where, base, bias, out_weight, *blocks)


def along(value, axis, partner):
    count = lax.axis_size(axis)
    return lax.ppermute(value, axis, [(source, partner(source)) for source in range(count)])


def ahead_in_y(source, steps):
    z, rest = divmod(source, Y_SIZE * X_SIZE * CORES)
    y, rest = divmod(rest, X_SIZE * CORES)
    return (z * Y_SIZE + (y - steps) % Y_SIZE) * X_SIZE * CORES + rest


Z_GROUPS = [
    [shard_at(z, y, x, core) for z in range(Z_SIZE)]
    for y in range(Y_SIZE)
    for x in range(X_SIZE)
    for core in range(CORES)
]
YZ_GROUPS = [
    [shard_at(z, y, x, core) for y in range(Y_SIZE) for z in range(Z_SIZE)]
    for x in range(X_SIZE)
    for core in range(CORES)
]


def exchange(value, axis, groups):
    return lax.all_to_all(
        value, axis, split_axis=0, concat_axis=0, tiled=True, axis_index_groups=groups
    )


def fresh_weight_blocks(role, shard, dense_state, dense_squares, dense_grads):
    layers, width, _ = dense_grads.shape
    rows = layers * width
    parts = Y_SIZE * Z_SIZE
    half = width // CORES
    piece = rows // parts
    core = shard % CORES
    at = (shard // (X_SIZE * CORES)) % Y_SIZE * Z_SIZE + shard // (Y_SIZE * X_SIZE * CORES)

    def own_piece(array):
        return lax.dynamic_slice(
            array.reshape(rows, width), (at * piece, core * half), (piece, half)
        )

    state = own_piece(dense_state)
    squares = own_piece(dense_squares)
    trained = lax.ppermute(state, "role", [(0, 1)])

    grads = dense_grads.reshape(parts, ROLES, piece // ROLES, width)

    def half_of(which):
        return lax.dynamic_slice(
            grads, (0, role, 0, which * half), (parts, 1, piece // ROLES, half)
        )[:, 0]

    pair = half_of(core) + along(half_of(1 - core), "shard", lambda s: s ^ 1)
    term = jnp.sum(exchange(pair, "shard", YZ_GROUPS), axis=0)
    both = ("role", "shard")
    side = X_SIZE * CORES // 2

    def from_ring(other_role, other_x):
        return along(term, both, lambda s: s ^ (SHARDS * other_role + side * other_x))

    mine = term + from_ring(0, 1)
    theirs = from_ring(1, 0) + from_ring(1, 1)
    trainer = role == 0
    summed = jnp.concatenate(
        [jnp.where(trainer, mine, theirs), jnp.where(trainer, theirs, mine)], axis=0
    )
    linear = jnp.where(trainer, state, trained)
    dense_linear, dense_sumsq, prior = ftrl_step(linear, squares, summed, DENSE_SHRINK)
    fresh = ftrl_weight(dense_linear, dense_sumsq, DENSE_SHRINK)
    weights = jnp.where(trainer, fresh, state + (fresh - prior)).astype(jnp.bfloat16)
    gathered = exchange(
        jnp.broadcast_to(weights, (Z_SIZE,) + weights.shape), "shard", Z_GROUPS
    ).reshape(Z_SIZE * piece, half)
    own = [gathered]
    for steps in range(1, Y_SIZE):
        own.append(along(gathered, "shard", functools.partial(ahead_in_y, steps=steps)))
    other = [along(block, "shard", lambda s: s ^ 1) for block in own]
    return own + other


def on_device(
    tables,
    row_squares,
    update_slots,
    update_counts,
    row_grads,
    dense_state,
    dense_squares,
    dense_grads,
    cross_bias,
    out_weight,
    cand_owner,
    cand_slot,
):
    role = lax.axis_index("role")
    shard = lax.axis_index("shard")
    fields = cand_owner.shape[2]
    requests, places = route(cand_owner[0].T, cand_slot[0].T)
    asked = exchange(requests, "shard", None)
    slots = update_slots.reshape(1, -1)
    new_linear, weights, fresh = train_rows(
        update_counts, slots, tables[0], row_squares, row_grads
    )
    arrived = lax.ppermute(fresh, "role", [(0, 1)])
    table_result, lookup = serve_rows(
        role.reshape(1), update_counts, slots, arrived, tables[0], new_linear, weights
    )
    blocks = fresh_weight_blocks(role, shard, dense_state[0], dense_squares, dense_grads[0])
    answers = answer_rows(asked, lookup)
    answered = exchange(answers.reshape(SHARDS, CAP, LANES), "shard", None)
    base = arrange_rows(places, answered.reshape(SHARDS * CAP, LANES), fields)
    where = jnp.stack([(shard // (X_SIZE * CORES)) % Y_SIZE, shard % CORES]).astype(jnp.int32)
    scores = cross_scores(where, base, cross_bias, out_weight.reshape(1, -1), blocks)
    return (table_result[None], scores[:1])


def solution(mesh):
    return jax.shard_map(
        on_device,
        mesh=mesh,
        in_specs=(
            P("role", "shard", None),
            P("shard", None),
            P("shard"),
            P("shard"),
            P("shard", None),
            P("role", None, None, None),
            P(),
            P("shard", None, None, None),
            P(),
            P(),
            P("role", "shard", None),
            P("role", "shard", None),
        ),
        out_specs=(P("role", "shard", None), P("role", "shard")),
        check_vma=False,
    )
```

```python
import jax
import jax.numpy as jnp
from jax import lax
from jax.experimental import pallas as pl
from jax.experimental.pallas import tpu as pltpu
from jax.sharding import PartitionSpec as P

ROW_SHRINK = 0.25
DENSE_SHRINK = 0.05
CAP = 32
LANES = 128
SHARDS = 128
ROLES = 2
Z_SIZE, Y_SIZE, X_SIZE, CORES = 8, 4, 2, 2
PLANE = Y_SIZE * X_SIZE
NEAR = 4
ASKED = 8
VMEM_LIMIT = 40 * 1024 * 1024


def ftrl_weight(linear, squares, shrink):
    return -(linear - jnp.clip(linear, -shrink, shrink)) / (1.0 + jnp.sqrt(squares))


def ftrl_step(linear, squares, gradient, shrink):
    prior = ftrl_weight(linear, squares, shrink)
    fresh_squares = squares + gradient * gradient
    sigma_step = jnp.sqrt(fresh_squares) - jnp.sqrt(squares)
    return (linear + gradient - sigma_step * prior, fresh_squares, prior)


def iota(shape, dim):
    return lax.broadcasted_iota(jnp.int32, shape, dim)


def kernel_call(body, out_shape, flops=0, bytes_accessed=0, vmem=VMEM_LIMIT, **options):
    return pl.pallas_call(
        body,
        out_shape=out_shape,
        compiler_params=pltpu.CompilerParams(vmem_limit_bytes=vmem),
        cost_estimate=pl.CostEstimate(
            flops=flops, bytes_accessed=bytes_accessed, transcendentals=0
        ),
        **options,
    )


VMEM = pl.BlockSpec(memory_space=pltpu.VMEM)
SMEM = pl.BlockSpec(memory_space=pltpu.SMEM)
ANY = pl.BlockSpec(memory_space=pl.ANY)


def position():
    shard = lax.axis_index("shard")
    core, plane = lax.rem(shard, CORES), lax.rem(shard // CORES, PLANE)
    return lax.axis_index("role"), shard, plane, core


def tile_copies(grad_ref, state_ref, square_ref, send_ref, keep_ref, own_state_ref, own_square_ref, arrived):
    role, _, plane, core = position()
    piece = own_state_ref.shape[1]
    share = piece // ROLES
    tiles = own_state_ref.shape[0]
    copies = []

    def copy(source, target):
        copies.append(pltpu.make_async_copy(source, target, arrived.at[len(copies)]))

    def columns(flip, tile):
        return pl.ds(pl.multiple_of(((core ^ flip) * tiles + tile) * LANES, LANES), LANES)

    for tile in range(tiles):
        for flip, target in ((1, send_ref), (0, keep_ref)):
            for at in range(PLANE):
                first = pl.multiple_of((plane ^ at) * piece + role * share, share)
                copy(
                    grad_ref.at[pl.ds(first, share), columns(flip, tile)],
                    target.at[at, pl.ds(tile * share, share)],
                )
        rows = pl.ds(pl.multiple_of(plane * piece, piece), piece)
        copy(state_ref.at[rows, columns(0, tile)], own_state_ref.at[tile])
        copy(square_ref.at[rows, columns(0, tile)], own_square_ref.at[tile])
    return copies


def front_body(owner_ref, slot_ref, grad_ref, state_ref, square_ref, place_ref, send_ref, keep_ref, own_state_ref, own_square_ref, arrived):
    copies = tile_copies(
        grad_ref, state_ref, square_ref, send_ref, keep_ref, own_state_ref, own_square_ref, arrived
    )
    for copy in copies:
        copy.start()
    _, shard, _, _ = position()
    fields, examples = owner_ref.shape
    shape = (SHARDS, examples)
    rows = iota(shape, 0)
    relative = owner_ref[...] ^ shard
    core, plane, z = relative & 1, (relative >> 1) & (PLANE - 1), relative >> 4
    order = (z >> 2) * 64 + core * 32 + plane * NEAR + (z & (NEAR - 1))
    member = jnp.zeros(shape, jnp.float32)
    wanted = jnp.zeros(shape, jnp.float32)
    for field in range(fields):
        named = order[field : field + 1, :] == rows
        member = jnp.where(named, 1.0, member)
        wanted = jnp.where(named, slot_ref[field : field + 1, :].astype(jnp.float32), wanted)
    earlier = jnp.where(iota((examples, examples), 0) < iota((examples, examples), 1), 1.0, 0.0)
    ranks = jnp.dot(
        member.astype(jnp.bfloat16),
        earlier.astype(jnp.bfloat16),
        preferred_element_type=jnp.float32,
    )
    places = []
    for field in range(fields):
        named = order[field : field + 1, :] == rows
        rank = jnp.sum(jnp.where(named, ranks, 0.0), axis=0, keepdims=True)
        places.append(owner_ref[field : field + 1, :] * CAP + rank.astype(jnp.int32))
    place_ref[...] = jnp.concatenate(
        places + [jnp.zeros((8 - fields, examples), jnp.int32)], axis=0
    )
    ranks = jnp.where(member > 0.5, ranks, -1.0)
    requests = jnp.zeros((SHARDS, LANES), jnp.float32)
    lanes = iota((SHARDS, LANES), 1)
    for rank in range(CAP):
        column = jnp.sum(
            jnp.where(ranks == float(rank), wanted, 0.0), axis=1, keepdims=True
        )
        requests = jnp.where(lanes == rank, column, requests)
    packed = jnp.concatenate(
        [requests[at : at + CAP, :CAP] for at in range(0, SHARDS, CAP)], axis=1
    )
    other_core = (iota(packed.shape, 1) & CAP) != 0
    dense = send_ref.shape[1] - ASKED
    for target, asked in (
        (send_ref, jnp.where(other_core, packed, 0.0)),
        (keep_ref, jnp.where(other_core, 0.0, packed)),
    ):
        for at in range(PLANE):
            target[at, dense:, :] = jnp.concatenate(
                [
                    asked[at * NEAR : (at + 1) * NEAR, :],
                    jnp.zeros((ASKED - NEAR, LANES), jnp.float32),
                ],
                axis=0,
            )
    for copy in copies:
        copy.wait()


def front(owners, slots, grads, state, squares):
    fields, examples = owners.shape
    rows, width = grads.shape
    piece, tiles = rows // PLANE, width // CORES // LANES
    blocks = jax.ShapeDtypeStruct(
        (PLANE, piece // ROLES * tiles + ASKED, LANES), jnp.float32
    )
    own = jax.ShapeDtypeStruct((tiles, piece, LANES), jnp.float32)
    return kernel_call(
        front_body,
        (jax.ShapeDtypeStruct((8, examples), jnp.int32), blocks, blocks, own, own),
        flops=10_000_000,
        bytes_accessed=4_000_000,
        vmem=60 * 1024 * 1024,
        in_specs=[VMEM, VMEM, ANY, ANY, ANY],
        out_specs=(VMEM,) * 5,
        scratch_shapes=[pltpu.SemaphoreType.DMA((tiles * (2 * PLANE + 2),))],
    )(owners, slots, grads, state, squares)


def pair_body(keep_ref, arrived_ref, *out_refs):
    for at, out_ref in enumerate(out_refs):
        out_ref[...] = keep_ref[at] + arrived_ref[at]


def pair_sums(keep, arrived):
    shape = jax.ShapeDtypeStruct(keep.shape[1:], keep.dtype)
    return kernel_call(
        pair_body, (shape,) * PLANE, in_specs=[VMEM] * 2, out_specs=(VMEM,) * PLANE
    )(keep, arrived)


def summed(refs, rows):
    values = [ref[:rows, :] for ref in refs]
    while len(values) > 1:
        values = [left + right for left, right in zip(values[::2], values[1::2])]
    return values[0]


def plane_body(*refs):
    in_refs, out_refs = refs[:PLANE], refs[PLANE:]
    dense = out_refs[0].shape[0] - ASKED
    total = summed(in_refs, dense)
    for z, out_ref in enumerate(out_refs):
        out_ref[:dense, :] = total
        out_ref[dense:, :] = jnp.concatenate(
            [ref[dense + z : dense + z + 1, :] for ref in in_refs], axis=0
        )


def plane_sums(parts):
    shape = jax.ShapeDtypeStruct(parts[0].shape, jnp.float32)
    return kernel_call(
        plane_body, (shape,) * NEAR, in_specs=[VMEM] * PLANE, out_specs=(VMEM,) * NEAR
    )(*parts)


def near_body(*refs):
    in_refs, (both_ref, dense_ref) = refs[:NEAR], refs[NEAR:]
    dense = dense_ref.shape[0]
    total = summed(in_refs, dense)
    dense_ref[...] = total
    both_ref[:dense, :] = total
    for z, ref in enumerate(in_refs):
        first = dense + z * ASKED
        both_ref[first : first + ASKED, :] = ref[dense:, :]


def near_sums(parts):
    rows = parts[0].shape[0] - ASKED
    return kernel_call(
        near_body,
        (
            jax.ShapeDtypeStruct((rows + NEAR * ASKED, LANES), jnp.float32),
            jax.ShapeDtypeStruct((rows, LANES), jnp.float32),
        ),
        in_specs=[VMEM] * NEAR,
        out_specs=(VMEM,) * 2,
    )(*parts)


def weight_body(own_ref, far_ref, other_ref, other_far_ref, state_ref, trained_ref, square_ref, out_ref):
    role = lax.axis_index("role")
    tiles, piece, _ = state_ref.shape
    share = piece // ROLES
    dense = tiles * share
    mine = own_ref[:dense, :] + far_ref[:dense, :]
    theirs = other_ref[...] + other_far_ref[...]
    parts = (jnp.where(role == 0, mine, theirs), jnp.where(role == 0, theirs, mine))
    for tile in range(tiles):
        gradient = jnp.concatenate(
            [part[tile * share : (tile + 1) * share, :] for part in parts], axis=0
        )
        state = state_ref[tile]
        linear = jnp.where(role == 0, state, trained_ref[tile * piece : (tile + 1) * piece, :])
        dense_linear, dense_sumsq, prior = ftrl_step(
            linear, square_ref[tile], gradient, DENSE_SHRINK
        )
        fresh = ftrl_weight(dense_linear, dense_sumsq, DENSE_SHRINK)
        weights = jnp.where(role == 0, fresh, state + (fresh - prior))
        out_ref[tile * piece : (tile + 1) * piece, :] = weights.astype(jnp.bfloat16)


def piece_weights(own, far, other, other_far, state, trained, squares):
    tiles, piece, _ = state.shape
    return kernel_call(
        weight_body,
        jax.ShapeDtypeStruct((tiles * piece, LANES), jnp.bfloat16),
        in_specs=[VMEM] * 7,
        out_specs=VMEM,
    )(own, far, other, other_far, state, trained, squares)


def used_slots(slot_ref, count):
    slots = slot_ref[...]
    return jnp.where(iota(slots.shape, 1) < count, slots, -1)


def rows_of_block(slots, first, rows):
    hit = slots == iota((rows, slots.shape[1]), 0) + first
    return jnp.where(hit, 1.0, 0.0).astype(jnp.bfloat16)


def train_body(count_ref, slot_ref, held_ref, square_ref, grad_ref, state_ref, new_ref, weight_ref, fresh_ref, parts, total):
    step = pl.program_id(0)
    rows = held_ref.shape[0]

    @pl.when(step == 0)
    def _():
        grads = grad_ref[...]
        high = grads.astype(jnp.bfloat16)
        rest = grads - high.astype(jnp.float32)
        middle = rest.astype(jnp.bfloat16)
        low = (rest - middle.astype(jnp.float32)).astype(jnp.bfloat16)
        parts[...] = jnp.concatenate([high, middle, low], axis=1)
        total[...] = jnp.zeros_like(total)

    spread = rows_of_block(used_slots(slot_ref, count_ref[0]), step * rows, rows)
    sums = jnp.dot(spread, parts[...], preferred_element_type=jnp.float32)
    gradient = (sums[:, :LANES] + sums[:, LANES : 2 * LANES]) + sums[:, 2 * LANES :]
    linear, squares, _ = ftrl_step(held_ref[...], square_ref[...], gradient, ROW_SHRINK)
    new_ref[...] = linear
    weights = ftrl_weight(linear, squares, ROW_SHRINK).astype(jnp.bfloat16)
    weight_ref[...] = weights
    total[...] += lax.dot_general(
        spread, weights, (((0,), (0,)), ((), ())), preferred_element_type=jnp.float32
    )

    @pl.when(step == pl.num_programs(0) - 1)
    def _():
        updates = total.shape[0]
        fresh_ref[:updates, :] = total[...]
        fresh_ref[updates:, :] = state_ref[...]


def train_rows(count, slots, held, squares, grads, state):
    rows, width = held.shape
    updates = grads.shape[0]
    block = 512
    by_rows = pl.BlockSpec((block, width), lambda i: (i, 0))
    return kernel_call(
        train_body,
        (
            jax.ShapeDtypeStruct((rows, width), jnp.float32),
            jax.ShapeDtypeStruct((rows, width), jnp.bfloat16),
            jax.ShapeDtypeStruct((updates + state.shape[0], width), jnp.float32),
        ),
        grid=(rows // block,),
        in_specs=[
            SMEM,
            pl.BlockSpec((1, updates), lambda i: (0, 0)),
            by_rows,
            by_rows,
            pl.BlockSpec((updates, width), lambda i: (0, 0)),
            pl.BlockSpec(state.shape, lambda i: (0, 0)),
        ],
        out_specs=(
            by_rows,
            by_rows,
            pl.BlockSpec((updates + state.shape[0], width), lambda i: (0, 0)),
        ),
        scratch_shapes=[
            pltpu.VMEM((updates, 3 * width), jnp.bfloat16),
            pltpu.VMEM((updates, width), jnp.float32),
        ],
    )(count, slots, held, squares, grads, state)


def serve_body(count_ref, slot_ref, arrived_ref, held_ref, new_ref, weight_ref, table_ref, lookup_ref):
    step = pl.program_id(0)
    rows = held_ref.shape[0]
    role = lax.axis_index("role")

    @pl.when(role == 0)
    def _():
        table_ref[...] = new_ref[...]
        lookup_ref[...] = weight_ref[...]

    @pl.when(role != 0)
    def _():
        spread = rows_of_block(used_slots(slot_ref, count_ref[0]), step * rows, rows)
        arrived = arrived_ref[: slot_ref.shape[1], :].astype(jnp.bfloat16)
        sums = jnp.dot(
            spread,
            jnp.concatenate([arrived, jnp.ones_like(arrived)], axis=1),
            preferred_element_type=jnp.float32,
        )
        table = jnp.where(sums[:, LANES:] > 0.5, sums[:, :LANES], held_ref[...])
        table_ref[...] = table
        lookup_ref[...] = table.astype(jnp.bfloat16)


def serve_rows(count, slots, arrived, held, new_linear, weights):
    rows, width = held.shape
    updates = slots.shape[1]
    block = 1024
    by_rows = pl.BlockSpec((block, width), lambda i: (i, 0))
    return kernel_call(
        serve_body,
        (
            jax.ShapeDtypeStruct((rows, width), jnp.float32),
            jax.ShapeDtypeStruct((rows, width), jnp.bfloat16),
        ),
        grid=(rows // block,),
        in_specs=[
            SMEM,
            pl.BlockSpec((1, updates), lambda i: (0, 0)),
            pl.BlockSpec((updates, width), lambda i: (0, 0)),
            by_rows,
            by_rows,
            by_rows,
        ],
        out_specs=(by_rows, by_rows),
    )(count, slots, arrived, held, new_linear, weights)


def looked_up(column, folded):
    rows, height = column.shape[0], folded.shape[0]
    spread = jnp.broadcast_to(column, (rows, LANES))
    within = jnp.where((spread & (LANES - 1)) == iota((rows, LANES), 1), 1.0, 0.0).astype(
        jnp.bfloat16
    )
    block = ((spread & (height - 1)) >> 7).astype(jnp.float32).astype(jnp.bfloat16)
    none = jnp.zeros_like(within)
    hot = jnp.concatenate(
        [jnp.where(block == jnp.bfloat16(at), within, none) for at in range(height // LANES)],
        axis=1,
    )
    both = jnp.dot(hot, folded, preferred_element_type=jnp.float32)
    return jnp.where(spread < height, both[:, :LANES], both[:, LANES:]).astype(jnp.bfloat16)


def fold(source_ref, target_ref):
    height = target_ref.shape[0]
    target_ref[:, :LANES] = source_ref[:height, :]
    target_ref[:, LANES:] = source_ref[height:, :]


def answer_body(near_ref, far_ref, table_ref, answer_ref, columns, folded):
    _, shard, _, _ = position()
    first = near_ref.shape[0] - NEAR * ASKED
    near, far = near_ref[first:, :], far_ref[first:, :]
    asked = jnp.where(iota(near.shape, 1) < LANES // 2, near, far)
    wide = jnp.concatenate([asked, jnp.zeros((LANES - asked.shape[0], LANES), jnp.float32)], axis=0)
    columns[...] = jnp.transpose(wide)[:, : asked.shape[0]].astype(jnp.int32)
    fold(table_ref, folded)
    for at in range(0, NEAR * PLANE, 2):
        found = looked_up(
            jnp.concatenate([columns[:, at : at + 1], columns[:, at + 1 : at + 2]], axis=0),
            folded[...],
        )
        for part in range(2 * LANES // CAP):
            row, lane = at + part // NEAR, part % NEAR
            z = (lane >> 1) * NEAR + row // PLANE
            relative = (z * PLANE + row % PLANE) * CORES + (lane & 1)
            to = pl.multiple_of((relative ^ shard) * CAP, CAP)
            answer_ref[pl.ds(to, CAP), :] = found[part * CAP : (part + 1) * CAP, :]


def answer_rows(near, far, table):
    rows, width = table.shape
    return kernel_call(
        answer_body,
        jax.ShapeDtypeStruct((SHARDS * CAP, width), jnp.bfloat16),
        flops=2 * SHARDS * CAP * rows * width,
        bytes_accessed=2_000_000,
        in_specs=[VMEM] * 3,
        out_specs=VMEM,
        scratch_shapes=[
            pltpu.VMEM((LANES, NEAR * PLANE), jnp.int32),
            pltpu.VMEM((rows // 2, 2 * width), jnp.bfloat16),
        ],
    )(near, far, table)


def arrange_body(place_ref, answer_ref, base_ref, columns, folded):
    columns[...] = jnp.transpose(place_ref[...])
    fold(answer_ref, folded)
    examples = columns.shape[0]
    block = 256
    for field in range(base_ref.shape[1] // LANES):
        for at in range(0, examples, block):
            base_ref[at : at + block, field * LANES : (field + 1) * LANES] = looked_up(
                columns[at : at + block, field : field + 1], folded[...]
            )


def arrange_rows(places, answers, fields):
    examples = places.shape[1]
    rows, width = answers.shape
    return kernel_call(
        arrange_body,
        jax.ShapeDtypeStruct((examples, fields * width), jnp.bfloat16),
        flops=2 * examples * fields * rows * width,
        bytes_accessed=2_000_000,
        in_specs=[VMEM, VMEM],
        out_specs=VMEM,
        scratch_shapes=[
            pltpu.VMEM((examples, 8), jnp.int32),
            pltpu.VMEM((rows // 2, 2 * width), jnp.bfloat16),
        ],
    )(places, answers)


def cross_body(base_ref, bias_ref, out_ref, *refs):
    block_refs, score_ref, weights = refs[:-2], refs[-2], refs[-1]
    _, _, plane, core = position()
    tiles = weights.shape[1] // LANES // CORES
    piece = block_refs[0].shape[0] // tiles
    for flip in range(CORES):
        for at in range(PLANE):
            block_ref = block_refs[flip * PLANE + at]
            first = pl.multiple_of((plane ^ at) * piece, piece)
            for tile in range(tiles):
                left = pl.multiple_of(((core ^ flip) * tiles + tile) * LANES, LANES)
                weights[pl.ds(first, piece), pl.ds(left, LANES)] = block_ref[
                    tile * piece : (tile + 1) * piece, :
                ]
    width = base_ref.shape[1]
    base = base_ref[...].astype(jnp.float32)
    crossed = base
    for layer in range(bias_ref.shape[0]):
        mixed = jnp.dot(
            crossed.astype(jnp.bfloat16),
            weights[layer * width : (layer + 1) * width, :],
            preferred_element_type=jnp.float32,
        )
        crossed = base * (mixed + bias_ref[layer : layer + 1, :]) + crossed
    scores = jnp.sum(crossed * out_ref[...], axis=1, keepdims=True)
    score_ref[...] = jnp.transpose(jnp.broadcast_to(scores, (scores.shape[0], LANES)))[:1, :]


def cross_scores(base, bias, out_weight, blocks):
    examples, width = base.shape
    layers = bias.shape[0]
    return kernel_call(
        cross_body,
        jax.ShapeDtypeStruct((1, examples), jnp.float32),
        flops=2 * examples * width * width * layers,
        bytes_accessed=3_000_000,
        in_specs=[VMEM] * (3 + len(blocks)),
        out_specs=VMEM,
        scratch_shapes=[pltpu.VMEM((layers * width, width), jnp.bfloat16)],
    )(base, bias, out_weight, *blocks)


BOTH = ("role", "shard")
CORE_BIT, PLANE_BIT, Z_BIT, FAR_BIT, ROLE_BIT = 1, 2, 16, 64, 128


def swapped(value, bits):
    count = ROLES * SHARDS
    return lax.ppermute(value, BOTH, [(source, source ^ bits) for source in range(count)])


def exchange(value):
    return lax.all_to_all(value, "shard", split_axis=0, concat_axis=0, tiled=True)


def on_device(
    tables,
    row_squares,
    update_slots,
    update_counts,
    row_grads,
    dense_state,
    dense_squares,
    dense_grads,
    cross_bias,
    out_weight,
    cand_owner,
    cand_slot,
):
    fields = cand_owner.shape[2]
    rows = dense_squares.shape[0] * dense_squares.shape[1]
    places, send, keep, own_state, own_squares = front(
        cand_owner[0].T,
        cand_slot[0].T,
        dense_grads[0].reshape(rows, -1),
        dense_state[0].reshape(rows, -1),
        dense_squares.reshape(rows, -1),
    )
    parts = pair_sums(keep, swapped(send, CORE_BIT))
    slots = update_slots.reshape(1, -1)
    new_linear, weights, fresh = train_rows(
        update_counts, slots, tables[0], row_squares, row_grads, own_state.reshape(-1, LANES)
    )
    arrived = lax.ppermute(fresh, "role", [(0, 1)])
    table_result, lookup = serve_rows(
        update_counts, slots, arrived, tables[0], new_linear, weights
    )
    parts = plane_sums(
        [parts[0]] + [swapped(parts[at], at * PLANE_BIT) for at in range(1, PLANE)]
    )
    both, dense = near_sums(
        [parts[0]] + [swapped(parts[z], z * Z_BIT) for z in range(1, NEAR)]
    )
    far = swapped(both, FAR_BIT)
    other, other_far = swapped(dense, ROLE_BIT), swapped(dense, ROLE_BIT + FAR_BIT)
    answers = answer_rows(both, far, lookup)
    answered = exchange(answers.reshape(SHARDS, CAP, LANES))
    piece = piece_weights(
        both, far, other, other_far, own_state, arrived[slots.shape[1] :], own_squares
    )
    blocks = [piece] + [swapped(piece, at * PLANE_BIT) for at in range(1, PLANE)]
    blocks = blocks + [swapped(block, CORE_BIT) for block in blocks]
    base = arrange_rows(places, answered.reshape(SHARDS * CAP, LANES), fields)
    scores = cross_scores(base, cross_bias, out_weight.reshape(1, -1), blocks)
    return (table_result[None], scores)


def solution(mesh):
    return jax.shard_map(
        on_device,
        mesh=mesh,
        in_specs=(
            P("role", "shard", None),
            P("shard", None),
            P("shard"),
            P("shard"),
            P("shard", None),
            P("role", None, None, None),
            P(),
            P("shard", None, None, None),
            P(),
            P(),
            P("role", "shard", None),
            P("role", "shard", None),
        ),
        out_specs=(P("role", "shard", None), P("role", "shard")),
        check_vma=False,
    )
```

```python
import jax
import jax.numpy as jnp
from jax import lax
from jax.experimental import pallas as pl
from jax.experimental.pallas import tpu as pltpu
from jax.sharding import PartitionSpec as P

ROW_SHRINK = 0.25
DENSE_SHRINK = 0.05
CAP = 32
LANES = 128
SHARDS = 128
ROLES = 2
CORES = 2
TILES = 2
SHARE = 12
PACKED = 16
VMEM_LIMIT = 40 * 1024 * 1024


def ftrl_weight(linear, squares, shrink):
    return -(linear - jnp.clip(linear, -shrink, shrink)) / (1.0 + jnp.sqrt(squares))


def ftrl_step(linear, squares, gradient, shrink):
    prior = ftrl_weight(linear, squares, shrink)
    fresh_squares = squares + gradient * gradient
    sigma_step = jnp.sqrt(fresh_squares) - jnp.sqrt(squares)
    return (linear + gradient - sigma_step * prior, fresh_squares, prior)


def iota(shape, dim):
    return lax.broadcasted_iota(jnp.int32, shape, dim)


def kernel_call(body, out_shape, flops=0, bytes_accessed=0, vmem=VMEM_LIMIT, **options):
    return pl.pallas_call(
        body,
        out_shape=out_shape,
        compiler_params=pltpu.CompilerParams(vmem_limit_bytes=vmem),
        cost_estimate=pl.CostEstimate(
            flops=flops, bytes_accessed=bytes_accessed, transcendentals=0
        ),
        **options,
    )


VMEM = pl.BlockSpec(memory_space=pltpu.VMEM)
SMEM = pl.BlockSpec(memory_space=pltpu.SMEM)
ANY = pl.BlockSpec(memory_space=pl.ANY)


def position():
    shard = lax.axis_index("shard")
    return lax.axis_index("role"), shard, lax.rem(shard, CORES)


def piece_copies(array_ref, own_ref):
    _, shard, _ = position()
    rows = array_ref.shape[0] // ROLES
    pairs = []
    for half in range(ROLES):
        first = pl.multiple_of(half * rows + shard // 4 * (2 * SHARE), 2 * SHARE)
        for core in range(CORES):
            left = pl.multiple_of((core * TILES + lax.rem(shard, TILES)) * LANES, LANES)
            pairs.append(
                (
                    array_ref.at[pl.ds(first, 2 * SHARE), pl.ds(left, LANES)],
                    own_ref.at[half, core],
                )
            )
    return pairs


def half_copies(grad_ref, send_ref, keep_ref):
    role, _, core = position()
    rows = grad_ref.shape[0] // ROLES
    pairs = []
    for flip, target in ((1, send_ref), (0, keep_ref)):
        for tile in range(TILES):
            left = pl.multiple_of(((core ^ flip) * TILES + tile) * LANES, LANES)
            first = pl.multiple_of(role * rows, rows)
            pairs.append(
                (grad_ref.at[pl.ds(first, rows), pl.ds(left, LANES)], target.at[tile])
            )
    return pairs


def front_body(owner_ref, slot_ref, grad_ref, state_ref, square_ref, place_ref, request_ref, send_ref, keep_ref, own_state_ref, own_square_ref, arrived):
    pairs = (
        half_copies(grad_ref, send_ref, keep_ref)
        + piece_copies(state_ref, own_state_ref)
        + piece_copies(square_ref, own_square_ref)
    )
    copies = [
        pltpu.make_async_copy(source, target, arrived.at[at])
        for at, (source, target) in enumerate(pairs)
    ]
    for copy in copies:
        copy.start()
    fields, examples = owner_ref.shape
    shape = (SHARDS, examples)
    shard_ids = iota(shape, 0)
    member = jnp.zeros(shape, jnp.float32)
    wanted = jnp.zeros(shape, jnp.float32)
    for field in range(fields):
        named = owner_ref[field : field + 1, :] == shard_ids
        member = jnp.where(named, 1.0, member)
        wanted = jnp.where(named, slot_ref[field : field + 1, :].astype(jnp.float32), wanted)
    earlier = jnp.where(iota((examples, examples), 0) < iota((examples, examples), 1), 1.0, 0.0)
    ranks = jnp.dot(
        member.astype(jnp.bfloat16),
        earlier.astype(jnp.bfloat16),
        preferred_element_type=jnp.float32,
    )
    places = []
    for field in range(fields):
        owners = owner_ref[field : field + 1, :]
        rank = jnp.sum(jnp.where(owners == shard_ids, ranks, 0.0), axis=0, keepdims=True)
        places.append(owners * CAP + rank.astype(jnp.int32))
    place_ref[...] = jnp.concatenate(
        places + [jnp.zeros((8 - fields, examples), jnp.int32)], axis=0
    )
    ranks = jnp.where(member > 0.5, ranks, -1.0)
    requests = jnp.zeros((SHARDS, LANES), jnp.float32)
    lanes = iota((SHARDS, LANES), 1)
    for rank in range(CAP):
        column = jnp.sum(
            jnp.where(ranks == float(rank), wanted, 0.0), axis=1, keepdims=True
        )
        requests = jnp.where(lanes == rank, column, requests)
    asked = requests[:, :CAP].astype(jnp.int32)
    request_ref[...] = jnp.concatenate(
        [asked >> 4, asked & 15, jnp.zeros((SHARDS, LANES - 2 * CAP), jnp.int32)], axis=1
    ).astype(jnp.float32)
    for copy in copies:
        copy.wait()


def front(owners, slots, grads, state, squares):
    fields, examples = owners.shape
    halves = jax.ShapeDtypeStruct((TILES, grads.shape[0] // ROLES, LANES), jnp.float32)
    own = jax.ShapeDtypeStruct((ROLES, CORES, 2 * SHARE, LANES), jnp.float32)
    return kernel_call(
        front_body,
        (
            jax.ShapeDtypeStruct((8, examples), jnp.int32),
            jax.ShapeDtypeStruct((SHARDS, LANES), jnp.float32),
            halves,
            halves,
            own,
            own,
        ),
        flops=10_000_000,
        bytes_accessed=4_000_000,
        vmem=60 * 1024 * 1024,
        in_specs=[VMEM, VMEM, ANY, ANY, ANY],
        out_specs=(VMEM,) * 6,
        scratch_shapes=[pltpu.SemaphoreType.DMA((2 * TILES + 4 * ROLES,))],
    )(owners, slots, grads, state, squares)


def pack_body(keep_ref, arrived_ref, request_ref, packed_ref):
    for block in range(SHARDS // 4):
        rows = slice(block * 2 * SHARE, (block + 1) * 2 * SHARE)
        for tile in range(TILES):
            terms = keep_ref[tile, rows, :] + arrived_ref[tile, rows, :]
            for part in range(2):
                shard = block * 4 + part * TILES + tile
                packed_ref[shard] = jnp.concatenate(
                    [
                        terms[part * SHARE : (part + 1) * SHARE, :],
                        request_ref[shard : shard + 1, :],
                        jnp.zeros((PACKED - SHARE - 1, LANES), jnp.float32),
                    ],
                    axis=0,
                ).astype(jnp.bfloat16)


def pack(keep, arrived, requests):
    return kernel_call(
        pack_body,
        jax.ShapeDtypeStruct((SHARDS, PACKED, LANES), jnp.bfloat16),
        in_specs=[VMEM] * 3,
        out_specs=VMEM,
    )(keep, arrived, requests)


def unpack_body(packed_ref, sum_ref, asked_ref):
    for core in range(CORES):
        total = jnp.zeros((PACKED, LANES), jnp.float32)
        for shard in range(core, SHARDS, CORES):
            packed = packed_ref[shard].astype(jnp.float32)
            total = total + packed
            asked_ref[shard : shard + 1, :] = packed[SHARE : SHARE + 1, :]
        sum_ref[core] = total


def unpack(packed):
    return kernel_call(
        unpack_body,
        (
            jax.ShapeDtypeStruct((CORES, PACKED, LANES), jnp.float32),
            jax.ShapeDtypeStruct((SHARDS, LANES), jnp.float32),
        ),
        in_specs=[VMEM],
        out_specs=(VMEM, VMEM),
    )(packed)


def used_slots(slot_ref, count):
    slots = slot_ref[...]
    return jnp.where(iota(slots.shape, 1) < count, slots, -1)


def rows_of_block(slots, first, rows):
    hit = slots == iota((rows, slots.shape[1]), 0) + first
    return jnp.where(hit, 1.0, 0.0).astype(jnp.bfloat16)


def train_body(count_ref, slot_ref, held_ref, square_ref, grad_ref, state_ref, new_ref, weight_ref, fresh_ref, parts, total):
    step = pl.program_id(0)
    rows = held_ref.shape[0]

    @pl.when(step == 0)
    def _():
        grads = grad_ref[...]
        high = grads.astype(jnp.bfloat16)
        rest = grads - high.astype(jnp.float32)
        middle = rest.astype(jnp.bfloat16)
        low = (rest - middle.astype(jnp.float32)).astype(jnp.bfloat16)
        parts[...] = jnp.concatenate([high, middle, low], axis=1)
        total[...] = jnp.zeros_like(total)

    spread = rows_of_block(used_slots(slot_ref, count_ref[0]), step * rows, rows)
    sums = jnp.dot(spread, parts[...], preferred_element_type=jnp.float32)
    gradient = (sums[:, :LANES] + sums[:, LANES : 2 * LANES]) + sums[:, 2 * LANES :]
    linear, squares, _ = ftrl_step(held_ref[...], square_ref[...], gradient, ROW_SHRINK)
    new_ref[...] = linear
    weights = ftrl_weight(linear, squares, ROW_SHRINK).astype(jnp.bfloat16)
    weight_ref[...] = weights
    total[...] += lax.dot_general(
        spread, weights, (((0,), (0,)), ((), ())), preferred_element_type=jnp.float32
    )

    @pl.when(step == pl.num_programs(0) - 1)
    def _():
        updates = total.shape[0]
        fresh_ref[:updates, :] = total[...]
        fresh_ref[updates:, :] = state_ref[...]


def train_rows(count, slots, held, squares, grads, state):
    rows, width = held.shape
    updates = grads.shape[0]
    block = 512
    by_rows = pl.BlockSpec((block, width), lambda i: (i, 0))
    return kernel_call(
        train_body,
        (
            jax.ShapeDtypeStruct((rows, width), jnp.float32),
            jax.ShapeDtypeStruct((rows, width), jnp.bfloat16),
            jax.ShapeDtypeStruct((updates + state.shape[0], width), jnp.float32),
        ),
        grid=(rows // block,),
        in_specs=[
            SMEM,
            pl.BlockSpec((1, updates), lambda i: (0, 0)),
            by_rows,
            by_rows,
            pl.BlockSpec((updates, width), lambda i: (0, 0)),
            pl.BlockSpec(state.shape, lambda i: (0, 0)),
        ],
        out_specs=(
            by_rows,
            by_rows,
            pl.BlockSpec((updates + state.shape[0], width), lambda i: (0, 0)),
        ),
        scratch_shapes=[
            pltpu.VMEM((updates, 3 * width), jnp.bfloat16),
            pltpu.VMEM((updates, width), jnp.float32),
        ],
    )(count, slots, held, squares, grads, state)


def serve_body(count_ref, slot_ref, arrived_ref, held_ref, new_ref, weight_ref, table_ref, lookup_ref):
    step = pl.program_id(0)
    rows = held_ref.shape[0]
    role = lax.axis_index("role")

    @pl.when(role == 0)
    def _():
        table_ref[...] = new_ref[...]
        lookup_ref[...] = weight_ref[...]

    @pl.when(role != 0)
    def _():
        spread = rows_of_block(used_slots(slot_ref, count_ref[0]), step * rows, rows)
        arrived = arrived_ref[: slot_ref.shape[1], :].astype(jnp.bfloat16)
        sums = jnp.dot(
            spread,
            jnp.concatenate([arrived, jnp.ones_like(arrived)], axis=1),
            preferred_element_type=jnp.float32,
        )
        table = jnp.where(sums[:, LANES:] > 0.5, sums[:, :LANES], held_ref[...])
        table_ref[...] = table
        lookup_ref[...] = table.astype(jnp.bfloat16)


def serve_rows(count, slots, arrived, held, new_linear, weights):
    rows, width = held.shape
    updates = slots.shape[1]
    block = 1024
    by_rows = pl.BlockSpec((block, width), lambda i: (i, 0))
    return kernel_call(
        serve_body,
        (
            jax.ShapeDtypeStruct((rows, width), jnp.float32),
            jax.ShapeDtypeStruct((rows, width), jnp.bfloat16),
        ),
        grid=(rows // block,),
        in_specs=[
            SMEM,
            pl.BlockSpec((1, updates), lambda i: (0, 0)),
            pl.BlockSpec((updates, width), lambda i: (0, 0)),
            by_rows,
            by_rows,
            by_rows,
        ],
        out_specs=(by_rows, by_rows),
    )(count, slots, arrived, held, new_linear, weights)


def looked_up(column, folded):
    rows, height = column.shape[0], folded.shape[0]
    spread = jnp.broadcast_to(column, (rows, LANES))
    within = jnp.where((spread & (LANES - 1)) == iota((rows, LANES), 1), 1.0, 0.0).astype(
        jnp.bfloat16
    )
    block = ((spread & (height - 1)) >> 7).astype(jnp.float32).astype(jnp.bfloat16)
    none = jnp.zeros_like(within)
    hot = jnp.concatenate(
        [jnp.where(block == jnp.bfloat16(at), within, none) for at in range(height // LANES)],
        axis=1,
    )
    both = jnp.dot(hot, folded, preferred_element_type=jnp.float32)
    return jnp.where(spread < height, both[:, :LANES], both[:, LANES:]).astype(jnp.bfloat16)


def fold(source_ref, target_ref):
    height = target_ref.shape[0]
    target_ref[:, :LANES] = source_ref[:height, :]
    target_ref[:, LANES:] = source_ref[height:, :]


def piece_weights(sum_ref, other_ref, state_ref, trained_ref, square_ref):
    role, shard, _ = position()
    later = lax.rem(shard // TILES, 2) == 1

    def own(values):
        return jnp.where(later, values[SHARE : 2 * SHARE, :], values[:SHARE, :])

    halves = []
    for half in range(ROLES):
        parts = []
        for core in range(CORES):
            gradient = jnp.where(role == half, sum_ref[core], other_ref[core])[:SHARE, :]
            first = (half * CORES + core) * 2 * SHARE
            state = own(state_ref[half, core])
            trained = own(trained_ref[first : first + 2 * SHARE, :])
            linear = jnp.where(role == 0, state, trained)
            dense_linear, dense_sumsq, prior = ftrl_step(
                linear, own(square_ref[half, core]), gradient, DENSE_SHRINK
            )
            fresh = ftrl_weight(dense_linear, dense_sumsq, DENSE_SHRINK)
            parts.append(jnp.where(role == 0, fresh, state + (fresh - prior)))
        halves.append(jnp.concatenate(parts, axis=0).astype(jnp.bfloat16))
    return halves


def answer_body(asked_ref, table_ref, sum_ref, other_ref, state_ref, trained_ref, square_ref, answer_ref, columns, folded):
    digits = asked_ref[...]
    wide = jnp.concatenate(
        [
            digits[:, :CAP] * 16.0 + digits[:, CAP : 2 * CAP],
            jnp.zeros((SHARDS, LANES - CAP), jnp.float32),
        ],
        axis=1,
    )
    columns[...] = jnp.transpose(wide)[:CAP, :].astype(jnp.int32)
    fold(table_ref, folded)
    halves = piece_weights(sum_ref, other_ref, state_ref, trained_ref, square_ref)
    group = 8
    for at in range(0, SHARDS, group):
        asked = jnp.concatenate(
            [columns[:, shard : shard + 1] for shard in range(at, at + group)], axis=0
        )
        found = looked_up(asked, folded[...])
        for part in range(group):
            answer_ref[at + part] = jnp.concatenate(
                [found[part * CAP : (part + 1) * CAP, :], halves[(at + part) % CORES]], axis=0
            )


def answer_rows(asked, table, sums, other_sums, state, trained, squares):
    rows, width = table.shape
    return kernel_call(
        answer_body,
        jax.ShapeDtypeStruct((SHARDS, CAP + CORES * SHARE, width), jnp.bfloat16),
        flops=2 * SHARDS * CAP * rows * width,
        bytes_accessed=2_000_000,
        in_specs=[VMEM] * 7,
        out_specs=VMEM,
        scratch_shapes=[
            pltpu.VMEM((CAP, SHARDS), jnp.int32),
            pltpu.VMEM((rows // 2, 2 * width), jnp.bfloat16),
        ],
    )(asked, table, sums, other_sums, state, trained, squares)


def collect_body(answer_ref, half_ref):
    for block in range(SHARDS // 8):
        for core in range(CORES):
            for tile in range(TILES):
                first = CAP + core * SHARE
                parts = [
                    answer_ref[block * 8 + part * TILES + tile].astype(jnp.float32)[
                        first : first + SHARE, :
                    ]
                    for part in range(4)
                ]
                left = (core * TILES + tile) * LANES
                half_ref[block * 4 * SHARE : (block + 1) * 4 * SHARE, left : left + LANES] = (
                    jnp.concatenate(parts, axis=0).astype(jnp.bfloat16)
                )


def collect(answers):
    return kernel_call(
        collect_body,
        jax.ShapeDtypeStruct(
            (SHARDS // 2 * SHARE, CORES * TILES * LANES), jnp.bfloat16
        ),
        in_specs=[VMEM],
        out_specs=VMEM,
    )(answers)


def arrange_body(place_ref, answer_ref, base_ref, columns, folded):
    columns[...] = jnp.transpose(place_ref[...])
    for shard in range(SHARDS):
        side, at = divmod(shard, SHARDS // 2)
        folded[at * CAP : (at + 1) * CAP, side * LANES : (side + 1) * LANES] = answer_ref[shard][
            :CAP, :
        ]
    examples = columns.shape[0]
    block = 256
    for field in range(base_ref.shape[1] // LANES):
        for at in range(0, examples, block):
            base_ref[at : at + block, field * LANES : (field + 1) * LANES] = looked_up(
                columns[at : at + block, field : field + 1], folded[...]
            )


def arrange_rows(places, answers, fields):
    examples = places.shape[1]
    rows, width = SHARDS * CAP, answers.shape[2]
    return kernel_call(
        arrange_body,
        jax.ShapeDtypeStruct((examples, fields * width), jnp.bfloat16),
        flops=2 * examples * fields * rows * width,
        bytes_accessed=2_000_000,
        in_specs=[VMEM, VMEM],
        out_specs=VMEM,
        scratch_shapes=[
            pltpu.VMEM((examples, 8), jnp.int32),
            pltpu.VMEM((rows // 2, 2 * width), jnp.bfloat16),
        ],
    )(places, answers)


def cross_body(base_ref, bias_ref, out_ref, own_ref, other_ref, score_ref, weights):
    _, _, core = position()
    rows = own_ref.shape[0]
    weights[pl.ds(pl.multiple_of(core * rows, rows), rows), :] = own_ref[...]
    weights[pl.ds(pl.multiple_of((1 - core) * rows, rows), rows), :] = other_ref[...]
    width = base_ref.shape[1]
    base = base_ref[...].astype(jnp.float32)
    crossed = base
    for layer in range(bias_ref.shape[0]):
        mixed = jnp.dot(
            crossed.astype(jnp.bfloat16),
            weights[layer * width : (layer + 1) * width, :],
            preferred_element_type=jnp.float32,
        )
        crossed = base * (mixed + bias_ref[layer : layer + 1, :]) + crossed
    scores = jnp.sum(crossed * out_ref[...], axis=1, keepdims=True)
    score_ref[...] = jnp.transpose(jnp.broadcast_to(scores, (scores.shape[0], LANES)))[:1, :]


def cross_scores(base, bias, out_weight, own, other):
    examples, width = base.shape
    layers = bias.shape[0]
    return kernel_call(
        cross_body,
        jax.ShapeDtypeStruct((1, examples), jnp.float32),
        flops=2 * examples * width * width * layers,
        bytes_accessed=3_000_000,
        in_specs=[VMEM] * 5,
        out_specs=VMEM,
        scratch_shapes=[pltpu.VMEM((layers * width, width), jnp.bfloat16)],
    )(base, bias, out_weight, own, other)


BOTH = ("role", "shard")
CORE_BIT, ROLE_BIT = 1, 128


def swapped(value, bits):
    count = ROLES * SHARDS
    return lax.ppermute(value, BOTH, [(source, source ^ bits) for source in range(count)])


def exchange(value):
    return lax.all_to_all(value, "shard", split_axis=0, concat_axis=0, tiled=True)


def on_device(
    tables,
    row_squares,
    update_slots,
    update_counts,
    row_grads,
    dense_state,
    dense_squares,
    dense_grads,
    cross_bias,
    out_weight,
    cand_owner,
    cand_slot,
):
    fields = cand_owner.shape[2]
    rows = dense_squares.shape[0] * dense_squares.shape[1]
    places, requests, send, keep, own_state, own_squares = front(
        cand_owner[0].T,
        cand_slot[0].T,
        dense_grads[0].reshape(rows, -1),
        dense_state[0].reshape(rows, -1),
        dense_squares.reshape(rows, -1),
    )
    sums, asked = unpack(exchange(pack(keep, swapped(send, CORE_BIT), requests)))
    slots = update_slots.reshape(1, -1)
    new_linear, weights, fresh = train_rows(
        update_counts, slots, tables[0], row_squares, row_grads, own_state.reshape(-1, LANES)
    )
    arrived = lax.ppermute(fresh, "role", [(0, 1)])
    table_result, lookup = serve_rows(
        update_counts, slots, arrived, tables[0], new_linear, weights
    )
    answers = exchange(
        answer_rows(
            asked,
            lookup,
            sums,
            swapped(sums, ROLE_BIT),
            own_state,
            arrived[slots.shape[1] :],
            own_squares,
        )
    )
    half = collect(answers)
    base = arrange_rows(places, answers, fields)
    scores = cross_scores(
        base, cross_bias, out_weight.reshape(1, -1), half, swapped(half, CORE_BIT)
    )
    return (table_result[None], scores)


def solution(mesh):
    return jax.shard_map(
        on_device,
        mesh=mesh,
        in_specs=(
            P("role", "shard", None),
            P("shard", None),
            P("shard"),
            P("shard"),
            P("shard", None),
            P("role", None, None, None),
            P(),
            P("shard", None, None, None),
            P(),
            P(),
            P("role", "shard", None),
            P("role", "shard", None),
        ),
        out_specs=(P("role", "shard", None), P("role", "shard")),
        check_vma=False,
    )
```

```python
import jax
import jax.numpy as jnp
from jax import lax
from jax.experimental import pallas as pl
from jax.experimental.pallas import tpu as pltpu
from jax.sharding import PartitionSpec as P

ROW_SHRINK = 0.25
DENSE_SHRINK = 0.05
CAP = 32
LANES = 128
SHARDS = 128
ROLES = 2
Z_SIZE, Y_SIZE, X_SIZE, CORES = 8, 4, 2, 2
BLOCKS = Z_SIZE * Y_SIZE
Z_ORDER = (0, 1, 7, 3, 4, 2, 5, 6)
TILES = 2
SHARE = 12
PACKED = 16
VMEM_LIMIT = 24 * 1024 * 1024


def ftrl_weight(linear, squares, shrink):
    return -(linear - jnp.clip(linear, -shrink, shrink)) / (1.0 + jnp.sqrt(squares))


def ftrl_step(linear, squares, gradient, shrink):
    prior = ftrl_weight(linear, squares, shrink)
    fresh_squares = squares + gradient * gradient
    sigma_step = jnp.sqrt(fresh_squares) - jnp.sqrt(squares)
    return (linear + gradient - sigma_step * prior, fresh_squares, prior)


def iota(shape, dim):
    return lax.broadcasted_iota(jnp.int32, shape, dim)


def kernel_call(body, out_shape, flops=0, bytes_accessed=0, vmem=VMEM_LIMIT, **options):
    return pl.pallas_call(
        body,
        out_shape=out_shape,
        compiler_params=pltpu.CompilerParams(vmem_limit_bytes=vmem),
        cost_estimate=pl.CostEstimate(
            flops=flops, bytes_accessed=bytes_accessed, transcendentals=0
        ),
        **options,
    )


VMEM = pl.BlockSpec(memory_space=pltpu.VMEM)
SMEM = pl.BlockSpec(memory_space=pltpu.SMEM)
ANY = pl.BlockSpec(memory_space=pl.ANY)
HBM = pl.BlockSpec(memory_space=pltpu.HBM)


def position():
    shard = lax.axis_index("shard")
    return lax.axis_index("role"), shard, lax.rem(shard, CORES)


def half_copies(grad_ref, target_ref, flip, arrived):
    role, _, core = position()
    copies = []
    for tile in range(TILES):
        left = pl.multiple_of(((core ^ flip) * TILES + tile) * LANES, LANES)
        copies.append(
            pltpu.make_async_copy(
                grad_ref.at[:, role, :, pl.ds(left, LANES)], target_ref.at[tile], arrived.at[tile]
            )
        )
    return copies


def fetch_body(grad_ref, state_ref, square_ref, send_ref, keep_ref, own_state_ref, own_square_ref, arrived):
    _, shard, core = position()
    copies = half_copies(grad_ref, send_ref, 1, arrived.at[:TILES])
    copies += half_copies(grad_ref, keep_ref, 0, arrived.at[TILES : 2 * TILES])
    block = shard // (X_SIZE * CORES)
    for source, target in ((state_ref, own_state_ref), (square_ref, own_square_ref)):
        for column in range(CORES):
            left = pl.multiple_of((column * TILES + core) * LANES, LANES)
            copies.append(
                pltpu.make_async_copy(
                    source.at[block, :, :, pl.ds(left, LANES)],
                    target.at[column],
                    arrived.at[len(copies)],
                )
            )
    for copy in copies:
        copy.start()
    for copy in copies:
        copy.wait()


def fetch(grads, state, squares):
    halves = jax.ShapeDtypeStruct((TILES, BLOCKS, 2 * SHARE, LANES), jnp.float32)
    own = jax.ShapeDtypeStruct((CORES, ROLES, 2 * SHARE, LANES), jnp.float32)
    return kernel_call(
        fetch_body,
        (halves, halves, own, own),
        bytes_accessed=4_000_000,
        vmem=52 * 1024 * 1024,
        in_specs=[HBM] * 3,
        out_specs=(VMEM,) * 4,
        scratch_shapes=[pltpu.SemaphoreType.DMA((2 * TILES + 2 * CORES,))],
    )(grads, state, squares)


def route_body(owner_ref, slot_ref, place_ref, request_ref):
    fields, examples = owner_ref.shape
    shape = (SHARDS, examples)
    shard_ids = iota(shape, 0)
    member = jnp.zeros(shape, jnp.float32)
    wanted = jnp.zeros(shape, jnp.float32)
    for field in range(fields):
        named = owner_ref[field : field + 1, :] == shard_ids
        member = jnp.where(named, 1.0, member)
        wanted = jnp.where(named, slot_ref[field : field + 1, :].astype(jnp.float32), wanted)
    earlier = jnp.where(iota((examples, examples), 0) < iota((examples, examples), 1), 1.0, 0.0)
    ranks = jnp.dot(
        member.astype(jnp.bfloat16),
        earlier.astype(jnp.bfloat16),
        preferred_element_type=jnp.float32,
    )
    places = []
    for field in range(fields):
        owners = owner_ref[field : field + 1, :]
        rank = jnp.sum(jnp.where(owners == shard_ids, ranks, 0.0), axis=0, keepdims=True)
        places.append(owners * CAP + rank.astype(jnp.int32))
    place_ref[...] = jnp.concatenate(
        places + [jnp.zeros((8 - fields, examples), jnp.int32)], axis=0
    )
    ranks = jnp.where(member > 0.5, ranks, -1.0)
    requests = jnp.zeros((SHARDS, LANES), jnp.float32)
    lanes = iota((SHARDS, LANES), 1)
    for rank in range(CAP):
        column = jnp.sum(
            jnp.where(ranks == float(rank), wanted, 0.0), axis=1, keepdims=True
        )
        requests = jnp.where(lanes == rank, column, requests)
    asked = requests[:, :CAP].astype(jnp.int32)
    request_ref[...] = jnp.concatenate(
        [asked >> 4, asked & 15, jnp.zeros((SHARDS, LANES - 2 * CAP), jnp.int32)], axis=1
    ).astype(jnp.float32)


def route(owners, slots):
    examples = owners.shape[1]
    return kernel_call(
        route_body,
        (
            jax.ShapeDtypeStruct((8, examples), jnp.int32),
            jax.ShapeDtypeStruct((SHARDS, LANES), jnp.float32),
        ),
        in_specs=[VMEM, VMEM],
        out_specs=(VMEM, VMEM),
    )(owners, slots)


def pack_body(keep_ref, arrived_ref, request_ref, packed_ref):
    for block in range(BLOCKS):
        for tile in range(TILES):
            terms = keep_ref[tile, block] + arrived_ref[tile, block]
            for part in range(X_SIZE):
                shard = (block * X_SIZE + part) * CORES + tile
                packed_ref[shard] = jnp.concatenate(
                    [
                        terms[part * SHARE : (part + 1) * SHARE, :],
                        request_ref[shard : shard + 1, :],
                        jnp.zeros((PACKED - SHARE - 1, LANES), jnp.float32),
                    ],
                    axis=0,
                ).astype(jnp.bfloat16)


def pack(keep, arrived, requests):
    return kernel_call(
        pack_body,
        jax.ShapeDtypeStruct((SHARDS, PACKED, LANES), jnp.bfloat16),
        in_specs=[VMEM] * 3,
        out_specs=VMEM,
    )(keep, arrived, requests)


def unpack_body(packed_ref, lookup_ref, sum_ref, asked_ref):
    for core in range(CORES):
        total = jnp.zeros((PACKED, LANES), jnp.float32)
        for shard in range(core, SHARDS, CORES):
            packed = packed_ref[shard].astype(jnp.float32)
            total = total + packed
            asked_ref[shard : shard + 1, :] = packed[SHARE : SHARE + 1, :]
        sum_ref[core] = total


def unpack(packed, lookup):
    return kernel_call(
        unpack_body,
        (
            jax.ShapeDtypeStruct((CORES, PACKED, LANES), jnp.float32),
            jax.ShapeDtypeStruct((SHARDS, LANES), jnp.float32),
        ),
        in_specs=[VMEM, ANY],
        out_specs=(VMEM, VMEM),
    )(packed, lookup)


def used_slots(slot_ref, count):
    slots = slot_ref[...]
    return jnp.where(iota(slots.shape, 1) < count, slots, -1)


def rows_of_block(slots, first, rows):
    hit = slots == iota((rows, slots.shape[1]), 0) + first
    return jnp.where(hit, 1.0, 0.0).astype(jnp.bfloat16)


def train_body(count_ref, slot_ref, held_ref, square_ref, grad_ref, new_ref, weight_ref, fresh_ref, parts, total):
    step = pl.program_id(0)
    rows = held_ref.shape[0]

    @pl.when(step == 0)
    def _():
        grads = grad_ref[...]
        high = grads.astype(jnp.bfloat16)
        rest = grads - high.astype(jnp.float32)
        middle = rest.astype(jnp.bfloat16)
        low = (rest - middle.astype(jnp.float32)).astype(jnp.bfloat16)
        parts[...] = jnp.concatenate([high, middle, low], axis=1)
        total[...] = jnp.zeros_like(total)

    spread = rows_of_block(used_slots(slot_ref, count_ref[0]), step * rows, rows)
    sums = jnp.dot(spread, parts[...], preferred_element_type=jnp.float32)
    gradient = (sums[:, :LANES] + sums[:, LANES : 2 * LANES]) + sums[:, 2 * LANES :]
    linear, squares, _ = ftrl_step(held_ref[...], square_ref[...], gradient, ROW_SHRINK)
    new_ref[...] = linear
    weights = ftrl_weight(linear, squares, ROW_SHRINK).astype(jnp.bfloat16)
    weight_ref[...] = weights
    total[...] += lax.dot_general(
        spread, weights, (((0,), (0,)), ((), ())), preferred_element_type=jnp.float32
    )

    @pl.when(step == pl.num_programs(0) - 1)
    def _():
        fresh_ref[...] = total[...].astype(jnp.bfloat16)


def train_rows(count, slots, held, squares, grads):
    rows, width = held.shape
    updates = grads.shape[0]
    block = 512
    by_rows = pl.BlockSpec((block, width), lambda i: (i, 0))
    return kernel_call(
        train_body,
        (
            jax.ShapeDtypeStruct((rows, width), jnp.float32),
            jax.ShapeDtypeStruct((rows, width), jnp.bfloat16),
            jax.ShapeDtypeStruct((updates, width), jnp.bfloat16),
        ),
        grid=(rows // block,),
        in_specs=[
            SMEM,
            pl.BlockSpec((1, updates), lambda i: (0, 0)),
            by_rows,
            by_rows,
            pl.BlockSpec((updates, width), lambda i: (0, 0)),
        ],
        out_specs=(
            by_rows,
            by_rows,
            pl.BlockSpec((updates, width), lambda i: (0, 0)),
        ),
        scratch_shapes=[
            pltpu.VMEM((updates, 3 * width), jnp.bfloat16),
            pltpu.VMEM((updates, width), jnp.float32),
        ],
    )(count, slots, held, squares, grads)


def serve_body(count_ref, slot_ref, arrived_ref, held_ref, new_ref, weight_ref, table_ref, lookup_ref):
    step = pl.program_id(0)
    rows = held_ref.shape[0]
    role = lax.axis_index("role")

    @pl.when(role == 0)
    def _():
        table_ref[...] = new_ref[...]
        lookup_ref[...] = weight_ref[...]

    @pl.when(role != 0)
    def _():
        spread = rows_of_block(used_slots(slot_ref, count_ref[0]), step * rows, rows)
        arrived = arrived_ref[...]
        sums = jnp.dot(
            spread,
            jnp.concatenate([arrived, jnp.ones_like(arrived)], axis=1),
            preferred_element_type=jnp.float32,
        )
        table = jnp.where(sums[:, LANES:] > 0.5, sums[:, :LANES], held_ref[...])
        table_ref[...] = table
        lookup_ref[...] = table.astype(jnp.bfloat16)


def serve_rows(count, slots, arrived, held, new_linear, weights):
    rows, width = held.shape
    updates = slots.shape[1]
    block = 1024
    by_rows = pl.BlockSpec((block, width), lambda i: (i, 0))
    return kernel_call(
        serve_body,
        (
            jax.ShapeDtypeStruct((rows, width), jnp.float32),
            jax.ShapeDtypeStruct((rows, width), jnp.bfloat16),
        ),
        grid=(rows // block,),
        in_specs=[
            SMEM,
            pl.BlockSpec((1, updates), lambda i: (0, 0)),
            pl.BlockSpec((updates, width), lambda i: (0, 0)),
            by_rows,
            by_rows,
            by_rows,
        ],
        out_specs=(by_rows, by_rows),
    )(count, slots, arrived, held, new_linear, weights)


def looked_up(column, folded):
    rows, height = column.shape[0], folded.shape[0]
    spread = jnp.broadcast_to(column, (rows, LANES))
    within = jnp.where((spread & (LANES - 1)) == iota((rows, LANES), 1), 1.0, 0.0).astype(
        jnp.bfloat16
    )
    block = ((spread & (height - 1)) >> 7).astype(jnp.float32).astype(jnp.bfloat16)
    none = jnp.zeros_like(within)
    hot = jnp.concatenate(
        [jnp.where(block == jnp.bfloat16(at), within, none) for at in range(height // LANES)],
        axis=1,
    )
    both = jnp.dot(hot, folded, preferred_element_type=jnp.float32)
    return jnp.where(spread < height, both[:, :LANES], both[:, LANES:]).astype(jnp.bfloat16)


def fold(source_ref, target_ref):
    height = target_ref.shape[0]
    target_ref[:, :LANES] = source_ref[:height, :]
    target_ref[:, LANES:] = source_ref[height:, :]


def piece_body(sum_ref, other_ref, state_ref, trained_ref, square_ref, answer_ref, piece_ref):
    role, shard, _ = position()
    later = lax.rem(shard // CORES, X_SIZE) == 1

    def own(values):
        return jnp.where(later, values[SHARE : 2 * SHARE, :], values[:SHARE, :])

    parts = []
    for half in range(ROLES):
        for column in range(CORES):
            gradient = jnp.where(role == half, sum_ref[column], other_ref[column])[:SHARE, :]
            state = own(state_ref[column, half])
            trained = own(trained_ref[column, half])
            linear = jnp.where(role == 0, state, trained)
            dense_linear, dense_sumsq, prior = ftrl_step(
                linear, own(square_ref[column, half]), gradient, DENSE_SHRINK
            )
            fresh = ftrl_weight(dense_linear, dense_sumsq, DENSE_SHRINK)
            parts.append(jnp.where(role == 0, fresh, state + (fresh - prior)))
    piece_ref[...] = jnp.concatenate(parts, axis=0).astype(jnp.bfloat16)


def piece_weights(sums, other, state, trained, squares, answers):
    return kernel_call(
        piece_body,
        jax.ShapeDtypeStruct((ROLES * CORES * SHARE, LANES), jnp.bfloat16),
        in_specs=[VMEM] * 5 + [ANY],
        out_specs=VMEM,
    )(sums, other, state, trained, squares, answers)


def answer_body(asked_ref, table_ref, answer_ref, columns, folded):
    digits = asked_ref[...]
    wide = jnp.concatenate(
        [
            digits[:, :CAP] * 16.0 + digits[:, CAP : 2 * CAP],
            jnp.zeros((SHARDS, LANES - CAP), jnp.float32),
        ],
        axis=1,
    )
    columns[...] = jnp.transpose(wide)[:CAP, :].astype(jnp.int32)
    fold(table_ref, folded)
    group = 8
    for at in range(0, SHARDS, group):
        asked = jnp.concatenate(
            [columns[:, shard : shard + 1] for shard in range(at, at + group)], axis=0
        )
        answer_ref[at * CAP : (at + group) * CAP, :] = looked_up(asked, folded[...])


def answer_rows(asked, table):
    rows, width = table.shape
    return kernel_call(
        answer_body,
        jax.ShapeDtypeStruct((SHARDS * CAP, width), jnp.bfloat16),
        in_specs=[VMEM] * 2,
        out_specs=VMEM,
        scratch_shapes=[
            pltpu.VMEM((CAP, SHARDS), jnp.int32),
            pltpu.VMEM((rows // 2, 2 * width), jnp.bfloat16),
        ],
    )(asked, table)


def after_body(value_ref, other_ref, out_ref):
    del value_ref, other_ref, out_ref


def after(value, other):
    return kernel_call(
        after_body,
        jax.ShapeDtypeStruct(value.shape, value.dtype),
        in_specs=[ANY, ANY],
        out_specs=ANY,
        input_output_aliases={0: 0},
    )(value, other)


def collect_body(*refs):
    piece_refs, tile_ref = refs[:Y_SIZE], refs[Y_SIZE]
    _, shard, _ = position()
    x = lax.rem(shard // CORES, X_SIZE)
    y = lax.rem(shard // (X_SIZE * CORES), Y_SIZE)
    z = shard // (Y_SIZE * X_SIZE * CORES)
    piece = ROLES * CORES * SHARE
    for y_flip, ref in enumerate(piece_refs):
        for at, steps in enumerate(Z_ORDER):
            near = ref[at * piece : (at + 1) * piece, :].astype(jnp.float32)
            far = ref[(Z_SIZE + at) * piece : (Z_SIZE + at + 1) * piece, :].astype(jnp.float32)
            first, second = jnp.where(x == 0, near, far), jnp.where(x == 0, far, near)
            block = lax.rem(z + steps, Z_SIZE) * Y_SIZE + (y ^ y_flip)
            rows = pl.ds(pl.multiple_of(block * piece, piece), piece)
            for column in range(CORES):
                parts = []
                for half in range(ROLES):
                    start = (half * CORES + column) * SHARE
                    parts += [values[start : start + SHARE, :] for values in (first, second)]
                tile_ref[column, rows, :] = jnp.concatenate(parts, axis=0).astype(jnp.bfloat16)


def collect(pieces):
    rows = BLOCKS * ROLES * X_SIZE * SHARE
    return kernel_call(
        collect_body,
        jax.ShapeDtypeStruct((CORES, rows, LANES), jnp.bfloat16),
        in_specs=[VMEM] * Y_SIZE,
        out_specs=VMEM,
    )(*pieces)


def arrange_body(place_ref, answer_ref, base_ref, columns, folded):
    columns[...] = jnp.transpose(place_ref[...])
    fold(answer_ref, folded)
    examples = columns.shape[0]
    block = 256
    for field in range(base_ref.shape[1] // LANES):
        for at in range(0, examples, block):
            base_ref[at : at + block, field * LANES : (field + 1) * LANES] = looked_up(
                columns[at : at + block, field : field + 1], folded[...]
            )


def arrange_rows(places, answers, fields):
    examples = places.shape[1]
    rows, width = answers.shape
    return kernel_call(
        arrange_body,
        jax.ShapeDtypeStruct((examples, fields * width), jnp.bfloat16),
        flops=2 * examples * fields * rows * width,
        bytes_accessed=2_000_000,
        in_specs=[VMEM, VMEM],
        out_specs=VMEM,
        scratch_shapes=[
            pltpu.VMEM((examples, 8), jnp.int32),
            pltpu.VMEM((rows // 2, 2 * width), jnp.bfloat16),
        ],
    )(places, answers)


def cross_body(base_ref, bias_ref, out_ref, own_ref, other_ref, score_ref, weights):
    _, _, core = position()
    for column in range(CORES):
        for flip, tile_ref in ((0, own_ref), (1, other_ref)):
            left = pl.multiple_of((column * TILES + (core ^ flip)) * LANES, LANES)
            weights[:, pl.ds(left, LANES)] = tile_ref[column]
    width = base_ref.shape[1]
    base = base_ref[...].astype(jnp.float32)
    crossed = base
    for layer in range(bias_ref.shape[0]):
        mixed = jnp.dot(
            crossed.astype(jnp.bfloat16),
            weights[layer * width : (layer + 1) * width, :],
            preferred_element_type=jnp.float32,
        )
        crossed = base * (mixed + bias_ref[layer : layer + 1, :]) + crossed
    scores = jnp.sum(crossed * out_ref[...], axis=1, keepdims=True)
    score_ref[...] = jnp.transpose(jnp.broadcast_to(scores, (scores.shape[0], LANES)))[:1, :]


def cross_scores(base, bias, out_weight, own, other):
    examples, width = base.shape
    layers = bias.shape[0]
    return kernel_call(
        cross_body,
        jax.ShapeDtypeStruct((1, examples), jnp.float32),
        flops=2 * examples * width * width * layers,
        bytes_accessed=3_000_000,
        in_specs=[VMEM] * 5,
        out_specs=VMEM,
        scratch_shapes=[pltpu.VMEM((layers * width, width), jnp.bfloat16)],
    )(base, bias, out_weight, own, other)


BOTH = ("role", "shard")
CORE_BIT, X_BIT, Y_BIT, ROLE_BIT = 1, 2, 4, 128


def swapped(value, bits):
    count = ROLES * SHARDS
    return lax.ppermute(value, BOTH, [(source, source ^ bits) for source in range(count)])


def from_ahead(value, steps):
    span = SHARDS // Z_SIZE
    return lax.ppermute(
        value,
        "shard",
        [((source + steps * span) % SHARDS, source) for source in range(SHARDS)],
    )


def exchange(value):
    return lax.all_to_all(value, "shard", split_axis=0, concat_axis=0, tiled=True)


def on_device(
    tables,
    row_squares,
    update_slots,
    update_counts,
    row_grads,
    dense_state,
    dense_squares,
    dense_grads,
    cross_bias,
    out_weight,
    cand_owner,
    cand_slot,
):
    fields = cand_owner.shape[2]
    blocks = (BLOCKS, ROLES, 2 * SHARE, dense_squares.shape[2])
    grads = dense_grads.reshape(blocks)
    send, keep, own_state, own_squares = fetch(
        grads, dense_state.reshape(blocks), dense_squares.reshape(blocks)
    )
    paired = swapped(send, CORE_BIT)
    trained = lax.ppermute(own_state, "role", [(0, 1)])
    places, requests = route(cand_owner[0].T, cand_slot[0].T)
    packed = exchange(pack(keep, paired, requests))
    slots = update_slots.reshape(1, -1)
    new_linear, weights, fresh = train_rows(
        update_counts, slots, tables[0], row_squares, row_grads
    )
    arrived = lax.ppermute(fresh, "role", [(0, 1)])
    table_result, lookup = serve_rows(
        update_counts, slots, arrived, tables[0], new_linear, weights
    )
    sums, asked = unpack(packed, lookup)
    answers = answer_rows(asked, lookup)
    piece = piece_weights(
        sums, swapped(sums, ROLE_BIT), own_state, trained, own_squares, answers
    )
    near = [piece, from_ahead(piece, 1), from_ahead(piece, -1)]
    three = jnp.concatenate(near, axis=0)
    pieces = jnp.concatenate(
        [three, from_ahead(three, 3), from_ahead(three[: 2 * piece.shape[0]], -3)], axis=0
    )
    answers = after(answers, pieces)
    answered = exchange(answers.reshape(SHARDS, CAP, LANES))
    pieces = jnp.concatenate([pieces, swapped(pieces, X_BIT)], axis=0)
    tiles = collect(
        [pieces] + [swapped(pieces, flip * Y_BIT) for flip in range(1, Y_SIZE)]
    )
    base = arrange_rows(places, answered.reshape(SHARDS * CAP, LANES), fields)
    scores = cross_scores(
        base, cross_bias, out_weight.reshape(1, -1), tiles, swapped(tiles, CORE_BIT)
    )
    return (table_result[None], scores)


def solution(mesh):
    return jax.shard_map(
        on_device,
        mesh=mesh,
        in_specs=(
            P("role", "shard", None),
            P("shard", None),
            P("shard"),
            P("shard"),
            P("shard", None),
            P("role", None, None, None),
            P(),
            P("shard", None, None, None),
            P(),
            P(),
            P("role", "shard", None),
            P("role", "shard", None),
        ),
        out_specs=(P("role", "shard", None), P("role", "shard")),
        check_vma=False,
    )
```

```python
import jax
import jax.numpy as jnp
from jax import lax
from jax.experimental import pallas as pl
from jax.experimental.pallas import tpu as pltpu
from jax.sharding import PartitionSpec as P

ROW_SHRINK = 0.25
DENSE_SHRINK = 0.05
CAP = 32
LANES = 128
SHARDS = 128
ROLES = 2
Z_SIZE, Y_SIZE, X_SIZE, CORES = 8, 4, 2, 2
BLOCKS = Z_SIZE * Y_SIZE
Z_ORDER = (0, 1, 7, 3, 4, 2, 6, 5)
TILES = 2
SHARE = 12
PACKED = 16
VMEM_LIMIT = 24 * 1024 * 1024


def ftrl_weight(linear, squares, shrink):
    return -(linear - jnp.clip(linear, -shrink, shrink)) / (1.0 + jnp.sqrt(squares))


def ftrl_step(linear, squares, gradient, shrink):
    prior = ftrl_weight(linear, squares, shrink)
    fresh_squares = squares + gradient * gradient
    sigma_step = jnp.sqrt(fresh_squares) - jnp.sqrt(squares)
    return (linear + gradient - sigma_step * prior, fresh_squares, prior)


def iota(shape, dim):
    return lax.broadcasted_iota(jnp.int32, shape, dim)


def kernel_call(body, out_shape, flops=0, bytes_accessed=0, vmem=VMEM_LIMIT, **options):
    return pl.pallas_call(
        body,
        out_shape=out_shape,
        compiler_params=pltpu.CompilerParams(vmem_limit_bytes=vmem),
        cost_estimate=pl.CostEstimate(
            flops=flops, bytes_accessed=bytes_accessed, transcendentals=0
        ),
        **options,
    )


VMEM = pl.BlockSpec(memory_space=pltpu.VMEM)
SMEM = pl.BlockSpec(memory_space=pltpu.SMEM)
ANY = pl.BlockSpec(memory_space=pl.ANY)
HBM = pl.BlockSpec(memory_space=pltpu.HBM)


def position():
    shard = lax.axis_index("shard")
    return lax.axis_index("role"), shard, lax.rem(shard, CORES)


def half_copies(grad_ref, target_ref, flip, arrived):
    role, _, core = position()
    copies = []
    for tile in range(TILES):
        left = pl.multiple_of(((core ^ flip) * TILES + tile) * LANES, LANES)
        copies.append(
            pltpu.make_async_copy(
                grad_ref.at[:, role, :, pl.ds(left, LANES)], target_ref.at[tile], arrived.at[tile]
            )
        )
    return copies


def fetch_body(grad_ref, state_ref, square_ref, send_ref, keep_ref, own_state_ref, own_square_ref, arrived):
    _, shard, core = position()
    copies = half_copies(grad_ref, send_ref, 1, arrived.at[:TILES])
    copies += half_copies(grad_ref, keep_ref, 0, arrived.at[TILES : 2 * TILES])
    block = shard // (X_SIZE * CORES)
    for source, target in ((state_ref, own_state_ref), (square_ref, own_square_ref)):
        for column in range(CORES):
            left = pl.multiple_of((column * TILES + core) * LANES, LANES)
            copies.append(
                pltpu.make_async_copy(
                    source.at[block, :, :, pl.ds(left, LANES)],
                    target.at[column],
                    arrived.at[len(copies)],
                )
            )
    for copy in copies:
        copy.start()
    for copy in copies:
        copy.wait()


def fetch(grads, state, squares):
    halves = jax.ShapeDtypeStruct((TILES, BLOCKS, 2 * SHARE, LANES), jnp.float32)
    own = jax.ShapeDtypeStruct((CORES, ROLES, 2 * SHARE, LANES), jnp.float32)
    return kernel_call(
        fetch_body,
        (halves, halves, own, own),
        bytes_accessed=4_000_000,
        vmem=52 * 1024 * 1024,
        in_specs=[HBM] * 3,
        out_specs=(VMEM,) * 4,
        scratch_shapes=[pltpu.SemaphoreType.DMA((2 * TILES + 2 * CORES,))],
    )(grads, state, squares)


def route_body(owner_ref, slot_ref, place_ref, request_ref):
    fields, examples = owner_ref.shape
    shape = (SHARDS, examples)
    shard_ids = iota(shape, 0)
    member = jnp.zeros(shape, jnp.float32)
    wanted = jnp.zeros(shape, jnp.float32)
    for field in range(fields):
        named = owner_ref[field : field + 1, :] == shard_ids
        member = jnp.where(named, 1.0, member)
        wanted = jnp.where(named, slot_ref[field : field + 1, :].astype(jnp.float32), wanted)
    earlier = jnp.where(iota((examples, examples), 0) < iota((examples, examples), 1), 1.0, 0.0)
    ranks = jnp.dot(
        member.astype(jnp.bfloat16),
        earlier.astype(jnp.bfloat16),
        preferred_element_type=jnp.float32,
    )
    places = []
    for field in range(fields):
        owners = owner_ref[field : field + 1, :]
        rank = jnp.sum(jnp.where(owners == shard_ids, ranks, 0.0), axis=0, keepdims=True)
        places.append(owners * CAP + rank.astype(jnp.int32))
    place_ref[...] = jnp.concatenate(
        places + [jnp.zeros((8 - fields, examples), jnp.int32)], axis=0
    )
    ranks = jnp.where(member > 0.5, ranks, -1.0)
    requests = jnp.zeros((SHARDS, LANES), jnp.float32)
    lanes = iota((SHARDS, LANES), 1)
    for rank in range(CAP):
        column = jnp.sum(
            jnp.where(ranks == float(rank), wanted, 0.0), axis=1, keepdims=True
        )
        requests = jnp.where(lanes == rank, column, requests)
    asked = requests[:, :CAP].astype(jnp.int32)
    request_ref[...] = jnp.concatenate(
        [asked >> 4, asked & 15, jnp.zeros((SHARDS, LANES - 2 * CAP), jnp.int32)], axis=1
    ).astype(jnp.float32)


def route(owners, slots):
    examples = owners.shape[1]
    return kernel_call(
        route_body,
        (
            jax.ShapeDtypeStruct((8, examples), jnp.int32),
            jax.ShapeDtypeStruct((SHARDS, LANES), jnp.float32),
        ),
        in_specs=[VMEM, VMEM],
        out_specs=(VMEM, VMEM),
    )(owners, slots)


def pack_body(keep_ref, arrived_ref, request_ref, packed_ref):
    for block in range(BLOCKS):
        for tile in range(TILES):
            terms = keep_ref[tile, block] + arrived_ref[tile, block]
            for part in range(X_SIZE):
                shard = (block * X_SIZE + part) * CORES + tile
                packed_ref[shard] = jnp.concatenate(
                    [
                        terms[part * SHARE : (part + 1) * SHARE, :],
                        request_ref[shard : shard + 1, :],
                        jnp.zeros((PACKED - SHARE - 1, LANES), jnp.float32),
                    ],
                    axis=0,
                ).astype(jnp.bfloat16)


def pack(keep, arrived, requests):
    return kernel_call(
        pack_body,
        jax.ShapeDtypeStruct((SHARDS, PACKED, LANES), jnp.bfloat16),
        in_specs=[VMEM] * 3,
        out_specs=VMEM,
    )(keep, arrived, requests)


def unpack_body(packed_ref, lookup_ref, sum_ref, asked_ref):
    for core in range(CORES):
        total = jnp.zeros((PACKED, LANES), jnp.float32)
        for shard in range(core, SHARDS, CORES):
            packed = packed_ref[shard].astype(jnp.float32)
            total = total + packed
            asked_ref[shard : shard + 1, :] = packed[SHARE : SHARE + 1, :]
        sum_ref[core] = total


def unpack(packed, lookup):
    return kernel_call(
        unpack_body,
        (
            jax.ShapeDtypeStruct((CORES, PACKED, LANES), jnp.float32),
            jax.ShapeDtypeStruct((SHARDS, LANES), jnp.float32),
        ),
        in_specs=[VMEM, ANY],
        out_specs=(VMEM, VMEM),
    )(packed, lookup)


def used_slots(slot_ref, count):
    slots = slot_ref[...]
    return jnp.where(iota(slots.shape, 1) < count, slots, -1)


def rows_of_block(slots, first, rows):
    hit = slots == iota((rows, slots.shape[1]), 0) + first
    return jnp.where(hit, 1.0, 0.0).astype(jnp.bfloat16)


def train_body(count_ref, slot_ref, held_ref, square_ref, grad_ref, new_ref, weight_ref, fresh_ref, parts, total):
    step = pl.program_id(0)
    rows = held_ref.shape[0]

    @pl.when(step == 0)
    def _():
        grads = grad_ref[...]
        high = grads.astype(jnp.bfloat16)
        rest = grads - high.astype(jnp.float32)
        middle = rest.astype(jnp.bfloat16)
        low = (rest - middle.astype(jnp.float32)).astype(jnp.bfloat16)
        parts[...] = jnp.concatenate([high, middle, low], axis=1)
        total[...] = jnp.zeros_like(total)

    spread = rows_of_block(used_slots(slot_ref, count_ref[0]), step * rows, rows)
    sums = jnp.dot(spread, parts[...], preferred_element_type=jnp.float32)
    gradient = (sums[:, :LANES] + sums[:, LANES : 2 * LANES]) + sums[:, 2 * LANES :]
    linear, squares, _ = ftrl_step(held_ref[...], square_ref[...], gradient, ROW_SHRINK)
    new_ref[...] = linear
    weights = ftrl_weight(linear, squares, ROW_SHRINK).astype(jnp.bfloat16)
    weight_ref[...] = weights
    total[...] += lax.dot_general(
        spread, weights, (((0,), (0,)), ((), ())), preferred_element_type=jnp.float32
    )

    @pl.when(step == pl.num_programs(0) - 1)
    def _():
        fresh_ref[...] = total[...].astype(jnp.bfloat16)


def train_rows(count, slots, held, squares, grads):
    rows, width = held.shape
    updates = grads.shape[0]
    block = 512
    by_rows = pl.BlockSpec((block, width), lambda i: (i, 0))
    return kernel_call(
        train_body,
        (
            jax.ShapeDtypeStruct((rows, width), jnp.float32),
            jax.ShapeDtypeStruct((rows, width), jnp.bfloat16),
            jax.ShapeDtypeStruct((updates, width), jnp.bfloat16),
        ),
        grid=(rows // block,),
        in_specs=[
            SMEM,
            pl.BlockSpec((1, updates), lambda i: (0, 0)),
            by_rows,
            by_rows,
            pl.BlockSpec((updates, width), lambda i: (0, 0)),
        ],
        out_specs=(
            by_rows,
            by_rows,
            pl.BlockSpec((updates, width), lambda i: (0, 0)),
        ),
        scratch_shapes=[
            pltpu.VMEM((updates, 3 * width), jnp.bfloat16),
            pltpu.VMEM((updates, width), jnp.float32),
        ],
    )(count, slots, held, squares, grads)


def serve_body(count_ref, slot_ref, arrived_ref, held_ref, new_ref, weight_ref, table_ref, lookup_ref):
    step = pl.program_id(0)
    rows = held_ref.shape[0]
    role = lax.axis_index("role")

    @pl.when(role == 0)
    def _():
        table_ref[...] = new_ref[...]
        lookup_ref[...] = weight_ref[...]

    @pl.when(role != 0)
    def _():
        spread = rows_of_block(used_slots(slot_ref, count_ref[0]), step * rows, rows)
        arrived = arrived_ref[...]
        sums = jnp.dot(
            spread,
            jnp.concatenate([arrived, jnp.ones_like(arrived)], axis=1),
            preferred_element_type=jnp.float32,
        )
        table = jnp.where(sums[:, LANES:] > 0.5, sums[:, :LANES], held_ref[...])
        table_ref[...] = table
        lookup_ref[...] = table.astype(jnp.bfloat16)


def serve_rows(count, slots, arrived, held, new_linear, weights):
    rows, width = held.shape
    updates = slots.shape[1]
    block = 1024
    by_rows = pl.BlockSpec((block, width), lambda i: (i, 0))
    return kernel_call(
        serve_body,
        (
            jax.ShapeDtypeStruct((rows, width), jnp.float32),
            jax.ShapeDtypeStruct((rows, width), jnp.bfloat16),
        ),
        grid=(rows // block,),
        in_specs=[
            SMEM,
            pl.BlockSpec((1, updates), lambda i: (0, 0)),
            pl.BlockSpec((updates, width), lambda i: (0, 0)),
            by_rows,
            by_rows,
            by_rows,
        ],
        out_specs=(by_rows, by_rows),
    )(count, slots, arrived, held, new_linear, weights)


def looked_up(column, folded):
    rows, height = column.shape[0], folded.shape[0]
    spread = jnp.broadcast_to(column, (rows, LANES))
    within = jnp.where((spread & (LANES - 1)) == iota((rows, LANES), 1), 1.0, 0.0).astype(
        jnp.bfloat16
    )
    block = ((spread & (height - 1)) >> 7).astype(jnp.float32).astype(jnp.bfloat16)
    none = jnp.zeros_like(within)
    hot = jnp.concatenate(
        [jnp.where(block == jnp.bfloat16(at), within, none) for at in range(height // LANES)],
        axis=1,
    )
    both = jnp.dot(hot, folded, preferred_element_type=jnp.float32)
    return jnp.where(spread < height, both[:, :LANES], both[:, LANES:]).astype(jnp.bfloat16)


def fold(source_ref, target_ref):
    height = target_ref.shape[0]
    target_ref[:, :LANES] = source_ref[:height, :]
    target_ref[:, LANES:] = source_ref[height:, :]


def piece_body(sum_ref, other_ref, state_ref, trained_ref, square_ref, piece_ref):
    role, shard, _ = position()
    later = lax.rem(shard // CORES, X_SIZE) == 1

    def own(values):
        return jnp.where(later, values[SHARE : 2 * SHARE, :], values[:SHARE, :])

    parts = []
    for half in range(ROLES):
        for column in range(CORES):
            gradient = jnp.where(role == half, sum_ref[column], other_ref[column])[:SHARE, :]
            state = own(state_ref[column, half])
            trained = own(trained_ref[column, half])
            linear = jnp.where(role == 0, state, trained)
            dense_linear, dense_sumsq, prior = ftrl_step(
                linear, own(square_ref[column, half]), gradient, DENSE_SHRINK
            )
            fresh = ftrl_weight(dense_linear, dense_sumsq, DENSE_SHRINK)
            parts.append(jnp.where(role == 0, fresh, state + (fresh - prior)))
    piece_ref[...] = jnp.concatenate(parts, axis=0).astype(jnp.bfloat16)


def piece_weights(sums, other, state, trained, squares):
    return kernel_call(
        piece_body,
        jax.ShapeDtypeStruct((ROLES * CORES * SHARE, LANES), jnp.bfloat16),
        in_specs=[VMEM] * 5,
        out_specs=VMEM,
    )(sums, other, state, trained, squares)


def answer_body(asked_ref, table_ref, late_ref, answer_ref, columns, folded):
    digits = asked_ref[...]
    wide = jnp.concatenate(
        [
            digits[:, :CAP] * 16.0 + digits[:, CAP : 2 * CAP],
            jnp.zeros((SHARDS, LANES - CAP), jnp.float32),
        ],
        axis=1,
    )
    columns[...] = jnp.transpose(wide)[:CAP, :].astype(jnp.int32)
    fold(table_ref, folded)
    group = 8
    for at in range(0, SHARDS, group):
        asked = jnp.concatenate(
            [columns[:, shard : shard + 1] for shard in range(at, at + group)], axis=0
        )
        answer_ref[at * CAP : (at + group) * CAP, :] = looked_up(asked, folded[...])


def answer_rows(asked, table, late):
    rows, width = table.shape
    return kernel_call(
        answer_body,
        jax.ShapeDtypeStruct((SHARDS * CAP, width), jnp.bfloat16),
        in_specs=[VMEM] * 2 + [ANY],
        out_specs=VMEM,
        scratch_shapes=[
            pltpu.VMEM((CAP, SHARDS), jnp.int32),
            pltpu.VMEM((rows // 2, 2 * width), jnp.bfloat16),
        ],
    )(asked, table, late)


def after_body(value_ref, other_ref, out_ref):
    del value_ref, other_ref, out_ref


def after(value, other):
    return kernel_call(
        after_body,
        jax.ShapeDtypeStruct(value.shape, value.dtype),
        in_specs=[ANY, ANY],
        out_specs=ANY,
        input_output_aliases={0: 0},
    )(value, other)


def collect_body(*refs):
    piece_refs, tile_ref = refs[:Y_SIZE], refs[Y_SIZE]
    _, shard, _ = position()
    x = lax.rem(shard // CORES, X_SIZE)
    y = lax.rem(shard // (X_SIZE * CORES), Y_SIZE)
    z = shard // (Y_SIZE * X_SIZE * CORES)
    piece = ROLES * CORES * SHARE
    for y_flip, ref in enumerate(piece_refs):
        for at, steps in enumerate(Z_ORDER):
            near = ref[at * piece : (at + 1) * piece, :].astype(jnp.float32)
            far = ref[(Z_SIZE + at) * piece : (Z_SIZE + at + 1) * piece, :].astype(jnp.float32)
            first, second = jnp.where(x == 0, near, far), jnp.where(x == 0, far, near)
            block = lax.rem(z + steps, Z_SIZE) * Y_SIZE + (y ^ y_flip)
            rows = pl.ds(pl.multiple_of(block * piece, piece), piece)
            for column in range(CORES):
                parts = []
                for half in range(ROLES):
                    start = (half * CORES + column) * SHARE
                    parts += [values[start : start + SHARE, :] for values in (first, second)]
                tile_ref[rows, column * LANES : (column + 1) * LANES] = jnp.concatenate(
                    parts, axis=0
                ).astype(jnp.bfloat16)


def collect(pieces):
    rows = BLOCKS * ROLES * X_SIZE * SHARE
    return kernel_call(
        collect_body,
        jax.ShapeDtypeStruct((rows, CORES * LANES), jnp.bfloat16),
        in_specs=[VMEM] * Y_SIZE,
        out_specs=VMEM,
    )(*pieces)


def arrange_body(place_ref, answer_ref, base_ref, columns, folded):
    columns[...] = jnp.transpose(place_ref[...])
    fold(answer_ref, folded)
    examples = columns.shape[0]
    block = 256
    for field in range(base_ref.shape[1] // LANES):
        for at in range(0, examples, block):
            base_ref[at : at + block, field * LANES : (field + 1) * LANES] = looked_up(
                columns[at : at + block, field : field + 1], folded[...]
            )


def arrange_rows(places, answers, fields):
    examples = places.shape[1]
    rows, width = answers.shape
    return kernel_call(
        arrange_body,
        jax.ShapeDtypeStruct((examples, fields * width), jnp.bfloat16),
        flops=2 * examples * fields * rows * width,
        bytes_accessed=2_000_000,
        in_specs=[VMEM, VMEM],
        out_specs=VMEM,
        scratch_shapes=[
            pltpu.VMEM((examples, 8), jnp.int32),
            pltpu.VMEM((rows // 2, 2 * width), jnp.bfloat16),
        ],
    )(places, answers)


def cross_body(base_ref, bias_ref, out_ref, own_ref, other_ref, score_ref):
    _, _, core = position()
    width = base_ref.shape[1]
    base = base_ref[...].astype(jnp.float32)
    crossed = base
    for layer in range(bias_ref.shape[0]):
        rows = slice(layer * width, (layer + 1) * width)
        inputs = crossed.astype(jnp.bfloat16)
        own, other = (
            jnp.dot(inputs, tile_ref[rows, :], preferred_element_type=jnp.float32)
            for tile_ref in (own_ref, other_ref)
        )
        even, odd = jnp.where(core == 0, own, other), jnp.where(core == 0, other, own)
        mixed = jnp.concatenate(
            [
                tiles[:, column * LANES : (column + 1) * LANES]
                for column in range(CORES)
                for tiles in (even, odd)
            ],
            axis=1,
        )
        crossed = base * (mixed + bias_ref[layer : layer + 1, :]) + crossed
    scores = jnp.sum(crossed * out_ref[...], axis=1, keepdims=True)
    score_ref[...] = jnp.transpose(jnp.broadcast_to(scores, (scores.shape[0], LANES)))[:1, :]


def cross_scores(base, bias, out_weight, own, other):
    examples, width = base.shape
    return kernel_call(
        cross_body,
        jax.ShapeDtypeStruct((1, examples), jnp.float32),
        flops=2 * examples * width * width * bias.shape[0],
        bytes_accessed=3_000_000,
        in_specs=[VMEM] * 5,
        out_specs=VMEM,
    )(base, bias, out_weight, own, other)


BOTH = ("role", "shard")
CORE_BIT, X_BIT, Y_BIT, ROLE_BIT = 1, 2, 4, 128


def swapped(value, bits):
    count = ROLES * SHARDS
    return lax.ppermute(value, BOTH, [(source, source ^ bits) for source in range(count)])


def from_ahead(value, steps):
    span = SHARDS // Z_SIZE
    return lax.ppermute(
        value,
        "shard",
        [((source + steps * span) % SHARDS, source) for source in range(SHARDS)],
    )


def exchange(value):
    return lax.all_to_all(value, "shard", split_axis=0, concat_axis=0, tiled=True)


def on_device(
    tables,
    row_squares,
    update_slots,
    update_counts,
    row_grads,
    dense_state,
    dense_squares,
    dense_grads,
    cross_bias,
    out_weight,
    cand_owner,
    cand_slot,
):
    fields = cand_owner.shape[2]
    blocks = (BLOCKS, ROLES, 2 * SHARE, dense_squares.shape[2])
    grads = dense_grads.reshape(blocks)
    send, keep, own_state, own_squares = fetch(
        grads, dense_state.reshape(blocks), dense_squares.reshape(blocks)
    )
    paired = swapped(send, CORE_BIT)
    trained = lax.ppermute(own_state, "role", [(0, 1)])
    places, requests = route(cand_owner[0].T, cand_slot[0].T)
    packed = exchange(pack(keep, paired, requests))
    slots = update_slots.reshape(1, -1)
    new_linear, weights, fresh = train_rows(
        update_counts, slots, tables[0], row_squares, row_grads
    )
    arrived = lax.ppermute(fresh, "role", [(0, 1)])
    table_result, lookup = serve_rows(
        update_counts, slots, arrived, tables[0], new_linear, weights
    )
    sums, asked = unpack(packed, lookup)
    piece = piece_weights(
        sums, swapped(sums, ROLE_BIT), own_state, trained, own_squares
    )
    ahead, behind = from_ahead(piece, 1), from_ahead(piece, -1)
    three = jnp.concatenate([piece, ahead, behind], axis=0)
    pieces = jnp.concatenate(
        [
            three,
            from_ahead(three, 3),
            from_ahead(jnp.concatenate([piece, behind], axis=0), -2),
        ],
        axis=0,
    )
    answers = after(answer_rows(asked, lookup, three), pieces)
    answered = exchange(answers.reshape(SHARDS, CAP, LANES))
    pieces = jnp.concatenate([pieces, swapped(pieces, X_BIT)], axis=0)
    tiles = collect(
        [pieces] + [swapped(pieces, flip * Y_BIT) for flip in range(1, Y_SIZE)]
    )
    base = arrange_rows(places, answered.reshape(SHARDS * CAP, LANES), fields)
    scores = cross_scores(
        base, cross_bias, out_weight.reshape(1, -1), tiles, swapped(tiles, CORE_BIT)
    )
    return (table_result[None], scores)


def solution(mesh):
    return jax.shard_map(
        on_device,
        mesh=mesh,
        in_specs=(
            P("role", "shard", None),
            P("shard", None),
            P("shard"),
            P("shard"),
            P("shard", None),
            P("role", None, None, None),
            P(),
            P("shard", None, None, None),
            P(),
            P(),
            P("role", "shard", None),
            P("role", "shard", None),
        ),
        out_specs=(P("role", "shard", None), P("role", "shard")),
        check_vma=False,
    )
```

```python
import jax
import jax.numpy as jnp
from jax import lax
from jax.experimental import pallas as pl
from jax.experimental.pallas import tpu as pltpu
from jax.sharding import PartitionSpec as P

ROW_SHRINK = 0.25
DENSE_SHRINK = 0.05
CAP = 32
LANES = 128
SHARDS = 128
ROLES = 2
Z_SIZE, Y_SIZE, X_SIZE, CORES = 8, 4, 2, 2
BLOCKS = Z_SIZE * Y_SIZE
Z_ORDER = (0, 1, 7, 3, 4, 2, 6, 5)
TILES = 2
SHARE = 12
PACKED = 16
VMEM_LIMIT = 24 * 1024 * 1024


def ftrl_weight(linear, squares, shrink):
    return -(linear - jnp.clip(linear, -shrink, shrink)) / (1.0 + jnp.sqrt(squares))


def ftrl_step(linear, squares, gradient, shrink):
    prior = ftrl_weight(linear, squares, shrink)
    fresh_squares = squares + gradient * gradient
    sigma_step = jnp.sqrt(fresh_squares) - jnp.sqrt(squares)
    return (linear + gradient - sigma_step * prior, fresh_squares, prior)


def iota(shape, dim):
    return lax.broadcasted_iota(jnp.int32, shape, dim)


def kernel_call(body, out_shape, flops=0, bytes_accessed=0, vmem=VMEM_LIMIT, **options):
    return pl.pallas_call(
        body,
        out_shape=out_shape,
        compiler_params=pltpu.CompilerParams(vmem_limit_bytes=vmem),
        cost_estimate=pl.CostEstimate(
            flops=flops, bytes_accessed=bytes_accessed, transcendentals=0
        ),
        **options,
    )


VMEM = pl.BlockSpec(memory_space=pltpu.VMEM)
SMEM = pl.BlockSpec(memory_space=pltpu.SMEM)
ANY = pl.BlockSpec(memory_space=pl.ANY)
HBM = pl.BlockSpec(memory_space=pltpu.HBM)


def position():
    shard = lax.axis_index("shard")
    return lax.axis_index("role"), shard, lax.rem(shard, CORES)


def half_copies(grad_ref, target_ref, flip, arrived):
    role, _, core = position()
    copies = []
    for tile in range(TILES):
        left = pl.multiple_of(((core ^ flip) * TILES + tile) * LANES, LANES)
        copies.append(
            pltpu.make_async_copy(
                grad_ref.at[:, role, :, pl.ds(left, LANES)], target_ref.at[tile], arrived.at[tile]
            )
        )
    return copies


def fetch_body(grad_ref, state_ref, square_ref, send_ref, keep_ref, own_state_ref, own_square_ref, arrived):
    _, shard, core = position()
    copies = half_copies(grad_ref, send_ref, 1, arrived.at[:TILES])
    copies += half_copies(grad_ref, keep_ref, 0, arrived.at[TILES : 2 * TILES])
    block = shard // (X_SIZE * CORES)
    for source, target in ((state_ref, own_state_ref), (square_ref, own_square_ref)):
        for column in range(CORES):
            left = pl.multiple_of((column * TILES + core) * LANES, LANES)
            copies.append(
                pltpu.make_async_copy(
                    source.at[block, :, :, pl.ds(left, LANES)],
                    target.at[column],
                    arrived.at[len(copies)],
                )
            )
    for copy in copies:
        copy.start()
    for copy in copies:
        copy.wait()


def fetch(grads, state, squares):
    halves = jax.ShapeDtypeStruct((TILES, BLOCKS, 2 * SHARE, LANES), jnp.float32)
    own = jax.ShapeDtypeStruct((CORES, ROLES, 2 * SHARE, LANES), jnp.float32)
    return kernel_call(
        fetch_body,
        (halves, halves, own, own),
        bytes_accessed=4_000_000,
        vmem=52 * 1024 * 1024,
        in_specs=[HBM] * 3,
        out_specs=(VMEM,) * 4,
        scratch_shapes=[pltpu.SemaphoreType.DMA((2 * TILES + 2 * CORES,))],
    )(grads, state, squares)


def route_body(owner_ref, slot_ref, place_ref, request_ref):
    fields, examples = owner_ref.shape
    shape = (SHARDS, examples)
    shard_ids = iota(shape, 0)
    member = jnp.zeros(shape, jnp.float32)
    wanted = jnp.zeros(shape, jnp.float32)
    for field in range(fields):
        named = owner_ref[field : field + 1, :] == shard_ids
        member = jnp.where(named, 1.0, member)
        wanted = jnp.where(named, slot_ref[field : field + 1, :].astype(jnp.float32), wanted)
    earlier = jnp.where(iota((examples, examples), 0) < iota((examples, examples), 1), 1.0, 0.0)
    ranks = jnp.dot(
        member.astype(jnp.bfloat16),
        earlier.astype(jnp.bfloat16),
        preferred_element_type=jnp.float32,
    )
    places = []
    for field in range(fields):
        owners = owner_ref[field : field + 1, :]
        rank = jnp.sum(jnp.where(owners == shard_ids, ranks, 0.0), axis=0, keepdims=True)
        places.append(owners * CAP + rank.astype(jnp.int32))
    place_ref[...] = jnp.concatenate(
        places + [jnp.zeros((8 - fields, examples), jnp.int32)], axis=0
    )
    ranks = jnp.where(member > 0.5, ranks, -1.0)
    requests = jnp.zeros((SHARDS, LANES), jnp.float32)
    lanes = iota((SHARDS, LANES), 1)
    for rank in range(CAP):
        column = jnp.sum(
            jnp.where(ranks == float(rank), wanted, 0.0), axis=1, keepdims=True
        )
        requests = jnp.where(lanes == rank, column, requests)
    asked = requests[:, :CAP].astype(jnp.int32)
    request_ref[...] = jnp.concatenate(
        [asked >> 4, asked & 15, jnp.zeros((SHARDS, LANES - 2 * CAP), jnp.int32)], axis=1
    ).astype(jnp.float32)


def route(owners, slots):
    examples = owners.shape[1]
    return kernel_call(
        route_body,
        (
            jax.ShapeDtypeStruct((8, examples), jnp.int32),
            jax.ShapeDtypeStruct((SHARDS, LANES), jnp.float32),
        ),
        in_specs=[VMEM, VMEM],
        out_specs=(VMEM, VMEM),
    )(owners, slots)


def pack_body(keep_ref, arrived_ref, request_ref, packed_ref):
    for block in range(BLOCKS):
        for tile in range(TILES):
            terms = keep_ref[tile, block] + arrived_ref[tile, block]
            for part in range(X_SIZE):
                shard = (block * X_SIZE + part) * CORES + tile
                packed_ref[shard] = jnp.concatenate(
                    [
                        terms[part * SHARE : (part + 1) * SHARE, :],
                        request_ref[shard : shard + 1, :],
                        jnp.zeros((PACKED - SHARE - 1, LANES), jnp.float32),
                    ],
                    axis=0,
                ).astype(jnp.bfloat16)


def pack(keep, arrived, requests):
    return kernel_call(
        pack_body,
        jax.ShapeDtypeStruct((SHARDS, PACKED, LANES), jnp.bfloat16),
        in_specs=[VMEM] * 3,
        out_specs=VMEM,
    )(keep, arrived, requests)


def unpack_body(packed_ref, lookup_ref, sum_ref, asked_ref):
    for core in range(CORES):
        total = jnp.zeros((PACKED, LANES), jnp.float32)
        for shard in range(core, SHARDS, CORES):
            packed = packed_ref[shard].astype(jnp.float32)
            total = total + packed
            asked_ref[shard : shard + 1, :] = packed[SHARE : SHARE + 1, :]
        sum_ref[core] = total


def unpack(packed, lookup):
    return kernel_call(
        unpack_body,
        (
            jax.ShapeDtypeStruct((CORES, PACKED, LANES), jnp.float32),
            jax.ShapeDtypeStruct((SHARDS, LANES), jnp.float32),
        ),
        in_specs=[VMEM, ANY],
        out_specs=(VMEM, VMEM),
    )(packed, lookup)


def used_slots(slot_ref, count):
    slots = slot_ref[...]
    return jnp.where(iota(slots.shape, 1) < count, slots, -1)


def rows_of_block(slots, first, rows):
    hit = slots == iota((rows, slots.shape[1]), 0) + first
    return jnp.where(hit, 1.0, 0.0).astype(jnp.bfloat16)


def train_body(count_ref, slot_ref, held_ref, square_ref, grad_ref, new_ref, weight_ref, fresh_ref, parts, total):
    step = pl.program_id(0)
    rows = held_ref.shape[0]

    @pl.when(step == 0)
    def _():
        grads = grad_ref[...]
        high = grads.astype(jnp.bfloat16)
        rest = grads - high.astype(jnp.float32)
        middle = rest.astype(jnp.bfloat16)
        low = (rest - middle.astype(jnp.float32)).astype(jnp.bfloat16)
        parts[...] = jnp.concatenate([high, middle, low], axis=1)
        total[...] = jnp.zeros_like(total)

    spread = rows_of_block(used_slots(slot_ref, count_ref[0]), step * rows, rows)
    sums = jnp.dot(spread, parts[...], preferred_element_type=jnp.float32)
    gradient = (sums[:, :LANES] + sums[:, LANES : 2 * LANES]) + sums[:, 2 * LANES :]
    linear, squares, _ = ftrl_step(held_ref[...], square_ref[...], gradient, ROW_SHRINK)
    new_ref[...] = linear
    weights = ftrl_weight(linear, squares, ROW_SHRINK).astype(jnp.bfloat16)
    weight_ref[...] = weights
    total[...] += lax.dot_general(
        spread, weights, (((0,), (0,)), ((), ())), preferred_element_type=jnp.float32
    )

    @pl.when(step == pl.num_programs(0) - 1)
    def _():
        fresh_ref[...] = total[...].astype(jnp.bfloat16)


def train_rows(count, slots, held, squares, grads):
    rows, width = held.shape
    updates = grads.shape[0]
    block = 512
    by_rows = pl.BlockSpec((block, width), lambda i: (i, 0))
    return kernel_call(
        train_body,
        (
            jax.ShapeDtypeStruct((rows, width), jnp.float32),
            jax.ShapeDtypeStruct((rows, width), jnp.bfloat16),
            jax.ShapeDtypeStruct((updates, width), jnp.bfloat16),
        ),
        grid=(rows // block,),
        in_specs=[
            SMEM,
            pl.BlockSpec((1, updates), lambda i: (0, 0)),
            by_rows,
            by_rows,
            pl.BlockSpec((updates, width), lambda i: (0, 0)),
        ],
        out_specs=(
            by_rows,
            by_rows,
            pl.BlockSpec((updates, width), lambda i: (0, 0)),
        ),
        scratch_shapes=[
            pltpu.VMEM((updates, 3 * width), jnp.bfloat16),
            pltpu.VMEM((updates, width), jnp.float32),
        ],
    )(count, slots, held, squares, grads)


def serve_body(count_ref, slot_ref, arrived_ref, held_ref, new_ref, weight_ref, table_ref, lookup_ref):
    step = pl.program_id(0)
    rows = held_ref.shape[0]
    role = lax.axis_index("role")

    @pl.when(role == 0)
    def _():
        table_ref[...] = new_ref[...]
        lookup_ref[...] = weight_ref[...]

    @pl.when(role != 0)
    def _():
        spread = rows_of_block(used_slots(slot_ref, count_ref[0]), step * rows, rows)
        arrived = arrived_ref[...]
        sums = jnp.dot(
            spread,
            jnp.concatenate([arrived, jnp.ones_like(arrived)], axis=1),
            preferred_element_type=jnp.float32,
        )
        table = jnp.where(sums[:, LANES:] > 0.5, sums[:, :LANES], held_ref[...])
        table_ref[...] = table
        lookup_ref[...] = table.astype(jnp.bfloat16)


def serve_rows(count, slots, arrived, held, new_linear, weights):
    rows, width = held.shape
    updates = slots.shape[1]
    block = 1024
    by_rows = pl.BlockSpec((block, width), lambda i: (i, 0))
    return kernel_call(
        serve_body,
        (
            jax.ShapeDtypeStruct((rows, width), jnp.float32),
            jax.ShapeDtypeStruct((rows, width), jnp.bfloat16),
        ),
        grid=(rows // block,),
        in_specs=[
            SMEM,
            pl.BlockSpec((1, updates), lambda i: (0, 0)),
            pl.BlockSpec((updates, width), lambda i: (0, 0)),
            by_rows,
            by_rows,
            by_rows,
        ],
        out_specs=(by_rows, by_rows),
    )(count, slots, arrived, held, new_linear, weights)


def looked_up(column, folded):
    rows, height = column.shape[0], folded.shape[0]
    spread = jnp.broadcast_to(column, (rows, LANES))
    within = jnp.where((spread & (LANES - 1)) == iota((rows, LANES), 1), 1.0, 0.0).astype(
        jnp.bfloat16
    )
    block = ((spread & (height - 1)) >> 7).astype(jnp.float32).astype(jnp.bfloat16)
    none = jnp.zeros_like(within)
    hot = jnp.concatenate(
        [jnp.where(block == jnp.bfloat16(at), within, none) for at in range(height // LANES)],
        axis=1,
    )
    both = jnp.dot(hot, folded, preferred_element_type=jnp.float32)
    return jnp.where(spread < height, both[:, :LANES], both[:, LANES:]).astype(jnp.bfloat16)


def fold(source_ref, target_ref):
    height = target_ref.shape[0]
    target_ref[:, :LANES] = source_ref[:height, :]
    target_ref[:, LANES:] = source_ref[height:, :]


def piece_body(sum_ref, other_ref, state_ref, trained_ref, square_ref, answer_ref, piece_ref):
    role, shard, _ = position()
    later = lax.rem(shard // CORES, X_SIZE) == 1

    def own(values):
        return jnp.where(later, values[SHARE : 2 * SHARE, :], values[:SHARE, :])

    parts = []
    for half in range(ROLES):
        for column in range(CORES):
            gradient = jnp.where(role == half, sum_ref[column], other_ref[column])[:SHARE, :]
            state = own(state_ref[column, half])
            trained = own(trained_ref[column, half])
            linear = jnp.where(role == 0, state, trained)
            dense_linear, dense_sumsq, prior = ftrl_step(
                linear, own(square_ref[column, half]), gradient, DENSE_SHRINK
            )
            fresh = ftrl_weight(dense_linear, dense_sumsq, DENSE_SHRINK)
            parts.append(jnp.where(role == 0, fresh, state + (fresh - prior)))
    piece_ref[...] = jnp.concatenate(parts, axis=0).astype(jnp.bfloat16)


def piece_weights(sums, other, state, trained, squares, answers):
    return kernel_call(
        piece_body,
        jax.ShapeDtypeStruct((ROLES * CORES * SHARE, LANES), jnp.bfloat16),
        in_specs=[VMEM] * 5 + [ANY],
        out_specs=VMEM,
    )(sums, other, state, trained, squares, answers)


def answer_body(asked_ref, table_ref, answer_ref, columns, folded):
    digits = asked_ref[...]
    wide = jnp.concatenate(
        [
            digits[:, :CAP] * 16.0 + digits[:, CAP : 2 * CAP],
            jnp.zeros((SHARDS, LANES - CAP), jnp.float32),
        ],
        axis=1,
    )
    columns[...] = jnp.transpose(wide)[:CAP, :].astype(jnp.int32)
    fold(table_ref, folded)
    group = 8
    for at in range(0, SHARDS, group):
        asked = jnp.concatenate(
            [columns[:, shard : shard + 1] for shard in range(at, at + group)], axis=0
        )
        answer_ref[at * CAP : (at + group) * CAP, :] = looked_up(asked, folded[...])


def answer_rows(asked, table):
    rows, width = table.shape
    return kernel_call(
        answer_body,
        jax.ShapeDtypeStruct((SHARDS * CAP, width), jnp.bfloat16),
        in_specs=[VMEM] * 2,
        out_specs=VMEM,
        scratch_shapes=[
            pltpu.VMEM((CAP, SHARDS), jnp.int32),
            pltpu.VMEM((rows // 2, 2 * width), jnp.bfloat16),
        ],
    )(asked, table)


def after_body(value_ref, other_ref, out_ref):
    del value_ref, other_ref, out_ref


def after(value, other):
    return kernel_call(
        after_body,
        jax.ShapeDtypeStruct(value.shape, value.dtype),
        in_specs=[ANY, ANY],
        out_specs=ANY,
        input_output_aliases={0: 0},
    )(value, other)


def collect_body(*refs):
    piece_refs, tile_ref = refs[:Y_SIZE], refs[Y_SIZE]
    _, shard, _ = position()
    x = lax.rem(shard // CORES, X_SIZE)
    y = lax.rem(shard // (X_SIZE * CORES), Y_SIZE)
    z = shard // (Y_SIZE * X_SIZE * CORES)
    piece = ROLES * CORES * SHARE
    for y_flip, ref in enumerate(piece_refs):
        for at, steps in enumerate(Z_ORDER):
            near = ref[at * piece : (at + 1) * piece, :].astype(jnp.float32)
            far = ref[(Z_SIZE + at) * piece : (Z_SIZE + at + 1) * piece, :].astype(jnp.float32)
            first, second = jnp.where(x == 0, near, far), jnp.where(x == 0, far, near)
            block = lax.rem(z + steps, Z_SIZE) * Y_SIZE + (y ^ y_flip)
            rows = pl.ds(pl.multiple_of(block * piece, piece), piece)
            for column in range(CORES):
                parts = []
                for half in range(ROLES):
                    start = (half * CORES + column) * SHARE
                    parts += [values[start : start + SHARE, :] for values in (first, second)]
                tile_ref[rows, column * LANES : (column + 1) * LANES] = jnp.concatenate(
                    parts, axis=0
                ).astype(jnp.bfloat16)


def collect(pieces):
    rows = BLOCKS * ROLES * X_SIZE * SHARE
    return kernel_call(
        collect_body,
        jax.ShapeDtypeStruct((rows, CORES * LANES), jnp.bfloat16),
        flops=9_000_000_000,
        in_specs=[VMEM] * Y_SIZE,
        out_specs=VMEM,
    )(*pieces)


def arrange_body(place_ref, answer_ref, base_ref, columns, folded):
    columns[...] = jnp.transpose(place_ref[...])
    fold(answer_ref, folded)
    examples = columns.shape[0]
    block = 256
    for field in range(base_ref.shape[1] // LANES):
        for at in range(0, examples, block):
            base_ref[at : at + block, field * LANES : (field + 1) * LANES] = looked_up(
                columns[at : at + block, field : field + 1], folded[...]
            )


def arrange_rows(places, answers, fields):
    examples = places.shape[1]
    rows, width = answers.shape
    return kernel_call(
        arrange_body,
        jax.ShapeDtypeStruct((examples, fields * width), jnp.bfloat16),
        flops=2 * examples * fields * rows * width,
        bytes_accessed=2_000_000,
        in_specs=[VMEM, VMEM],
        out_specs=VMEM,
        scratch_shapes=[
            pltpu.VMEM((examples, 8), jnp.int32),
            pltpu.VMEM((rows // 2, 2 * width), jnp.bfloat16),
        ],
    )(places, answers)


def cross_body(base_ref, bias_ref, out_ref, own_ref, other_ref, score_ref):
    _, _, core = position()
    width = base_ref.shape[1]
    base = base_ref[...].astype(jnp.float32)
    crossed = base
    for layer in range(bias_ref.shape[0]):
        rows = slice(layer * width, (layer + 1) * width)
        inputs = crossed.astype(jnp.bfloat16)
        own, other = (
            jnp.dot(inputs, tile_ref[rows, :], preferred_element_type=jnp.float32)
            for tile_ref in (own_ref, other_ref)
        )
        even, odd = jnp.where(core == 0, own, other), jnp.where(core == 0, other, own)
        mixed = jnp.concatenate(
            [
                tiles[:, column * LANES : (column + 1) * LANES]
                for column in range(CORES)
                for tiles in (even, odd)
            ],
            axis=1,
        )
        crossed = base * (mixed + bias_ref[layer : layer + 1, :]) + crossed
    scores = jnp.sum(crossed * out_ref[...], axis=1, keepdims=True)
    score_ref[...] = jnp.transpose(jnp.broadcast_to(scores, (scores.shape[0], LANES)))[:1, :]


def cross_scores(base, bias, out_weight, own, other):
    examples, width = base.shape
    return kernel_call(
        cross_body,
        jax.ShapeDtypeStruct((1, examples), jnp.float32),
        flops=2 * examples * width * width * bias.shape[0],
        bytes_accessed=3_000_000,
        in_specs=[VMEM] * 5,
        out_specs=VMEM,
    )(base, bias, out_weight, own, other)


BOTH = ("role", "shard")
CORE_BIT, X_BIT, Y_BIT, ROLE_BIT = 1, 2, 4, 128


def swapped(value, bits):
    count = ROLES * SHARDS
    return lax.ppermute(value, BOTH, [(source, source ^ bits) for source in range(count)])


def from_ahead(value, steps):
    span = SHARDS // Z_SIZE
    return lax.ppermute(
        value,
        "shard",
        [((source + steps * span) % SHARDS, source) for source in range(SHARDS)],
    )


def exchange(value):
    return lax.all_to_all(value, "shard", split_axis=0, concat_axis=0, tiled=True)


def on_device(
    tables,
    row_squares,
    update_slots,
    update_counts,
    row_grads,
    dense_state,
    dense_squares,
    dense_grads,
    cross_bias,
    out_weight,
    cand_owner,
    cand_slot,
):
    fields = cand_owner.shape[2]
    blocks = (BLOCKS, ROLES, 2 * SHARE, dense_squares.shape[2])
    grads = dense_grads.reshape(blocks)
    send, keep, own_state, own_squares = fetch(
        grads, dense_state.reshape(blocks), dense_squares.reshape(blocks)
    )
    paired = swapped(send, CORE_BIT)
    trained = lax.ppermute(own_state, "role", [(0, 1)])
    places, requests = route(cand_owner[0].T, cand_slot[0].T)
    packed = exchange(pack(keep, paired, requests))
    slots = update_slots.reshape(1, -1)
    new_linear, weights, fresh = train_rows(
        update_counts, slots, tables[0], row_squares, row_grads
    )
    arrived = lax.ppermute(fresh, "role", [(0, 1)])
    table_result, lookup = serve_rows(
        update_counts, slots, arrived, tables[0], new_linear, weights
    )
    sums, asked = unpack(packed, lookup)
    answers = answer_rows(asked, lookup)
    piece = piece_weights(
        sums, swapped(sums, ROLE_BIT), own_state, trained, own_squares, answers
    )
    ahead, behind = from_ahead(piece, 1), from_ahead(piece, -1)
    three = jnp.concatenate([piece, ahead, behind], axis=0)
    pieces = jnp.concatenate(
        [
            three,
            from_ahead(three, 3),
            from_ahead(jnp.concatenate([piece, behind], axis=0), -2),
        ],
        axis=0,
    )
    answers = after(answers, three)
    answered = exchange(answers.reshape(SHARDS, CAP, LANES))
    pieces = jnp.concatenate([pieces, swapped(pieces, X_BIT)], axis=0)
    tiles = collect(
        [pieces] + [swapped(pieces, flip * Y_BIT) for flip in range(1, Y_SIZE)]
    )
    base = arrange_rows(places, answered.reshape(SHARDS * CAP, LANES), fields)
    scores = cross_scores(
        base, cross_bias, out_weight.reshape(1, -1), tiles, swapped(tiles, CORE_BIT)
    )
    return (table_result[None], scores)


def solution(mesh):
    return jax.shard_map(
        on_device,
        mesh=mesh,
        in_specs=(
            P("role", "shard", None),
            P("shard", None),
            P("shard"),
            P("shard"),
            P("shard", None),
            P("role", None, None, None),
            P(),
            P("shard", None, None, None),
            P(),
            P(),
            P("role", "shard", None),
            P("role", "shard", None),
        ),
        out_specs=(P("role", "shard", None), P("role", "shard")),
        check_vma=False,
    )
```

```python
import jax
import jax.numpy as jnp
from jax import lax
from jax.experimental import pallas as pl
from jax.experimental.pallas import tpu as pltpu
from jax.sharding import PartitionSpec as P

ROW_SHRINK = 0.25
DENSE_SHRINK = 0.05
CAP = 32
LANES = 128
SHARDS = 128
ROLES = 2
Z_SIZE, Y_SIZE, X_SIZE, CORES = 8, 4, 2, 2
BLOCKS = Z_SIZE * Y_SIZE
Z_ORDER = (0, 1, 7, 5, 6, 4, 2, 3)
TILES = 2
SHARE = 12
PACKED = 16
VMEM_LIMIT = 24 * 1024 * 1024
FETCH_LIMIT = 52 * 1024 * 1024


def ftrl_weight(linear, squares, shrink):
    return -(linear - jnp.clip(linear, -shrink, shrink)) / (1.0 + jnp.sqrt(squares))


def ftrl_step(linear, squares, gradient, shrink):
    prior = ftrl_weight(linear, squares, shrink)
    fresh_squares = squares + gradient * gradient
    sigma_step = jnp.sqrt(fresh_squares) - jnp.sqrt(squares)
    return (linear + gradient - sigma_step * prior, fresh_squares, prior)


def iota(shape, dim):
    return lax.broadcasted_iota(jnp.int32, shape, dim)


def kernel_call(body, out_shape, flops=0, bytes_accessed=0, vmem=VMEM_LIMIT, **options):
    return pl.pallas_call(
        body,
        out_shape=out_shape,
        compiler_params=pltpu.CompilerParams(vmem_limit_bytes=vmem),
        cost_estimate=pl.CostEstimate(
            flops=flops, bytes_accessed=bytes_accessed, transcendentals=0
        ),
        **options,
    )


VMEM = pl.BlockSpec(memory_space=pltpu.VMEM)
SMEM = pl.BlockSpec(memory_space=pltpu.SMEM)
ANY = pl.BlockSpec(memory_space=pl.ANY)
HBM = pl.BlockSpec(memory_space=pltpu.HBM)


def position():
    shard = lax.axis_index("shard")
    return lax.axis_index("role"), shard, lax.rem(shard, CORES)


def half_copies(grad_ref, target_ref, flip, arrived):
    role, _, core = position()
    copies = []
    for tile in range(TILES):
        left = pl.multiple_of(((core ^ flip) * TILES + tile) * LANES, LANES)
        copies.append(
            pltpu.make_async_copy(
                grad_ref.at[:, role, :, pl.ds(left, LANES)], target_ref.at[tile], arrived.at[tile]
            )
        )
    return copies


def fetch_body(grad_ref, send_ref, arrived):
    copies = half_copies(grad_ref, send_ref, 1, arrived)
    for copy in copies:
        copy.start()
    for copy in copies:
        copy.wait()


def fetch(grads):
    return kernel_call(
        fetch_body,
        jax.ShapeDtypeStruct((TILES, BLOCKS, 2 * SHARE, LANES), jnp.float32),
        vmem=FETCH_LIMIT,
        in_specs=[HBM],
        out_specs=VMEM,
        scratch_shapes=[pltpu.SemaphoreType.DMA((TILES,))],
    )(grads)


def route_body(owner_ref, slot_ref, grad_ref, state_ref, square_ref, place_ref, request_ref, keep_ref, own_state_ref, own_square_ref, arrived):
    _, shard, core = position()
    copies = half_copies(grad_ref, keep_ref, 0, arrived)
    for source, target in ((state_ref, own_state_ref), (square_ref, own_square_ref)):
        for column in range(CORES):
            left = pl.multiple_of((column * TILES + core) * LANES, LANES)
            copies.append(
                pltpu.make_async_copy(
                    source.at[shard // (X_SIZE * CORES), :, :, pl.ds(left, LANES)],
                    target.at[column],
                    arrived.at[len(copies)],
                )
            )
    for copy in copies:
        copy.start()
    fields, examples = owner_ref.shape
    shape = (SHARDS, examples)
    shard_ids = iota(shape, 0)
    member = jnp.zeros(shape, jnp.float32)
    wanted = jnp.zeros(shape, jnp.float32)
    for field in range(fields):
        named = owner_ref[field : field + 1, :] == shard_ids
        member = jnp.where(named, 1.0, member)
        wanted = jnp.where(named, slot_ref[field : field + 1, :].astype(jnp.float32), wanted)
    earlier = jnp.where(iota((examples, examples), 0) < iota((examples, examples), 1), 1.0, 0.0)
    ranks = jnp.dot(
        member.astype(jnp.bfloat16),
        earlier.astype(jnp.bfloat16),
        preferred_element_type=jnp.float32,
    )
    places = []
    for field in range(fields):
        owners = owner_ref[field : field + 1, :]
        rank = jnp.sum(jnp.where(owners == shard_ids, ranks, 0.0), axis=0, keepdims=True)
        places.append(owners * CAP + rank.astype(jnp.int32))
    place_ref[...] = jnp.concatenate(
        places + [jnp.zeros((8 - fields, examples), jnp.int32)], axis=0
    )
    ranks = jnp.where(member > 0.5, ranks, -1.0)
    requests = jnp.zeros((SHARDS, LANES), jnp.float32)
    lanes = iota((SHARDS, LANES), 1)
    for rank in range(CAP):
        column = jnp.sum(
            jnp.where(ranks == float(rank), wanted, 0.0), axis=1, keepdims=True
        )
        requests = jnp.where(lanes == rank, column, requests)
    asked = requests[:, :CAP].astype(jnp.int32)
    request_ref[...] = jnp.concatenate(
        [asked >> 4, asked & 15, jnp.zeros((SHARDS, LANES - 2 * CAP), jnp.int32)], axis=1
    ).astype(jnp.float32)
    for copy in copies:
        copy.wait()


def route(owners, slots, grads, state, squares):
    examples = owners.shape[1]
    own = jax.ShapeDtypeStruct((CORES, ROLES, 2 * SHARE, LANES), jnp.float32)
    return kernel_call(
        route_body,
        (
            jax.ShapeDtypeStruct((8, examples), jnp.int32),
            jax.ShapeDtypeStruct((SHARDS, LANES), jnp.float32),
            jax.ShapeDtypeStruct((TILES, BLOCKS, 2 * SHARE, LANES), jnp.float32),
            own,
            own,
        ),
        vmem=FETCH_LIMIT,
        in_specs=[VMEM] * 2 + [HBM] * 3,
        out_specs=(VMEM,) * 5,
        scratch_shapes=[pltpu.SemaphoreType.DMA((TILES + 2 * CORES,))],
    )(owners, slots, grads, state, squares)


def pack_body(keep_ref, arrived_ref, request_ref, packed_ref):
    for block in range(BLOCKS):
        for tile in range(TILES):
            terms = keep_ref[tile, block] + arrived_ref[tile, block]
            for part in range(X_SIZE):
                shard = (block * X_SIZE + part) * CORES + tile
                packed_ref[shard] = jnp.concatenate(
                    [
                        terms[part * SHARE : (part + 1) * SHARE, :],
                        request_ref[shard : shard + 1, :],
                        jnp.zeros((PACKED - SHARE - 1, LANES), jnp.float32),
                    ],
                    axis=0,
                ).astype(jnp.bfloat16)


def pack(keep, arrived, requests):
    return kernel_call(
        pack_body,
        jax.ShapeDtypeStruct((SHARDS, PACKED, LANES), jnp.bfloat16),
        in_specs=[VMEM] * 3,
        out_specs=VMEM,
    )(keep, arrived, requests)


def unpack_body(packed_ref, lookup_ref, sum_ref, asked_ref):
    for core in range(CORES):
        total = jnp.zeros((PACKED, LANES), jnp.float32)
        for shard in range(core, SHARDS, CORES):
            packed = packed_ref[shard].astype(jnp.float32)
            total = total + packed
            asked_ref[shard : shard + 1, :] = packed[SHARE : SHARE + 1, :]
        sum_ref[core] = total


def unpack(packed, lookup):
    return kernel_call(
        unpack_body,
        (
            jax.ShapeDtypeStruct((CORES, PACKED, LANES), jnp.float32),
            jax.ShapeDtypeStruct((SHARDS, LANES), jnp.float32),
        ),
        in_specs=[VMEM, ANY],
        out_specs=(VMEM, VMEM),
    )(packed, lookup)


def used_slots(slot_ref, count):
    slots = slot_ref[...]
    return jnp.where(iota(slots.shape, 1) < count, slots, -1)


def rows_of_block(slots, first, rows):
    hit = slots == iota((rows, slots.shape[1]), 0) + first
    return jnp.where(hit, 1.0, 0.0).astype(jnp.bfloat16)


def train_body(count_ref, slot_ref, held_ref, square_ref, grad_ref, new_ref, weight_ref, fresh_ref, parts, total):
    step = pl.program_id(0)
    rows = held_ref.shape[0]

    @pl.when(step == 0)
    def _():
        grads = grad_ref[...]
        high = grads.astype(jnp.bfloat16)
        rest = grads - high.astype(jnp.float32)
        middle = rest.astype(jnp.bfloat16)
        low = (rest - middle.astype(jnp.float32)).astype(jnp.bfloat16)
        parts[...] = jnp.concatenate([high, middle, low], axis=1)
        total[...] = jnp.zeros_like(total)

    spread = rows_of_block(used_slots(slot_ref, count_ref[0]), step * rows, rows)
    sums = jnp.dot(spread, parts[...], preferred_element_type=jnp.float32)
    gradient = (sums[:, :LANES] + sums[:, LANES : 2 * LANES]) + sums[:, 2 * LANES :]
    linear, squares, _ = ftrl_step(held_ref[...], square_ref[...], gradient, ROW_SHRINK)
    new_ref[...] = linear
    weights = ftrl_weight(linear, squares, ROW_SHRINK).astype(jnp.bfloat16)
    weight_ref[...] = weights
    total[...] += lax.dot_general(
        spread, weights, (((0,), (0,)), ((), ())), preferred_element_type=jnp.float32
    )

    @pl.when(step == pl.num_programs(0) - 1)
    def _():
        fresh_ref[...] = total[...].astype(jnp.bfloat16)


def train_rows(count, slots, held, squares, grads):
    rows, width = held.shape
    updates = grads.shape[0]
    block = 512
    by_rows = pl.BlockSpec((block, width), lambda i: (i, 0))
    return kernel_call(
        train_body,
        (
            jax.ShapeDtypeStruct((rows, width), jnp.float32),
            jax.ShapeDtypeStruct((rows, width), jnp.bfloat16),
            jax.ShapeDtypeStruct((updates, width), jnp.bfloat16),
        ),
        grid=(rows // block,),
        in_specs=[
            SMEM,
            pl.BlockSpec((1, updates), lambda i: (0, 0)),
            by_rows,
            by_rows,
            pl.BlockSpec((updates, width), lambda i: (0, 0)),
        ],
        out_specs=(
            by_rows,
            by_rows,
            pl.BlockSpec((updates, width), lambda i: (0, 0)),
        ),
        scratch_shapes=[
            pltpu.VMEM((updates, 3 * width), jnp.bfloat16),
            pltpu.VMEM((updates, width), jnp.float32),
        ],
    )(count, slots, held, squares, grads)


def serve_body(count_ref, slot_ref, arrived_ref, held_ref, new_ref, weight_ref, table_ref, lookup_ref):
    step = pl.program_id(0)
    rows = held_ref.shape[0]
    role = lax.axis_index("role")

    @pl.when(role == 0)
    def _():
        table_ref[...] = new_ref[...]
        lookup_ref[...] = weight_ref[...]

    @pl.when(role != 0)
    def _():
        spread = rows_of_block(used_slots(slot_ref, count_ref[0]), step * rows, rows)
        arrived = arrived_ref[...]
        sums = jnp.dot(
            spread,
            jnp.concatenate([arrived, jnp.ones_like(arrived)], axis=1),
            preferred_element_type=jnp.float32,
        )
        table = jnp.where(sums[:, LANES:] > 0.5, sums[:, :LANES], held_ref[...])
        table_ref[...] = table
        lookup_ref[...] = table.astype(jnp.bfloat16)


def serve_rows(count, slots, arrived, held, new_linear, weights):
    rows, width = held.shape
    updates = slots.shape[1]
    block = 1024
    by_rows = pl.BlockSpec((block, width), lambda i: (i, 0))
    return kernel_call(
        serve_body,
        (
            jax.ShapeDtypeStruct((rows, width), jnp.float32),
            jax.ShapeDtypeStruct((rows, width), jnp.bfloat16),
        ),
        grid=(rows // block,),
        in_specs=[
            SMEM,
            pl.BlockSpec((1, updates), lambda i: (0, 0)),
            pl.BlockSpec((updates, width), lambda i: (0, 0)),
            by_rows,
            by_rows,
            by_rows,
        ],
        out_specs=(by_rows, by_rows),
    )(count, slots, arrived, held, new_linear, weights)


def looked_up(column, folded):
    rows, height = column.shape[0], folded.shape[0]
    spread = jnp.broadcast_to(column, (rows, LANES))
    within = jnp.where((spread & (LANES - 1)) == iota((rows, LANES), 1), 1.0, 0.0).astype(
        jnp.bfloat16
    )
    block = ((spread & (height - 1)) >> 7).astype(jnp.float32).astype(jnp.bfloat16)
    none = jnp.zeros_like(within)
    hot = jnp.concatenate(
        [jnp.where(block == jnp.bfloat16(at), within, none) for at in range(height // LANES)],
        axis=1,
    )
    both = jnp.dot(hot, folded, preferred_element_type=jnp.float32)
    return jnp.where(spread < height, both[:, :LANES], both[:, LANES:]).astype(jnp.bfloat16)


def fold(source_ref, target_ref):
    height = target_ref.shape[0]
    target_ref[:, :LANES] = source_ref[:height, :]
    target_ref[:, LANES:] = source_ref[height:, :]


def piece_body(sum_ref, other_ref, state_ref, trained_ref, square_ref, answer_ref, piece_ref):
    role, shard, _ = position()
    later = lax.rem(shard // CORES, X_SIZE) == 1

    def own(values):
        return jnp.where(later, values[SHARE : 2 * SHARE, :], values[:SHARE, :])

    parts = []
    for half in range(ROLES):
        for column in range(CORES):
            gradient = jnp.where(role == half, sum_ref[column], other_ref[column])[:SHARE, :]
            state = own(state_ref[column, half])
            trained = own(trained_ref[column, half])
            linear = jnp.where(role == 0, state, trained)
            dense_linear, dense_sumsq, prior = ftrl_step(
                linear, own(square_ref[column, half]), gradient, DENSE_SHRINK
            )
            fresh = ftrl_weight(dense_linear, dense_sumsq, DENSE_SHRINK)
            parts.append(jnp.where(role == 0, fresh, state + (fresh - prior)))
    piece_ref[...] = jnp.concatenate(parts, axis=0).astype(jnp.bfloat16)


def piece_weights(sums, other, state, trained, squares, answers):
    return kernel_call(
        piece_body,
        jax.ShapeDtypeStruct((ROLES * CORES * SHARE, LANES), jnp.bfloat16),
        in_specs=[VMEM] * 5 + [ANY],
        out_specs=VMEM,
    )(sums, other, state, trained, squares, answers)


def answer_body(asked_ref, table_ref, answer_ref, columns, folded):
    digits = asked_ref[...]
    wide = jnp.concatenate(
        [
            digits[:, :CAP] * 16.0 + digits[:, CAP : 2 * CAP],
            jnp.zeros((SHARDS, LANES - CAP), jnp.float32),
        ],
        axis=1,
    )
    columns[...] = jnp.transpose(wide)[:CAP, :].astype(jnp.int32)
    fold(table_ref, folded)
    group = 8
    for at in range(0, SHARDS, group):
        asked = jnp.concatenate(
            [columns[:, shard : shard + 1] for shard in range(at, at + group)], axis=0
        )
        answer_ref[at * CAP : (at + group) * CAP, :] = looked_up(asked, folded[...])


def answer_rows(asked, table):
    rows, width = table.shape
    return kernel_call(
        answer_body,
        jax.ShapeDtypeStruct((SHARDS * CAP, width), jnp.bfloat16),
        in_specs=[VMEM] * 2,
        out_specs=VMEM,
        scratch_shapes=[
            pltpu.VMEM((CAP, SHARDS), jnp.int32),
            pltpu.VMEM((rows // 2, 2 * width), jnp.bfloat16),
        ],
    )(asked, table)


def after_body(value_ref, other_ref, out_ref):
    del value_ref, other_ref, out_ref


def after(value, other):
    return kernel_call(
        after_body,
        jax.ShapeDtypeStruct(value.shape, value.dtype),
        in_specs=[ANY, ANY],
        out_specs=ANY,
        input_output_aliases={0: 0},
    )(value, other)


def collect_body(*refs):
    piece_refs, tile_ref = refs[:Y_SIZE], refs[Y_SIZE]
    _, shard, _ = position()
    x = lax.rem(shard // CORES, X_SIZE)
    y = lax.rem(shard // (X_SIZE * CORES), Y_SIZE)
    z = shard // (Y_SIZE * X_SIZE * CORES)
    piece = ROLES * CORES * SHARE
    for y_flip, ref in enumerate(piece_refs):
        for at, steps in enumerate(Z_ORDER):
            near = ref[at * piece : (at + 1) * piece, :].astype(jnp.float32)
            far = ref[(Z_SIZE + at) * piece : (Z_SIZE + at + 1) * piece, :].astype(jnp.float32)
            first, second = jnp.where(x == 0, near, far), jnp.where(x == 0, far, near)
            block = lax.rem(z + steps, Z_SIZE) * Y_SIZE + (y ^ y_flip)
            rows = pl.ds(pl.multiple_of(block * piece, piece), piece)
            for column in range(CORES):
                parts = []
                for half in range(ROLES):
                    start = (half * CORES + column) * SHARE
                    parts += [values[start : start + SHARE, :] for values in (first, second)]
                tile_ref[rows, column * LANES : (column + 1) * LANES] = jnp.concatenate(
                    parts, axis=0
                ).astype(jnp.bfloat16)


def collect(pieces):
    rows = BLOCKS * ROLES * X_SIZE * SHARE
    return kernel_call(
        collect_body,
        jax.ShapeDtypeStruct((rows, CORES * LANES), jnp.bfloat16),
        flops=9_000_000_000,
        in_specs=[VMEM] * Y_SIZE,
        out_specs=VMEM,
    )(*pieces)


def arrange_body(place_ref, answer_ref, base_ref, columns, folded):
    columns[...] = jnp.transpose(place_ref[...])
    fold(answer_ref, folded)
    examples = columns.shape[0]
    block = 256
    for field in range(base_ref.shape[1] // LANES):
        for at in range(0, examples, block):
            base_ref[at : at + block, field * LANES : (field + 1) * LANES] = looked_up(
                columns[at : at + block, field : field + 1], folded[...]
            )


def arrange_rows(places, answers, fields):
    examples = places.shape[1]
    rows, width = answers.shape
    return kernel_call(
        arrange_body,
        jax.ShapeDtypeStruct((examples, fields * width), jnp.bfloat16),
        flops=2 * examples * fields * rows * width,
        bytes_accessed=2_000_000,
        in_specs=[VMEM, VMEM],
        out_specs=VMEM,
        scratch_shapes=[
            pltpu.VMEM((examples, 8), jnp.int32),
            pltpu.VMEM((rows // 2, 2 * width), jnp.bfloat16),
        ],
    )(places, answers)


def cross_body(base_ref, bias_ref, out_ref, own_ref, other_ref, score_ref):
    _, _, core = position()
    width = base_ref.shape[1]
    base = base_ref[...].astype(jnp.float32)
    crossed = base
    for layer in range(bias_ref.shape[0]):
        rows = slice(layer * width, (layer + 1) * width)
        inputs = crossed.astype(jnp.bfloat16)
        own, other = (
            jnp.dot(inputs, tile_ref[rows, :], preferred_element_type=jnp.float32)
            for tile_ref in (own_ref, other_ref)
        )
        even, odd = jnp.where(core == 0, own, other), jnp.where(core == 0, other, own)
        mixed = jnp.concatenate(
            [
                tiles[:, column * LANES : (column + 1) * LANES]
                for column in range(CORES)
                for tiles in (even, odd)
            ],
            axis=1,
        )
        crossed = base * (mixed + bias_ref[layer : layer + 1, :]) + crossed
    scores = jnp.sum(crossed * out_ref[...], axis=1, keepdims=True)
    score_ref[...] = jnp.transpose(jnp.broadcast_to(scores, (scores.shape[0], LANES)))[:1, :]


def cross_scores(base, bias, out_weight, own, other):
    examples, width = base.shape
    return kernel_call(
        cross_body,
        jax.ShapeDtypeStruct((1, examples), jnp.float32),
        flops=2 * examples * width * width * bias.shape[0],
        bytes_accessed=3_000_000,
        in_specs=[VMEM] * 5,
        out_specs=VMEM,
    )(base, bias, out_weight, own, other)


BOTH = ("role", "shard")
CORE_BIT, X_BIT, Y_BIT, ROLE_BIT = 1, 2, 4, 128


def swapped(value, bits):
    count = ROLES * SHARDS
    return lax.ppermute(value, BOTH, [(source, source ^ bits) for source in range(count)])


def from_ahead(value, steps):
    span = SHARDS // Z_SIZE
    return lax.ppermute(
        value,
        "shard",
        [((source + steps * span) % SHARDS, source) for source in range(SHARDS)],
    )


def exchange(value):
    return lax.all_to_all(value, "shard", split_axis=0, concat_axis=0, tiled=True)


def on_device(
    tables,
    row_squares,
    update_slots,
    update_counts,
    row_grads,
    dense_state,
    dense_squares,
    dense_grads,
    cross_bias,
    out_weight,
    cand_owner,
    cand_slot,
):
    fields = cand_owner.shape[2]
    blocks = (BLOCKS, ROLES, 2 * SHARE, dense_squares.shape[2])
    grads = dense_grads.reshape(blocks)
    paired = swapped(fetch(grads), CORE_BIT)
    places, requests, keep, own_state, own_squares = route(
        cand_owner[0].T,
        cand_slot[0].T,
        grads,
        dense_state.reshape(blocks),
        dense_squares.reshape(blocks),
    )
    trained = lax.ppermute(own_state, "role", [(0, 1)])
    packed = exchange(pack(keep, paired, requests))
    slots = update_slots.reshape(1, -1)
    new_linear, weights, fresh = train_rows(
        update_counts, slots, tables[0], row_squares, row_grads
    )
    arrived = lax.ppermute(fresh, "role", [(0, 1)])
    table_result, lookup = serve_rows(
        update_counts, slots, arrived, tables[0], new_linear, weights
    )
    sums, asked = unpack(packed, lookup)
    answers = answer_rows(asked, lookup)
    piece = piece_weights(
        sums, swapped(sums, ROLE_BIT), own_state, trained, own_squares, answers
    )
    ahead, behind = from_ahead(piece, 1), from_ahead(piece, -1)
    three = jnp.concatenate([piece, ahead, behind], axis=0)
    pieces = jnp.concatenate(
        [
            three,
            from_ahead(three, -3),
            from_ahead(jnp.concatenate([piece, ahead], axis=0), 2),
        ],
        axis=0,
    )
    answers = after(answers, three)
    answered = exchange(answers.reshape(SHARDS, CAP, LANES))
    pieces = jnp.concatenate([pieces, swapped(pieces, X_BIT)], axis=0)
    tiles = collect(
        [pieces] + [swapped(pieces, flip * Y_BIT) for flip in range(1, Y_SIZE)]
    )
    base = arrange_rows(places, answered.reshape(SHARDS * CAP, LANES), fields)
    scores = cross_scores(
        base, cross_bias, out_weight.reshape(1, -1), tiles, swapped(tiles, CORE_BIT)
    )
    return (table_result[None], scores)


def solution(mesh):
    return jax.shard_map(
        on_device,
        mesh=mesh,
        in_specs=(
            P("role", "shard", None),
            P("shard", None),
            P("shard"),
            P("shard"),
            P("shard", None),
            P("role", None, None, None),
            P(),
            P("shard", None, None, None),
            P(),
            P(),
            P("role", "shard", None),
            P("role", "shard", None),
        ),
        out_specs=(P("role", "shard", None), P("role", "shard")),
        check_vma=False,
    )
```

```python
import jax
import jax.numpy as jnp
from jax import lax
from jax.experimental import pallas as pl
from jax.experimental.pallas import tpu as pltpu
from jax.sharding import PartitionSpec as P

ROW_SHRINK = 0.25
DENSE_SHRINK = 0.05
CAP = 32
FIRST = 96
LANES = 128
SHARDS = 128
ROLES = 2
Z_SIZE, Y_SIZE, X_SIZE, CORES = 8, 4, 2, 2
BLOCKS = Z_SIZE * Y_SIZE
Z_ORDER = (0, 1, 7, 5, 6, 4, 2, 3)
TILES = 2
SHARE = 12
PACKED = 16
VMEM_LIMIT = 24 * 1024 * 1024
FETCH_LIMIT = 52 * 1024 * 1024


def ftrl_weight(linear, squares, shrink):
    return -(linear - jnp.clip(linear, -shrink, shrink)) / (1.0 + jnp.sqrt(squares))


def ftrl_step(linear, squares, gradient, shrink):
    prior = ftrl_weight(linear, squares, shrink)
    fresh_squares = squares + gradient * gradient
    sigma_step = jnp.sqrt(fresh_squares) - jnp.sqrt(squares)
    return (linear + gradient - sigma_step * prior, fresh_squares, prior)


def iota(shape, dim):
    return lax.broadcasted_iota(jnp.int32, shape, dim)


def kernel_call(body, out_shape, flops=0, bytes_accessed=0, vmem=VMEM_LIMIT, **options):
    return pl.pallas_call(
        body,
        out_shape=out_shape,
        compiler_params=pltpu.CompilerParams(vmem_limit_bytes=vmem),
        cost_estimate=pl.CostEstimate(
            flops=flops, bytes_accessed=bytes_accessed, transcendentals=0
        ),
        **options,
    )


VMEM = pl.BlockSpec(memory_space=pltpu.VMEM)
SMEM = pl.BlockSpec(memory_space=pltpu.SMEM)
ANY = pl.BlockSpec(memory_space=pl.ANY)
HBM = pl.BlockSpec(memory_space=pltpu.HBM)


def position():
    shard = lax.axis_index("shard")
    return lax.axis_index("role"), shard, lax.rem(shard, CORES)


def half_copies(grad_ref, target_ref, flip, arrived):
    role, _, core = position()
    copies = []
    for tile in range(TILES):
        left = pl.multiple_of(((core ^ flip) * TILES + tile) * LANES, LANES)
        copies.append(
            pltpu.make_async_copy(
                grad_ref.at[:, role, :, pl.ds(left, LANES)], target_ref.at[tile], arrived.at[tile]
            )
        )
    return copies


def fetch_body(grad_ref, send_ref, arrived):
    copies = half_copies(grad_ref, send_ref, 1, arrived)
    for copy in copies:
        copy.start()
    for copy in copies:
        copy.wait()


def fetch(grads):
    return kernel_call(
        fetch_body,
        jax.ShapeDtypeStruct((TILES, BLOCKS, 2 * SHARE, LANES), jnp.float32),
        vmem=FETCH_LIMIT,
        in_specs=[HBM],
        out_specs=VMEM,
        scratch_shapes=[pltpu.SemaphoreType.DMA((TILES,))],
    )(grads)


def route_body(owner_ref, slot_ref, grad_ref, state_ref, square_ref, place_ref, request_ref, keep_ref, own_state_ref, own_square_ref, arrived):
    _, shard, core = position()
    copies = half_copies(grad_ref, keep_ref, 0, arrived)
    for source, target in ((state_ref, own_state_ref), (square_ref, own_square_ref)):
        for column in range(CORES):
            left = pl.multiple_of((column * TILES + core) * LANES, LANES)
            copies.append(
                pltpu.make_async_copy(
                    source.at[shard // (X_SIZE * CORES), :, :, pl.ds(left, LANES)],
                    target.at[column],
                    arrived.at[len(copies)],
                )
            )
    for copy in copies:
        copy.start()
    fields, examples = owner_ref.shape
    shape = (SHARDS, examples)
    shard_ids = iota(shape, 0)
    member = jnp.zeros(shape, jnp.float32)
    wanted = jnp.zeros(shape, jnp.float32)
    for field in range(fields):
        named = owner_ref[field : field + 1, :] == shard_ids
        member = jnp.where(named, 1.0, member)
        wanted = jnp.where(named, slot_ref[field : field + 1, :].astype(jnp.float32), wanted)
    earlier = jnp.where(iota((examples, examples), 0) < iota((examples, examples), 1), 1.0, 0.0)
    ranks = jnp.dot(
        member.astype(jnp.bfloat16),
        earlier.astype(jnp.bfloat16),
        preferred_element_type=jnp.float32,
    )
    places = []
    for field in range(fields):
        owners = owner_ref[field : field + 1, :]
        rank = jnp.sum(jnp.where(owners == shard_ids, ranks, 0.0), axis=0, keepdims=True)
        places.append(owners * CAP + rank.astype(jnp.int32))
    place_ref[...] = jnp.concatenate(
        places + [jnp.zeros((8 - fields, examples), jnp.int32)], axis=0
    )
    ranks = jnp.where(member > 0.5, ranks, -1.0)
    requests = jnp.zeros((SHARDS, LANES), jnp.float32)
    lanes = iota((SHARDS, LANES), 1)
    for rank in range(CAP):
        column = jnp.sum(
            jnp.where(ranks == float(rank), wanted, 0.0), axis=1, keepdims=True
        )
        requests = jnp.where(lanes == rank, column, requests)
    asked = requests[:, :CAP].astype(jnp.int32)
    request_ref[...] = jnp.concatenate(
        [asked >> 4, asked & 15, jnp.zeros((SHARDS, LANES - 2 * CAP), jnp.int32)], axis=1
    ).astype(jnp.float32)
    for copy in copies:
        copy.wait()


def route(owners, slots, grads, state, squares):
    examples = owners.shape[1]
    own = jax.ShapeDtypeStruct((CORES, ROLES, 2 * SHARE, LANES), jnp.float32)
    return kernel_call(
        route_body,
        (
            jax.ShapeDtypeStruct((8, examples), jnp.int32),
            jax.ShapeDtypeStruct((SHARDS, LANES), jnp.float32),
            jax.ShapeDtypeStruct((TILES, BLOCKS, 2 * SHARE, LANES), jnp.float32),
            own,
            own,
        ),
        vmem=FETCH_LIMIT,
        in_specs=[VMEM] * 2 + [HBM] * 3,
        out_specs=(VMEM,) * 5,
        scratch_shapes=[pltpu.SemaphoreType.DMA((TILES + 2 * CORES,))],
    )(owners, slots, grads, state, squares)


def pack_body(keep_ref, arrived_ref, request_ref, packed_ref):
    for block in range(BLOCKS):
        for tile in range(TILES):
            terms = keep_ref[tile, block] + arrived_ref[tile, block]
            for part in range(X_SIZE):
                shard = (block * X_SIZE + part) * CORES + tile
                packed_ref[shard] = jnp.concatenate(
                    [
                        terms[part * SHARE : (part + 1) * SHARE, :],
                        request_ref[shard : shard + 1, :],
                        jnp.zeros((PACKED - SHARE - 1, LANES), jnp.float32),
                    ],
                    axis=0,
                ).astype(jnp.bfloat16)


def pack(keep, arrived, requests):
    return kernel_call(
        pack_body,
        jax.ShapeDtypeStruct((SHARDS, PACKED, LANES), jnp.bfloat16),
        in_specs=[VMEM] * 3,
        out_specs=VMEM,
    )(keep, arrived, requests)


def unpack_body(packed_ref, lookup_ref, sum_ref, asked_ref):
    for core in range(CORES):
        total = jnp.zeros((PACKED, LANES), jnp.float32)
        for shard in range(core, SHARDS, CORES):
            packed = packed_ref[shard].astype(jnp.float32)
            total = total + packed
            asked_ref[shard : shard + 1, :] = packed[SHARE : SHARE + 1, :]
        sum_ref[core] = total


def unpack(packed, lookup):
    return kernel_call(
        unpack_body,
        (
            jax.ShapeDtypeStruct((CORES, PACKED, LANES), jnp.float32),
            jax.ShapeDtypeStruct((SHARDS, LANES), jnp.float32),
        ),
        in_specs=[VMEM, ANY],
        out_specs=(VMEM, VMEM),
    )(packed, lookup)


def used_slots(slot_ref, count):
    slots = slot_ref[...]
    return jnp.where(iota(slots.shape, 1) < count, slots, -1)


def rows_of_block(slots, first, rows):
    hit = slots == iota((rows, slots.shape[1]), 0) + first
    return jnp.where(hit, 1.0, 0.0).astype(jnp.bfloat16)


def train_body(count_ref, slot_ref, held_ref, square_ref, grad_ref, new_ref, weight_ref, fresh_ref, parts, total):
    step = pl.program_id(0)
    rows = held_ref.shape[0]

    @pl.when(step == 0)
    def _():
        grads = grad_ref[...]
        high = grads.astype(jnp.bfloat16)
        rest = grads - high.astype(jnp.float32)
        middle = rest.astype(jnp.bfloat16)
        low = (rest - middle.astype(jnp.float32)).astype(jnp.bfloat16)
        parts[...] = jnp.concatenate([high, middle, low], axis=1)
        total[...] = jnp.zeros_like(total)

    spread = rows_of_block(used_slots(slot_ref, count_ref[0]), step * rows, rows)
    sums = jnp.dot(spread, parts[...], preferred_element_type=jnp.float32)
    gradient = (sums[:, :LANES] + sums[:, LANES : 2 * LANES]) + sums[:, 2 * LANES :]
    linear, squares, _ = ftrl_step(held_ref[...], square_ref[...], gradient, ROW_SHRINK)
    new_ref[...] = linear
    weights = ftrl_weight(linear, squares, ROW_SHRINK).astype(jnp.bfloat16)
    weight_ref[...] = weights
    total[...] += lax.dot_general(
        spread, weights, (((0,), (0,)), ((), ())), preferred_element_type=jnp.float32
    )

    @pl.when(step == pl.num_programs(0) - 1)
    def _():
        fresh_ref[...] = total[...].astype(jnp.bfloat16)


def train_rows(count, slots, held, squares, grads):
    rows, width = held.shape
    updates = grads.shape[0]
    block = 512
    by_rows = pl.BlockSpec((block, width), lambda i: (i, 0))
    return kernel_call(
        train_body,
        (
            jax.ShapeDtypeStruct((rows, width), jnp.float32),
            jax.ShapeDtypeStruct((rows, width), jnp.bfloat16),
            jax.ShapeDtypeStruct((updates, width), jnp.bfloat16),
        ),
        grid=(rows // block,),
        in_specs=[
            SMEM,
            pl.BlockSpec((1, updates), lambda i: (0, 0)),
            by_rows,
            by_rows,
            pl.BlockSpec((updates, width), lambda i: (0, 0)),
        ],
        out_specs=(
            by_rows,
            by_rows,
            pl.BlockSpec((updates, width), lambda i: (0, 0)),
        ),
        scratch_shapes=[
            pltpu.VMEM((updates, 3 * width), jnp.bfloat16),
            pltpu.VMEM((updates, width), jnp.float32),
        ],
    )(count, slots, held, squares, grads)


def serve_body(count_ref, slot_ref, arrived_ref, held_ref, new_ref, weight_ref, table_ref, lookup_ref):
    step = pl.program_id(0)
    rows = held_ref.shape[0]
    role = lax.axis_index("role")

    @pl.when(role == 0)
    def _():
        table_ref[...] = new_ref[...]
        lookup_ref[...] = weight_ref[...]

    @pl.when(role != 0)
    def _():
        spread = rows_of_block(used_slots(slot_ref, count_ref[0]), step * rows, rows)
        arrived = arrived_ref[...]
        sums = jnp.dot(
            spread,
            jnp.concatenate([arrived, jnp.ones_like(arrived)], axis=1),
            preferred_element_type=jnp.float32,
        )
        table = jnp.where(sums[:, LANES:] > 0.5, sums[:, :LANES], held_ref[...])
        table_ref[...] = table
        lookup_ref[...] = table.astype(jnp.bfloat16)


def serve_rows(count, slots, arrived, held, new_linear, weights):
    rows, width = held.shape
    updates = slots.shape[1]
    block = 1024
    by_rows = pl.BlockSpec((block, width), lambda i: (i, 0))
    return kernel_call(
        serve_body,
        (
            jax.ShapeDtypeStruct((rows, width), jnp.float32),
            jax.ShapeDtypeStruct((rows, width), jnp.bfloat16),
        ),
        grid=(rows // block,),
        in_specs=[
            SMEM,
            pl.BlockSpec((1, updates), lambda i: (0, 0)),
            pl.BlockSpec((updates, width), lambda i: (0, 0)),
            by_rows,
            by_rows,
            by_rows,
        ],
        out_specs=(by_rows, by_rows),
    )(count, slots, arrived, held, new_linear, weights)


def looked_up(column, folded):
    rows, height = column.shape[0], folded.shape[0]
    spread = jnp.broadcast_to(column, (rows, LANES))
    within = jnp.where((spread & (LANES - 1)) == iota((rows, LANES), 1), 1.0, 0.0).astype(
        jnp.bfloat16
    )
    block = ((spread & (height - 1)) >> 7).astype(jnp.float32).astype(jnp.bfloat16)
    none = jnp.zeros_like(within)
    hot = jnp.concatenate(
        [jnp.where(block == jnp.bfloat16(at), within, none) for at in range(height // LANES)],
        axis=1,
    )
    both = jnp.dot(hot, folded, preferred_element_type=jnp.float32)
    return jnp.where(spread < height, both[:, :LANES], both[:, LANES:]).astype(jnp.bfloat16)


def fold(source_ref, target_ref):
    height = target_ref.shape[0]
    target_ref[:, :LANES] = source_ref[:height, :]
    target_ref[:, LANES:] = source_ref[height:, :]


def piece_body(sum_ref, other_ref, state_ref, trained_ref, square_ref, answer_ref, piece_ref):
    role, shard, _ = position()
    later = lax.rem(shard // CORES, X_SIZE) == 1

    def own(values):
        return jnp.where(later, values[SHARE : 2 * SHARE, :], values[:SHARE, :])

    parts = []
    for half in range(ROLES):
        for column in range(CORES):
            gradient = jnp.where(role == half, sum_ref[column], other_ref[column])[:SHARE, :]
            state = own(state_ref[column, half])
            trained = own(trained_ref[column, half])
            linear = jnp.where(role == 0, state, trained)
            dense_linear, dense_sumsq, prior = ftrl_step(
                linear, own(square_ref[column, half]), gradient, DENSE_SHRINK
            )
            fresh = ftrl_weight(dense_linear, dense_sumsq, DENSE_SHRINK)
            parts.append(jnp.where(role == 0, fresh, state + (fresh - prior)))
    piece_ref[...] = jnp.concatenate(parts, axis=0).astype(jnp.bfloat16)


def piece_weights(sums, other, state, trained, squares, answers):
    return kernel_call(
        piece_body,
        jax.ShapeDtypeStruct((ROLES * CORES * SHARE, LANES), jnp.bfloat16),
        in_specs=[VMEM] * 5 + [ANY],
        out_specs=VMEM,
    )(sums, other, state, trained, squares, answers)


def columns_of(asked_ref, columns):
    digits = asked_ref[...]
    wide = jnp.concatenate(
        [
            digits[:, :CAP] * 16.0 + digits[:, CAP : 2 * CAP],
            jnp.zeros((SHARDS, LANES - CAP), jnp.float32),
        ],
        axis=1,
    )
    columns[...] = jnp.transpose(wide)[:CAP, :].astype(jnp.int32)


def answer_body(asked_ref, table_ref, answer_ref, columns, folded):
    columns_of(asked_ref, columns)
    fold(table_ref, folded)
    answer_some(columns, folded, answer_ref, 0, FIRST, 0)


def answer_some(columns, folded, out_ref, first, last, offset):
    group = 8
    for at in range(first, last, group):
        asked = jnp.concatenate(
            [columns[:, shard : shard + 1] for shard in range(at, at + group)], axis=0
        )
        out_ref[at * CAP - offset : (at + group) * CAP - offset, :] = looked_up(asked, folded[...])


def answer_rest_body(asked_ref, table_ref, early_ref, late_ref, answer_ref, columns, folded, rest, written):
    del early_ref, late_ref
    columns_of(asked_ref, columns)
    fold(table_ref, folded)
    answer_some(columns, folded, rest, FIRST, SHARDS, FIRST * CAP)
    copy = pltpu.make_async_copy(
        rest, answer_ref.at[pl.ds(FIRST * CAP, (SHARDS - FIRST) * CAP)], written
    )
    copy.start()
    copy.wait()


def answer_rest(asked, table, answers, late):
    rows, width = table.shape
    return kernel_call(
        answer_rest_body,
        jax.ShapeDtypeStruct(answers.shape, answers.dtype),
        in_specs=[VMEM, VMEM, ANY, ANY],
        out_specs=ANY,
        input_output_aliases={2: 0},
        scratch_shapes=[
            pltpu.VMEM((CAP, SHARDS), jnp.int32),
            pltpu.VMEM((rows // 2, 2 * width), jnp.bfloat16),
            pltpu.VMEM(((SHARDS - FIRST) * CAP, width), jnp.bfloat16),
            pltpu.SemaphoreType.DMA,
        ],
    )(asked, table, answers, late)


def answer_rows(asked, table):
    rows, width = table.shape
    return kernel_call(
        answer_body,
        jax.ShapeDtypeStruct((SHARDS * CAP, width), jnp.bfloat16),
        in_specs=[VMEM] * 2,
        out_specs=VMEM,
        scratch_shapes=[
            pltpu.VMEM((CAP, SHARDS), jnp.int32),
            pltpu.VMEM((rows // 2, 2 * width), jnp.bfloat16),
        ],
    )(asked, table)


def after_body(value_ref, other_ref, out_ref):
    del value_ref, other_ref, out_ref


def after(value, other):
    return kernel_call(
        after_body,
        jax.ShapeDtypeStruct(value.shape, value.dtype),
        in_specs=[ANY, ANY],
        out_specs=ANY,
        input_output_aliases={0: 0},
    )(value, other)


def collect_body(*refs):
    piece_refs, tile_ref = refs[:Y_SIZE], refs[Y_SIZE]
    _, shard, _ = position()
    x = lax.rem(shard // CORES, X_SIZE)
    y = lax.rem(shard // (X_SIZE * CORES), Y_SIZE)
    z = shard // (Y_SIZE * X_SIZE * CORES)
    piece = ROLES * CORES * SHARE
    for y_flip, ref in enumerate(piece_refs):
        for at, steps in enumerate(Z_ORDER):
            near = ref[at * piece : (at + 1) * piece, :].astype(jnp.float32)
            far = ref[(Z_SIZE + at) * piece : (Z_SIZE + at + 1) * piece, :].astype(jnp.float32)
            first, second = jnp.where(x == 0, near, far), jnp.where(x == 0, far, near)
            block = lax.rem(z + steps, Z_SIZE) * Y_SIZE + (y ^ y_flip)
            rows = pl.ds(pl.multiple_of(block * piece, piece), piece)
            for column in range(CORES):
                parts = []
                for half in range(ROLES):
                    start = (half * CORES + column) * SHARE
                    parts += [values[start : start + SHARE, :] for values in (first, second)]
                tile_ref[rows, column * LANES : (column + 1) * LANES] = jnp.concatenate(
                    parts, axis=0
                ).astype(jnp.bfloat16)


def collect(pieces):
    rows = BLOCKS * ROLES * X_SIZE * SHARE
    return kernel_call(
        collect_body,
        jax.ShapeDtypeStruct((rows, CORES * LANES), jnp.bfloat16),
        flops=9_000_000_000,
        in_specs=[VMEM] * Y_SIZE,
        out_specs=VMEM,
    )(*pieces)


def arrange_body(place_ref, answer_ref, base_ref, columns, folded):
    columns[...] = jnp.transpose(place_ref[...])
    fold(answer_ref, folded)
    examples = columns.shape[0]
    block = 256
    for field in range(base_ref.shape[1] // LANES):
        for at in range(0, examples, block):
            base_ref[at : at + block, field * LANES : (field + 1) * LANES] = looked_up(
                columns[at : at + block, field : field + 1], folded[...]
            )


def arrange_rows(places, answers, fields):
    examples = places.shape[1]
    rows, width = answers.shape
    return kernel_call(
        arrange_body,
        jax.ShapeDtypeStruct((examples, fields * width), jnp.bfloat16),
        flops=2 * examples * fields * rows * width,
        bytes_accessed=2_000_000,
        in_specs=[VMEM, VMEM],
        out_specs=VMEM,
        scratch_shapes=[
            pltpu.VMEM((examples, 8), jnp.int32),
            pltpu.VMEM((rows // 2, 2 * width), jnp.bfloat16),
        ],
    )(places, answers)


def cross_body(base_ref, bias_ref, out_ref, own_ref, other_ref, score_ref):
    _, _, core = position()
    width = base_ref.shape[1]
    base = base_ref[...].astype(jnp.float32)
    crossed = base
    for layer in range(bias_ref.shape[0]):
        rows = slice(layer * width, (layer + 1) * width)
        inputs = crossed.astype(jnp.bfloat16)
        own, other = (
            jnp.dot(inputs, tile_ref[rows, :], preferred_element_type=jnp.float32)
            for tile_ref in (own_ref, other_ref)
        )
        even, odd = jnp.where(core == 0, own, other), jnp.where(core == 0, other, own)
        mixed = jnp.concatenate(
            [
                tiles[:, column * LANES : (column + 1) * LANES]
                for column in range(CORES)
                for tiles in (even, odd)
            ],
            axis=1,
        )
        crossed = base * (mixed + bias_ref[layer : layer + 1, :]) + crossed
    scores = jnp.sum(crossed * out_ref[...], axis=1, keepdims=True)
    score_ref[...] = jnp.transpose(jnp.broadcast_to(scores, (scores.shape[0], LANES)))[:1, :]


def cross_scores(base, bias, out_weight, own, other):
    examples, width = base.shape
    return kernel_call(
        cross_body,
        jax.ShapeDtypeStruct((1, examples), jnp.float32),
        flops=2 * examples * width * width * bias.shape[0],
        bytes_accessed=3_000_000,
        in_specs=[VMEM] * 5,
        out_specs=VMEM,
    )(base, bias, out_weight, own, other)


BOTH = ("role", "shard")
CORE_BIT, X_BIT, Y_BIT, ROLE_BIT = 1, 2, 4, 128


def swapped(value, bits):
    count = ROLES * SHARDS
    return lax.ppermute(value, BOTH, [(source, source ^ bits) for source in range(count)])


def from_ahead(value, steps):
    span = SHARDS // Z_SIZE
    return lax.ppermute(
        value,
        "shard",
        [((source + steps * span) % SHARDS, source) for source in range(SHARDS)],
    )


def exchange(value):
    return lax.all_to_all(value, "shard", split_axis=0, concat_axis=0, tiled=True)


def on_device(
    tables,
    row_squares,
    update_slots,
    update_counts,
    row_grads,
    dense_state,
    dense_squares,
    dense_grads,
    cross_bias,
    out_weight,
    cand_owner,
    cand_slot,
):
    fields = cand_owner.shape[2]
    blocks = (BLOCKS, ROLES, 2 * SHARE, dense_squares.shape[2])
    grads = dense_grads.reshape(blocks)
    paired = swapped(fetch(grads), CORE_BIT)
    places, requests, keep, own_state, own_squares = route(
        cand_owner[0].T,
        cand_slot[0].T,
        grads,
        dense_state.reshape(blocks),
        dense_squares.reshape(blocks),
    )
    trained = lax.ppermute(own_state, "role", [(0, 1)])
    packed = exchange(pack(keep, paired, requests))
    slots = update_slots.reshape(1, -1)
    new_linear, weights, fresh = train_rows(
        update_counts, slots, tables[0], row_squares, row_grads
    )
    arrived = lax.ppermute(fresh, "role", [(0, 1)])
    table_result, lookup = serve_rows(
        update_counts, slots, arrived, tables[0], new_linear, weights
    )
    sums, asked = unpack(packed, lookup)
    answers = answer_rows(asked, lookup)
    piece = piece_weights(
        sums, swapped(sums, ROLE_BIT), own_state, trained, own_squares, answers
    )
    ahead, behind = from_ahead(piece, 1), from_ahead(piece, -1)
    three = jnp.concatenate([piece, ahead, behind], axis=0)
    pieces = jnp.concatenate(
        [
            three,
            from_ahead(three, -3),
            from_ahead(jnp.concatenate([piece, ahead], axis=0), 2),
        ],
        axis=0,
    )
    answers = after(answer_rest(asked, lookup, answers, piece), three)
    answered = exchange(answers.reshape(SHARDS, CAP, LANES))
    pieces = jnp.concatenate([pieces, swapped(pieces, X_BIT)], axis=0)
    tiles = collect(
        [pieces] + [swapped(pieces, flip * Y_BIT) for flip in range(1, Y_SIZE)]
    )
    base = arrange_rows(places, answered.reshape(SHARDS * CAP, LANES), fields)
    scores = cross_scores(
        base, cross_bias, out_weight.reshape(1, -1), tiles, swapped(tiles, CORE_BIT)
    )
    return (table_result[None], scores)


def solution(mesh):
    return jax.shard_map(
        on_device,
        mesh=mesh,
        in_specs=(
            P("role", "shard", None),
            P("shard", None),
            P("shard"),
            P("shard"),
            P("shard", None),
            P("role", None, None, None),
            P(),
            P("shard", None, None, None),
            P(),
            P(),
            P("role", "shard", None),
            P("role", "shard", None),
        ),
        out_specs=(P("role", "shard", None), P("role", "shard")),
        check_vma=False,
    )
```

```python
import jax
import jax.numpy as jnp
from jax import lax
from jax.experimental import pallas as pl
from jax.experimental.pallas import tpu as pltpu
from jax.sharding import PartitionSpec as P

ROW_SHRINK = 0.25
DENSE_SHRINK = 0.05
CAP = 32
FIRST = 96
LANES = 128
SHARDS = 128
ROLES = 2
Z_SIZE, Y_SIZE, X_SIZE, CORES = 8, 4, 2, 2
BLOCKS = Z_SIZE * Y_SIZE
Z_ORDER = (0, 1, 7, 5, 6, 4, 2, 3)
TILES = 2
SHARE = 12
PACKED = 16
VMEM_LIMIT = 24 * 1024 * 1024
FETCH_LIMIT = 52 * 1024 * 1024


def ftrl_weight(linear, squares, shrink):
    return -(linear - jnp.clip(linear, -shrink, shrink)) / (1.0 + jnp.sqrt(squares))


def ftrl_step(linear, squares, gradient, shrink):
    prior = ftrl_weight(linear, squares, shrink)
    fresh_squares = squares + gradient * gradient
    sigma_step = jnp.sqrt(fresh_squares) - jnp.sqrt(squares)
    return (linear + gradient - sigma_step * prior, fresh_squares, prior)


def iota(shape, dim):
    return lax.broadcasted_iota(jnp.int32, shape, dim)


def kernel_call(body, out_shape, flops=0, bytes_accessed=0, vmem=VMEM_LIMIT, **options):
    return pl.pallas_call(
        body,
        out_shape=out_shape,
        compiler_params=pltpu.CompilerParams(vmem_limit_bytes=vmem),
        cost_estimate=pl.CostEstimate(
            flops=flops, bytes_accessed=bytes_accessed, transcendentals=0
        ),
        **options,
    )


VMEM = pl.BlockSpec(memory_space=pltpu.VMEM)
SMEM = pl.BlockSpec(memory_space=pltpu.SMEM)
ANY = pl.BlockSpec(memory_space=pl.ANY)
HBM = pl.BlockSpec(memory_space=pltpu.HBM)


def position():
    shard = lax.axis_index("shard")
    return lax.axis_index("role"), shard, lax.rem(shard, CORES)


def half_copies(grad_ref, target_ref, flip, arrived):
    role, _, core = position()
    copies = []
    for tile in range(TILES):
        left = pl.multiple_of(((core ^ flip) * TILES + tile) * LANES, LANES)
        copies.append(
            pltpu.make_async_copy(
                grad_ref.at[:, role, :, pl.ds(left, LANES)], target_ref.at[tile], arrived.at[tile]
            )
        )
    return copies


def fetch_body(grad_ref, send_ref, arrived):
    copies = half_copies(grad_ref, send_ref, 1, arrived)
    for copy in copies:
        copy.start()
    for copy in copies:
        copy.wait()


def fetch(grads):
    return kernel_call(
        fetch_body,
        jax.ShapeDtypeStruct((TILES, BLOCKS, 2 * SHARE, LANES), jnp.float32),
        vmem=FETCH_LIMIT,
        in_specs=[HBM],
        out_specs=VMEM,
        scratch_shapes=[pltpu.SemaphoreType.DMA((TILES,))],
    )(grads)


def route_body(owner_ref, slot_ref, grad_ref, state_ref, square_ref, place_ref, request_ref, keep_ref, own_state_ref, own_square_ref, arrived):
    _, shard, core = position()
    copies = half_copies(grad_ref, keep_ref, 0, arrived)
    for source, target in ((state_ref, own_state_ref), (square_ref, own_square_ref)):
        for column in range(CORES):
            left = pl.multiple_of((column * TILES + core) * LANES, LANES)
            copies.append(
                pltpu.make_async_copy(
                    source.at[shard // (X_SIZE * CORES), :, :, pl.ds(left, LANES)],
                    target.at[column],
                    arrived.at[len(copies)],
                )
            )
    for copy in copies:
        copy.start()
    fields, examples = owner_ref.shape
    shape = (SHARDS, examples)
    shard_ids = iota(shape, 0)
    member = jnp.zeros(shape, jnp.float32)
    wanted = jnp.zeros(shape, jnp.float32)
    for field in range(fields):
        named = owner_ref[field : field + 1, :] == shard_ids
        member = jnp.where(named, 1.0, member)
        wanted = jnp.where(named, slot_ref[field : field + 1, :].astype(jnp.float32), wanted)
    earlier = jnp.where(iota((examples, examples), 0) < iota((examples, examples), 1), 1.0, 0.0)
    ranks = jnp.dot(
        member.astype(jnp.bfloat16),
        earlier.astype(jnp.bfloat16),
        preferred_element_type=jnp.float32,
    )
    places = []
    for field in range(fields):
        owners = owner_ref[field : field + 1, :]
        rank = jnp.sum(jnp.where(owners == shard_ids, ranks, 0.0), axis=0, keepdims=True)
        places.append(owners * CAP + rank.astype(jnp.int32))
    place_ref[...] = jnp.concatenate(
        places + [jnp.zeros((8 - fields, examples), jnp.int32)], axis=0
    )
    ranks = jnp.where(member > 0.5, ranks, -1.0)
    requests = jnp.zeros((SHARDS, LANES), jnp.float32)
    lanes = iota((SHARDS, LANES), 1)
    for rank in range(CAP):
        column = jnp.sum(
            jnp.where(ranks == float(rank), wanted, 0.0), axis=1, keepdims=True
        )
        requests = jnp.where(lanes == rank, column, requests)
    asked = requests[:, :CAP].astype(jnp.int32)
    request_ref[...] = jnp.concatenate(
        [asked >> 4, asked & 15, jnp.zeros((SHARDS, LANES - 2 * CAP), jnp.int32)], axis=1
    ).astype(jnp.float32)
    for copy in copies:
        copy.wait()


def route(owners, slots, grads, state, squares):
    examples = owners.shape[1]
    own = jax.ShapeDtypeStruct((CORES, ROLES, 2 * SHARE, LANES), jnp.float32)
    return kernel_call(
        route_body,
        (
            jax.ShapeDtypeStruct((8, examples), jnp.int32),
            jax.ShapeDtypeStruct((SHARDS, LANES), jnp.float32),
            jax.ShapeDtypeStruct((TILES, BLOCKS, 2 * SHARE, LANES), jnp.float32),
            own,
            own,
        ),
        vmem=FETCH_LIMIT,
        in_specs=[VMEM] * 2 + [HBM] * 3,
        out_specs=(VMEM,) * 5,
        scratch_shapes=[pltpu.SemaphoreType.DMA((TILES + 2 * CORES,))],
    )(owners, slots, grads, state, squares)


def pack_body(keep_ref, arrived_ref, request_ref, packed_ref):
    for block in range(BLOCKS):
        for tile in range(TILES):
            terms = keep_ref[tile, block] + arrived_ref[tile, block]
            for part in range(X_SIZE):
                shard = (block * X_SIZE + part) * CORES + tile
                packed_ref[shard] = jnp.concatenate(
                    [
                        terms[part * SHARE : (part + 1) * SHARE, :],
                        request_ref[shard : shard + 1, :],
                        jnp.zeros((PACKED - SHARE - 1, LANES), jnp.float32),
                    ],
                    axis=0,
                ).astype(jnp.bfloat16)


def pack(keep, arrived, requests):
    return kernel_call(
        pack_body,
        jax.ShapeDtypeStruct((SHARDS, PACKED, LANES), jnp.bfloat16),
        in_specs=[VMEM] * 3,
        out_specs=VMEM,
    )(keep, arrived, requests)


def unpack_body(packed_ref, lookup_ref, sum_ref, asked_ref):
    for core in range(CORES):
        total = jnp.zeros((PACKED, LANES), jnp.float32)
        for shard in range(core, SHARDS, CORES):
            packed = packed_ref[shard].astype(jnp.float32)
            total = total + packed
            asked_ref[shard : shard + 1, :] = packed[SHARE : SHARE + 1, :]
        sum_ref[core] = total


def unpack(packed, lookup):
    return kernel_call(
        unpack_body,
        (
            jax.ShapeDtypeStruct((CORES, PACKED, LANES), jnp.float32),
            jax.ShapeDtypeStruct((SHARDS, LANES), jnp.float32),
        ),
        in_specs=[VMEM, ANY],
        out_specs=(VMEM, VMEM),
    )(packed, lookup)


def used_slots(slot_ref, count):
    slots = slot_ref[...]
    return jnp.where(iota(slots.shape, 1) < count, slots, -1)


def rows_of_block(slots, first, rows):
    hit = slots == iota((rows, slots.shape[1]), 0) + first
    return jnp.where(hit, 1.0, 0.0).astype(jnp.bfloat16)


def train_body(count_ref, slot_ref, held_ref, square_ref, grad_ref, new_ref, weight_ref, fresh_ref, parts, total):
    step = pl.program_id(0)
    rows = held_ref.shape[0]

    @pl.when(step == 0)
    def _():
        grads = grad_ref[...]
        high = grads.astype(jnp.bfloat16)
        rest = grads - high.astype(jnp.float32)
        middle = rest.astype(jnp.bfloat16)
        low = (rest - middle.astype(jnp.float32)).astype(jnp.bfloat16)
        parts[...] = jnp.concatenate([high, middle, low], axis=1)
        total[...] = jnp.zeros_like(total)

    spread = rows_of_block(used_slots(slot_ref, count_ref[0]), step * rows, rows)
    sums = jnp.dot(spread, parts[...], preferred_element_type=jnp.float32)
    gradient = (sums[:, :LANES] + sums[:, LANES : 2 * LANES]) + sums[:, 2 * LANES :]
    linear, squares, _ = ftrl_step(held_ref[...], square_ref[...], gradient, ROW_SHRINK)
    new_ref[...] = linear
    weights = ftrl_weight(linear, squares, ROW_SHRINK).astype(jnp.bfloat16)
    weight_ref[...] = weights
    total[...] += lax.dot_general(
        spread, weights, (((0,), (0,)), ((), ())), preferred_element_type=jnp.float32
    )

    @pl.when(step == pl.num_programs(0) - 1)
    def _():
        fresh_ref[...] = total[...].astype(jnp.bfloat16)


def train_rows(count, slots, held, squares, grads):
    rows, width = held.shape
    updates = grads.shape[0]
    block = 512
    by_rows = pl.BlockSpec((block, width), lambda i: (i, 0))
    return kernel_call(
        train_body,
        (
            jax.ShapeDtypeStruct((rows, width), jnp.float32),
            jax.ShapeDtypeStruct((rows, width), jnp.bfloat16),
            jax.ShapeDtypeStruct((updates, width), jnp.bfloat16),
        ),
        grid=(rows // block,),
        in_specs=[
            SMEM,
            pl.BlockSpec((1, updates), lambda i: (0, 0)),
            by_rows,
            by_rows,
            pl.BlockSpec((updates, width), lambda i: (0, 0)),
        ],
        out_specs=(
            by_rows,
            by_rows,
            pl.BlockSpec((updates, width), lambda i: (0, 0)),
        ),
        scratch_shapes=[
            pltpu.VMEM((updates, 3 * width), jnp.bfloat16),
            pltpu.VMEM((updates, width), jnp.float32),
        ],
    )(count, slots, held, squares, grads)


def serve_body(count_ref, slot_ref, arrived_ref, held_ref, new_ref, weight_ref, table_ref, lookup_ref):
    step = pl.program_id(0)
    rows = held_ref.shape[0]
    role = lax.axis_index("role")

    @pl.when(role == 0)
    def _():
        table_ref[...] = new_ref[...]
        lookup_ref[...] = weight_ref[...]

    @pl.when(role != 0)
    def _():
        spread = rows_of_block(used_slots(slot_ref, count_ref[0]), step * rows, rows)
        arrived = arrived_ref[...]
        sums = jnp.dot(
            spread,
            jnp.concatenate([arrived, jnp.ones_like(arrived)], axis=1),
            preferred_element_type=jnp.float32,
        )
        table = jnp.where(sums[:, LANES:] > 0.5, sums[:, :LANES], held_ref[...])
        table_ref[...] = table
        lookup_ref[...] = table.astype(jnp.bfloat16)


def serve_rows(count, slots, arrived, held, new_linear, weights):
    rows, width = held.shape
    updates = slots.shape[1]
    block = 1024
    by_rows = pl.BlockSpec((block, width), lambda i: (i, 0))
    return kernel_call(
        serve_body,
        (
            jax.ShapeDtypeStruct((rows, width), jnp.float32),
            jax.ShapeDtypeStruct((rows, width), jnp.bfloat16),
        ),
        grid=(rows // block,),
        in_specs=[
            SMEM,
            pl.BlockSpec((1, updates), lambda i: (0, 0)),
            pl.BlockSpec((updates, width), lambda i: (0, 0)),
            by_rows,
            by_rows,
            by_rows,
        ],
        out_specs=(by_rows, by_rows),
    )(count, slots, arrived, held, new_linear, weights)


def looked_up(column, folded):
    rows, height = column.shape[0], folded.shape[0]
    spread = jnp.broadcast_to(column, (rows, LANES))
    within = jnp.where((spread & (LANES - 1)) == iota((rows, LANES), 1), 1.0, 0.0).astype(
        jnp.bfloat16
    )
    block = ((spread & (height - 1)) >> 7).astype(jnp.float32).astype(jnp.bfloat16)
    none = jnp.zeros_like(within)
    hot = jnp.concatenate(
        [jnp.where(block == jnp.bfloat16(at), within, none) for at in range(height // LANES)],
        axis=1,
    )
    both = jnp.dot(hot, folded, preferred_element_type=jnp.float32)
    return jnp.where(spread < height, both[:, :LANES], both[:, LANES:]).astype(jnp.bfloat16)


def fold(source_ref, target_ref):
    height = target_ref.shape[0]
    target_ref[:, :LANES] = source_ref[:height, :]
    target_ref[:, LANES:] = source_ref[height:, :]


def piece_body(sum_ref, other_ref, state_ref, trained_ref, square_ref, answer_ref, piece_ref):
    role, shard, _ = position()
    later = lax.rem(shard // CORES, X_SIZE) == 1

    def own(values):
        return jnp.where(later, values[SHARE : 2 * SHARE, :], values[:SHARE, :])

    parts = []
    for half in range(ROLES):
        for column in range(CORES):
            gradient = jnp.where(role == half, sum_ref[column], other_ref[column])[:SHARE, :]
            state = own(state_ref[column, half])
            trained = own(trained_ref[column, half])
            linear = jnp.where(role == 0, state, trained)
            dense_linear, dense_sumsq, prior = ftrl_step(
                linear, own(square_ref[column, half]), gradient, DENSE_SHRINK
            )
            fresh = ftrl_weight(dense_linear, dense_sumsq, DENSE_SHRINK)
            parts.append(jnp.where(role == 0, fresh, state + (fresh - prior)))
    piece_ref[...] = jnp.concatenate(parts, axis=0).astype(jnp.bfloat16)


def piece_weights(sums, other, state, trained, squares, answers):
    return kernel_call(
        piece_body,
        jax.ShapeDtypeStruct((ROLES * CORES * SHARE, LANES), jnp.bfloat16),
        in_specs=[VMEM] * 5 + [ANY],
        out_specs=VMEM,
    )(sums, other, state, trained, squares, answers)


def columns_of(asked_ref, columns):
    digits = asked_ref[...]
    wide = jnp.concatenate(
        [
            digits[:, :CAP] * 16.0 + digits[:, CAP : 2 * CAP],
            jnp.zeros((SHARDS, LANES - CAP), jnp.float32),
        ],
        axis=1,
    )
    columns[...] = jnp.transpose(wide)[:CAP, :].astype(jnp.int32)


def answer_body(asked_ref, table_ref, answer_ref, columns, folded):
    columns_of(asked_ref, columns)
    fold(table_ref, folded)
    answer_some(columns, folded, answer_ref, 0, FIRST, 0)


def answer_some(columns, folded, out_ref, first, last, offset):
    group = 8
    for at in range(first, last, group):
        asked = jnp.concatenate(
            [columns[:, shard : shard + 1] for shard in range(at, at + group)], axis=0
        )
        out_ref[at * CAP - offset : (at + group) * CAP - offset, :] = looked_up(asked, folded[...])


def answer_rest_body(asked_ref, table_ref, early_ref, late_ref, answer_ref, columns, folded, rest, written):
    del early_ref, late_ref
    columns_of(asked_ref, columns)
    fold(table_ref, folded)
    answer_some(columns, folded, rest, FIRST, SHARDS, FIRST * CAP)
    copy = pltpu.make_async_copy(
        rest, answer_ref.at[pl.ds(FIRST * CAP, (SHARDS - FIRST) * CAP)], written
    )
    copy.start()
    copy.wait()


def answer_rest(asked, table, answers, late):
    rows, width = table.shape
    return kernel_call(
        answer_rest_body,
        jax.ShapeDtypeStruct(answers.shape, answers.dtype),
        in_specs=[VMEM, VMEM, ANY, ANY],
        out_specs=ANY,
        input_output_aliases={2: 0},
        scratch_shapes=[
            pltpu.VMEM((CAP, SHARDS), jnp.int32),
            pltpu.VMEM((rows // 2, 2 * width), jnp.bfloat16),
            pltpu.VMEM(((SHARDS - FIRST) * CAP, width), jnp.bfloat16),
            pltpu.SemaphoreType.DMA,
        ],
    )(asked, table, answers, late)


def answer_rows(asked, table):
    rows, width = table.shape
    return kernel_call(
        answer_body,
        jax.ShapeDtypeStruct((SHARDS * CAP, width), jnp.bfloat16),
        in_specs=[VMEM] * 2,
        out_specs=VMEM,
        scratch_shapes=[
            pltpu.VMEM((CAP, SHARDS), jnp.int32),
            pltpu.VMEM((rows // 2, 2 * width), jnp.bfloat16),
        ],
    )(asked, table)


def after_body(value_ref, other_ref, out_ref):
    del value_ref, other_ref, out_ref


def after(value, other):
    return kernel_call(
        after_body,
        jax.ShapeDtypeStruct(value.shape, value.dtype),
        in_specs=[ANY, ANY],
        out_specs=ANY,
        input_output_aliases={0: 0},
    )(value, other)


def collect_body(*refs):
    piece_refs, tile_ref = refs[:Y_SIZE], refs[Y_SIZE]
    _, shard, _ = position()
    x = lax.rem(shard // CORES, X_SIZE)
    y = lax.rem(shard // (X_SIZE * CORES), Y_SIZE)
    z = shard // (Y_SIZE * X_SIZE * CORES)
    piece = ROLES * CORES * SHARE
    for y_flip, ref in enumerate(piece_refs):
        for at, steps in enumerate(Z_ORDER):
            near = ref[at * piece : (at + 1) * piece, :].astype(jnp.float32)
            far = ref[(Z_SIZE + at) * piece : (Z_SIZE + at + 1) * piece, :].astype(jnp.float32)
            first, second = jnp.where(x == 0, near, far), jnp.where(x == 0, far, near)
            block = lax.rem(z + steps, Z_SIZE) * Y_SIZE + (y ^ y_flip)
            rows = pl.ds(pl.multiple_of(block * piece, piece), piece)
            for column in range(CORES):
                parts = []
                for half in range(ROLES):
                    start = (half * CORES + column) * SHARE
                    parts += [values[start : start + SHARE, :] for values in (first, second)]
                tile_ref[rows, column * LANES : (column + 1) * LANES] = jnp.concatenate(
                    parts, axis=0
                ).astype(jnp.bfloat16)


def collect(pieces):
    rows = BLOCKS * ROLES * X_SIZE * SHARE
    return kernel_call(
        collect_body,
        jax.ShapeDtypeStruct((rows, CORES * LANES), jnp.bfloat16),
        flops=9_000_000_000,
        in_specs=[VMEM] * Y_SIZE,
        out_specs=VMEM,
    )(*pieces)


def arrange_body(place_ref, answer_ref, base_ref, columns, folded):
    columns[...] = jnp.transpose(place_ref[...])
    fold(answer_ref, folded)
    examples = columns.shape[0]
    block = 256
    for field in range(base_ref.shape[1] // LANES):
        for at in range(0, examples, block):
            base_ref[at : at + block, field * LANES : (field + 1) * LANES] = looked_up(
                columns[at : at + block, field : field + 1], folded[...]
            )


def arrange_rows(places, answers, fields):
    examples = places.shape[1]
    rows, width = answers.shape
    return kernel_call(
        arrange_body,
        jax.ShapeDtypeStruct((examples, fields * width), jnp.bfloat16),
        flops=2 * examples * fields * rows * width,
        bytes_accessed=2_000_000,
        in_specs=[VMEM, VMEM],
        out_specs=VMEM,
        scratch_shapes=[
            pltpu.VMEM((examples, 8), jnp.int32),
            pltpu.VMEM((rows // 2, 2 * width), jnp.bfloat16),
        ],
    )(places, answers)


def cross_body(base_ref, bias_ref, out_ref, own_ref, other_ref, score_ref):
    _, _, core = position()
    width = base_ref.shape[1]
    base = base_ref[...].astype(jnp.float32)
    crossed = base
    for layer in range(bias_ref.shape[0]):
        rows = slice(layer * width, (layer + 1) * width)
        inputs = crossed.astype(jnp.bfloat16)
        own, other = (
            jnp.dot(inputs, tile_ref[rows, :], preferred_element_type=jnp.float32)
            for tile_ref in (own_ref, other_ref)
        )
        even, odd = jnp.where(core == 0, own, other), jnp.where(core == 0, other, own)
        mixed = jnp.concatenate(
            [
                tiles[:, column * LANES : (column + 1) * LANES]
                for column in range(CORES)
                for tiles in (even, odd)
            ],
            axis=1,
        )
        crossed = base * (mixed + bias_ref[layer : layer + 1, :]) + crossed
    scores = jnp.sum(crossed * out_ref[...], axis=1, keepdims=True)
    score_ref[...] = jnp.transpose(jnp.broadcast_to(scores, (scores.shape[0], LANES)))[:1, :]


def score_body(place_ref, answer_ref, bias_ref, out_ref, own_ref, other_ref, score_ref, columns, folded, base):
    arrange_body(place_ref, answer_ref, base, columns, folded)
    cross_body(base, bias_ref, out_ref, own_ref, other_ref, score_ref)


def score(places, answers, bias, out_weight, own, other):
    examples = places.shape[1]
    rows, lanes = answers.shape
    width = out_weight.shape[1]
    return kernel_call(
        score_body,
        jax.ShapeDtypeStruct((1, examples), jnp.float32),
        flops=2 * examples * width * (rows + width * bias.shape[0]),
        bytes_accessed=3_000_000,
        in_specs=[VMEM] * 6,
        out_specs=VMEM,
        scratch_shapes=[
            pltpu.VMEM((examples, 8), jnp.int32),
            pltpu.VMEM((rows // 2, 2 * lanes), jnp.bfloat16),
            pltpu.VMEM((examples, width), jnp.bfloat16),
        ],
    )(places, answers, bias, out_weight, own, other)


BOTH = ("role", "shard")
CORE_BIT, X_BIT, Y_BIT, ROLE_BIT = 1, 2, 4, 128


def swapped(value, bits):
    count = ROLES * SHARDS
    return lax.ppermute(value, BOTH, [(source, source ^ bits) for source in range(count)])


def from_ahead(value, steps):
    span = SHARDS // Z_SIZE
    return lax.ppermute(
        value,
        "shard",
        [((source + steps * span) % SHARDS, source) for source in range(SHARDS)],
    )


def exchange(value):
    return lax.all_to_all(value, "shard", split_axis=0, concat_axis=0, tiled=True)


def on_device(
    tables,
    row_squares,
    update_slots,
    update_counts,
    row_grads,
    dense_state,
    dense_squares,
    dense_grads,
    cross_bias,
    out_weight,
    cand_owner,
    cand_slot,
):
    fields = cand_owner.shape[2]
    blocks = (BLOCKS, ROLES, 2 * SHARE, dense_squares.shape[2])
    grads = dense_grads.reshape(blocks)
    paired = swapped(fetch(grads), CORE_BIT)
    places, requests, keep, own_state, own_squares = route(
        cand_owner[0].T,
        cand_slot[0].T,
        grads,
        dense_state.reshape(blocks),
        dense_squares.reshape(blocks),
    )
    trained = lax.ppermute(own_state, "role", [(0, 1)])
    packed = exchange(pack(keep, paired, requests))
    slots = update_slots.reshape(1, -1)
    new_linear, weights, fresh = train_rows(
        update_counts, slots, tables[0], row_squares, row_grads
    )
    arrived = lax.ppermute(fresh, "role", [(0, 1)])
    table_result, lookup = serve_rows(
        update_counts, slots, arrived, tables[0], new_linear, weights
    )
    sums, asked = unpack(packed, lookup)
    answers = answer_rows(asked, lookup)
    piece = piece_weights(
        sums, swapped(sums, ROLE_BIT), own_state, trained, own_squares, answers
    )
    ahead, behind = from_ahead(piece, 1), from_ahead(piece, -1)
    three = jnp.concatenate([piece, ahead, behind], axis=0)
    pieces = jnp.concatenate(
        [
            three,
            from_ahead(three, -3),
            from_ahead(jnp.concatenate([piece, ahead], axis=0), 2),
        ],
        axis=0,
    )
    answers = after(answer_rest(asked, lookup, answers, piece), three)
    answered = exchange(answers.reshape(SHARDS, CAP, LANES))
    pieces = jnp.concatenate([pieces, swapped(pieces, X_BIT)], axis=0)
    tiles = collect(
        [pieces] + [swapped(pieces, flip * Y_BIT) for flip in range(1, Y_SIZE)]
    )
    scores = score(
        places,
        answered.reshape(SHARDS * CAP, LANES),
        cross_bias,
        out_weight.reshape(1, -1),
        tiles,
        swapped(tiles, CORE_BIT),
    )
    return (table_result[None], scores)


def solution(mesh):
    return jax.shard_map(
        on_device,
        mesh=mesh,
        in_specs=(
            P("role", "shard", None),
            P("shard", None),
            P("shard"),
            P("shard"),
            P("shard", None),
            P("role", None, None, None),
            P(),
            P("shard", None, None, None),
            P(),
            P(),
            P("role", "shard", None),
            P("role", "shard", None),
        ),
        out_specs=(P("role", "shard", None), P("role", "shard")),
        check_vma=False,
    )
```
